32 devices in a mesh: dp: 16 (over z, y, x), blk: 2 (over core).
Axes of the slice: x: 2, y: 2, z: 4, core: 2. Of those that a mesh axis runs over, the one named last changes fastest.
Arguments:
- hidden_in: bfloat16 [16, 512, 768], P('dp', 'blk'), may hold values from -6 to 6
- project_weight: bfloat16 [768, 2304], replicated, may hold values from -0.21875 to 0.21875
- output_weight: bfloat16 [768, 768], replicated, may hold values from -1.25 to 1.25
- expand_weight: bfloat16 [768, 3072], replicated, may hold values from -0.21875 to 0.21875
- reduce_weight: bfloat16 [3072, 768], replicated, may hold values from -0.109375 to 0.109375
- query_bias: float32 [768], replicated, may hold values from -3 to 3
- value_bias: float32 [768], replicated, may hold values from -3 to 3
- output_bias: float32 [768], replicated, may hold values from -3 to 3
- first_gain: float32 [768], replicated, may hold values from 0.5 to 1.5
- first_shift: float32 [768], replicated, may hold values from -3 to 3
- expand_bias: float32 [3072], replicated, may hold values from -3 to 3
- reduce_bias: float32 [768], replicated, may hold values from -3 to 3
- second_gain: float32 [768], replicated, may hold values from 0.5 to 1.5
- second_shift: float32 [768], replicated, may hold values from -3 to 3
- upstream: bfloat16 [16, 512, 768], P('dp', 'blk'), may hold values from -6 to 6
- teacher_maps: bfloat16 [16, 12, 512, 512], P('dp', None, 'blk'), may hold values from 0.5 to 8
- start_vector: float32 [768], replicated, may hold values from -5 to 5
- end_vector: float32 [768], replicated, may hold values from -5 to 5
- valid_length: int32 [16], P('dp'), may hold values from 257 to 512, as said below
- start_index: int32 [16], P('dp'), may hold values from 1 to 511, as said below
- end_index: int32 [16], P('dp'), may hold values from 1 to 511, as said below
- answerable: int32 [16], P('dp'), may hold values 0 or 1
Outputs:
- layer_output: bfloat16 [16, 512, 768], P('dp', 'blk')
- input_gradient: bfloat16 [16, 512, 768], P('dp', 'blk')
- weight_gradients: float32 [7087104], P(('dp', 'blk'))
The draws below stay inside these ranges and needn't reach their ends.
Inputs may be any that keep to these rules, and one draw needn't show every extreme that they name: `valid_length`: tokens of a row at or beyond its length are padding; padding lies within a row's last 512 // 2 tokens; every fourth row, from the first, is at full length 512. start_index <= end_index < valid_length of the same row; full-length rows start at 511. start_index <= end_index < valid_length of the same row; full-length rows end at 511.
All inputs are finite; a program needn't handle non-finite values. No bound on the sum of `answerable` on one device may be relied on, other than what follows from the above.
Results may differ from the reference program's by a relative error of at most 0.014.
Values may be sent and summed in bfloat16 or wider, within the bound.
A program may use at most 192 MiB of HBM per device.

```python
import math
import jax
import jax.numpy as jnp
from jax import lax

D = 768
HEADS = 12
HEAD_DIM = 64
FF = 3072
SEQ = 512
ROWS = 16
N_BLK = 2


def lengths_of(key):
    key = jax.random.fold_in(key, 11)
    drawn_len = jax.random.randint(key, (ROWS,), SEQ - SEQ // N_BLK + 1, SEQ + 1)
    full_row = jnp.arange(ROWS) % 4 == 0
    return jnp.where(full_row, SEQ, drawn_len).astype(jnp.int32)


def spans_of(key):
    lengths = lengths_of(key)
    key = jax.random.fold_in(key, 13)
    start_key, width_key = jax.random.split(key)
    start_at = jax.random.randint(start_key, (ROWS,), 1, lengths)
    end_at = jax.random.randint(width_key, (ROWS,), start_at, lengths)
    start_at = jnp.where(lengths == SEQ, SEQ - 1, start_at)
    end_at = jnp.where(lengths == SEQ, SEQ - 1, end_at)
    return (start_at.astype(jnp.int32), end_at.astype(jnp.int32))


def draw_valid_length(key, part):
    return lengths_of(key)


def draw_start_index(key, part):
    return spans_of(key)[0]


def draw_end_index(key, part):
    return spans_of(key)[1]


def plant(result, key, low, top_value):
    index_at = [jax.random.randint(jax.random.fold_in(key, axis), (), 0, length) for axis, length in enumerate(result.shape)]
    longest = result.shape.index(max(result.shape))
    beside = index_at[:longest] + [(index_at[longest] + 1) % result.shape[longest]] + index_at[longest + 1:]
    return result.at[tuple(index_at)].set(low).at[tuple(beside)].set(top_value)


def levels(key, shape, cuts, least, top_value):
    loudness, own = 1.0, jax.random.fold_in(key, 6)
    for axis_at, parts in cuts:
        steps = jnp.exp(jax.random.uniform(jax.random.fold_in(own, axis_at), (parts,), jnp.float32, least / len(cuts), top_value / len(cuts)))
        loudness = loudness * jnp.repeat(steps, shape[axis_at] // parts).reshape([-1 if axis == axis_at else 1 for axis in range(len(shape))])
    return loudness


def bell_draw(own_key, extent, deviation, reach, pieces=(), kind=jnp.bfloat16):
    drawn = jax.random.normal(own_key, extent, jnp.float32) * deviation
    if len(pieces) > 0:
        drawn = levels(own_key, extent, pieces, -0.22, 0.18) * drawn
    return jnp.clip(drawn, min=-reach, max=reach).astype(kind)


def setup_inputs(seed: int = 0) -> dict:
    arg_keys = jax.random.split(jax.random.key(seed), 23)
    return {
        "hidden_in": bell_draw(arg_keys[0], (ROWS, SEQ, D), 1.0, 6.0, ((0, 16), (1, 2))),
        "project_weight": bell_draw(arg_keys[1], (D, 3 * D), D ** -0.5, 0.21875),
        "output_weight": bell_draw(arg_keys[2], (D, D), (max(D * 16 // SEQ, 1)) ** -0.5, 1.25),
        "expand_weight": bell_draw(arg_keys[3], (D, FF), D ** -0.5, 0.21875),
        "reduce_weight": bell_draw(arg_keys[4], (FF, D), FF ** -0.5, 0.109375),
        "query_bias": bell_draw(arg_keys[5], (D,), 0.5, 3.0, (), jnp.float32),
        "value_bias": bell_draw(arg_keys[6], (D,), 0.5, 3.0, (), jnp.float32),
        "output_bias": bell_draw(arg_keys[7], (D,), 0.5, 3.0, (), jnp.float32),
        "first_gain": jnp.clip(1.0 + 0.1 * jax.random.normal(arg_keys[8], (D,), jnp.float32), 0.5, 1.5),
        "first_shift": bell_draw(arg_keys[9], (D,), 0.5, 3.0, (), jnp.float32),
        "expand_bias": bell_draw(arg_keys[10], (FF,), 0.5, 3.0, (), jnp.float32),
        "reduce_bias": bell_draw(arg_keys[11], (D,), 0.5, 3.0, (), jnp.float32),
        "second_gain": jnp.clip(1.0 + 0.1 * jax.random.normal(arg_keys[12], (D,), jnp.float32), 0.5, 1.5),
        "second_shift": bell_draw(arg_keys[13], (D,), 0.5, 3.0, (), jnp.float32),
        "upstream": bell_draw(arg_keys[14], (ROWS, SEQ, D), 1.0, 6.0, ((0, 16), (1, 2))),
        "teacher_maps": jnp.clip(jnp.exp(math.log(8.0) - 2.7725887 * jax.random.uniform(arg_keys[15], (ROWS, HEADS, SEQ, SEQ), jnp.float32) ** levels(arg_keys[15], (ROWS, HEADS, SEQ, SEQ), ((0, 16), (2, 2)), -0.2, 0.2)), 0.5, 8.0).astype(jnp.bfloat16),
        "start_vector": bell_draw(arg_keys[16], (D,), 1.0, 5.0, (), jnp.float32),
        "end_vector": bell_draw(arg_keys[17], (D,), 1.0, 5.0, (), jnp.float32),
        "valid_length": draw_valid_length(jax.random.fold_in(arg_keys[22], 71), 0),
        "start_index": draw_start_index(jax.random.fold_in(arg_keys[22], 71), 0),
        "end_index": draw_end_index(jax.random.fold_in(arg_keys[22], 71), 0),
        "answerable": plant((jax.random.randint(arg_keys[21], (ROWS,), 0, 3) < 2).astype(jnp.int32), jax.random.fold_in(arg_keys[21], 1), 0, 1),
    }


@jax.custom_vjp
def low(v):
    return lax.optimization_barrier(v.astype(jnp.bfloat16)).astype(jnp.float32)

@jax.custom_vjp
def low_back(v):
    return v

def low_keep(v):
    return (low(v), None)

def low_pass(kept, grad):
    return (grad,)

def back_keep(v):
    return (v, None)

def back_low(kept, grad):
    return (low(grad),)
low.defvjp(low_keep, low_pass)
low_back.defvjp(back_keep, back_low)
highest = lax.Precision.HIGHEST
norm_eps = 1e-12

def layer_norm(field_in, gain_vec, shift_vec):
    centre = field_in - lax.optimization_barrier(jnp.mean(field_in, axis=-1, keepdims=True))
    spread = lax.optimization_barrier(jnp.mean(centre * centre, axis=-1, keepdims=True))
    return centre * lax.rsqrt(spread + norm_eps) * gain_vec + shift_vec

def forward(hidden, project_weight, output_weight, expand_weight, reduce_weight, query_bias, value_bias, output_bias, first_gain, first_shift, expand_bias, reduce_bias, second_gain, second_shift, key_live, teacher):
    group_rows, length, width = hidden.shape
    joined_bias = jnp.concatenate([query_bias, jnp.zeros_like(query_bias), value_bias])
    project = jnp.einsum('gld,de->gle', hidden, project_weight, precision=highest) + joined_bias
    project = low(low_back(project))
    queries = project[..., :width].reshape(group_rows, length, HEADS, HEAD_DIM)
    keys_all = project[..., width:2 * width].reshape(group_rows, length, HEADS, HEAD_DIM)
    values_all = project[..., 2 * width:].reshape(group_rows, length, HEADS, HEAD_DIM)
    scores = jnp.einsum('gqhe,gkhe->ghqk', queries, keys_all, precision=highest) * HEAD_DIM ** (-0.5)
    scores = low_back(scores)
    scores = jnp.where(key_live[:, None, None, :], scores, -1e+30)
    both_live = key_live[:, None, :, None] & key_live[:, None, None, :]
    teacher_live = jnp.where(both_live, teacher, 0.0)
    log_soft = jnp.where(both_live, jax.nn.log_softmax(scores, axis=-1), 0.0)
    distill = -jnp.sum(teacher_live * log_soft) / SEQ
    soft = low(jax.nn.softmax(scores, axis=-1))
    attended = jnp.einsum('ghqk,gkhe->gqhe', soft, values_all, precision=highest).reshape(group_rows, length, width)
    attended = low(low_back(attended))
    branch = low_back(jnp.einsum('gld,de->gle', attended, output_weight, precision=highest) + output_bias)
    mixed = layer_norm(hidden + branch, first_gain, first_shift)
    expanded = low_back(jnp.einsum('gld,df->glf', low(mixed), expand_weight, precision=highest) + expand_bias)
    active = low(jax.nn.gelu(expanded, approximate=False))
    reduced = low_back(jnp.einsum('glf,fd->gld', active, reduce_weight, precision=highest) + reduce_bias)
    return (layer_norm(mixed + reduced, second_gain, second_shift), distill)

def reference(hidden_in, project_weight, output_weight, expand_weight, reduce_weight, query_bias, value_bias, output_bias, first_gain, first_shift, expand_bias, reduce_bias, second_gain, second_shift, upstream, teacher_maps, start_vector, end_vector, valid_length, start_index, end_index, answerable):
    group_rows = math.gcd(ROWS, max(1, 4096 // SEQ))
    count = ROWS // group_rows
    params = tuple((entry.astype(jnp.float32) for entry in (project_weight, output_weight, expand_weight, reduce_weight, query_bias, value_bias, output_bias, first_gain, first_shift, expand_bias, reduce_bias, second_gain, second_shift)))
    positions = jnp.arange(SEQ, dtype=jnp.int32)
    live = positions[None, :] < valid_length[:, None]
    start_slot = jnp.where(answerable > 0, start_index, 0).astype(jnp.int32)
    end_slot = jnp.where(answerable > 0, end_index, 0).astype(jnp.int32)
    cotangent = upstream.astype(jnp.float32) * live[..., None].astype(jnp.float32) + (positions[None, :] == start_slot[:, None])[..., None].astype(jnp.float32) * start_vector + (positions[None, :] == end_slot[:, None])[..., None].astype(jnp.float32) * end_vector
    inputs = (hidden_in.astype(jnp.float32).reshape(count, group_rows, SEQ, D), cotangent.reshape(count, group_rows, SEQ, D), live.reshape(count, group_rows, SEQ), teacher_maps.reshape(count, group_rows, HEADS, SEQ, SEQ))

    def scan_step(totals, block_in):
        hidden_blk, cot_blk, live_blk, teacher_blk = block_in
        teacher_full = teacher_blk.astype(jnp.float32)

        def apply_layer(hidden_arg, *weights):
            return forward(hidden_arg, *weights, live_blk, teacher_full)
        (layer_blk, distill), pullback = jax.vjp(apply_layer, hidden_blk, *params)
        grad_list = pullback((cot_blk, jnp.ones_like(distill)))
        totals = tuple((total_one + grad_one for total_one, grad_one in zip(totals, grad_list[1:])))
        return (totals, (layer_blk.astype(jnp.bfloat16), grad_list[0].astype(jnp.bfloat16)))
    starting = tuple((jnp.zeros_like(entry) for entry in params))
    totals, (layer_parts, grad_parts) = lax.scan(scan_step, starting, inputs)
    layer_output = layer_parts.reshape(ROWS, SEQ, D)
    input_gradient = grad_parts.reshape(ROWS, SEQ, D)
    weight_gradients = jnp.concatenate([entry.reshape(-1) for entry in totals])
    return (layer_output, input_gradient, weight_gradients)
```

```python
import jax
import jax.numpy as jnp
from jax import lax
from jax.experimental import pallas as pl
from jax.experimental.pallas import tpu as pltpu
from jax.sharding import PartitionSpec as P

HEADS = 12
HEAD_DIM = 64
WIDTH = 768
FF = 3072
BLOCK = 256
ROW = 512
UNIT = 288
CHIPS = 16
LANES = 128

MESH = pl.DeviceIdType.MESH
LOW = jnp.bfloat16
FULL = jnp.float32

norm_eps = 1e-12


def dot_nn(left, right):
    return jnp.dot(left, right, preferred_element_type=FULL)


def dot_nt(left, right):
    return lax.dot_general(left, right, (((1,), (1,)), ((), ())), preferred_element_type=FULL)


def dot_tn(left, right):
    return lax.dot_general(left, right, (((0,), (0,)), ((), ())), preferred_element_type=FULL)


def both(own, other):
    return jnp.concatenate([own, other], axis=0)


def col_sum(field):
    return jnp.sum(field, axis=0, keepdims=True)


def row_mean(field):
    return jnp.mean(field, axis=-1, keepdims=True)


def aligned(start, step):
    return pl.multiple_of(start, step)


def layer_kernel(
    hidden,
    upstream,
    teacher,
    w_project,
    w_output,
    w_expand,
    w_reduce,
    query_bias,
    value_bias,
    output_bias,
    first_gain,
    first_shift,
    expand_bias,
    reduce_bias,
    second_gain,
    second_shift,
    start_vector,
    end_vector,
    valid_length,
    start_index,
    end_index,
    answerable,
    layer_output,
    input_gradient,
    grads,
    wp,
    wo,
    we,
    wr,
    te,
    up,
    x_row,
    q_own,
    k_row,
    v_row,
    soft,
    att_own,
    att_oth,
    mix_own,
    mix_oth,
    act_own,
    act_oth,
    slope,
    norm_one,
    resid_two,
    resid_one,
    gred_own,
    gred_oth,
    gexp_own,
    gexp_oth,
    gbr_own,
    gbr_oth,
    gatt,
    qt,
    gat,
    dkv_out,
    dkv_in,
    gpj_own,
    gpj_oth,
    live_map,
    grad,
    plane_in,
    plane_in2,
    chain_in,
    total,
    total_oth,
    flat,
    bias_sum,
    bias_in,
    load_sem,
    core_send,
    core_recv,
    s1_send,
    s1_recv,
    s2_send,
    s2_recv,
    chain_send,
    chain_recv,
    bias_send,
    bias_recv,
    fix_send,
    fix_recv,
):
    dp = lax.axis_index("dp")
    blk = lax.axis_index("blk")
    oth = 1 - blk
    xx = dp % 2
    yy = (dp // 2) % 2
    zz = dp // 4
    core_dev = (dp, oth)
    x_dev = (dp + 1 - 2 * xx, blk)
    y_dev = (dp + 2 - 4 * yy, blk)
    up_dev = (dp + 4, blk)
    down_dev = (dp - 4, blk)
    device = dp * 2 + blk

    def load(at, src, dst):
        copy = pltpu.make_async_copy(src, dst, load_sem.at[at])
        copy.start()
        return copy

    own_rows = pl.ds(aligned(blk * BLOCK, BLOCK), BLOCK)
    oth_rows = pl.ds(aligned(oth * BLOCK, BLOCK), BLOCK)
    load_x = load(0, hidden, x_row.at[own_rows])
    load_wp = load(1, w_project, wp)
    load_wo = load(2, w_output, wo)
    load_we = load(3, w_expand, we)
    load_wr = load(4, w_reduce, wr)
    load_up = load(5, upstream, up)
    load_te = load(6, teacher, te)

    barrier = pltpu.get_barrier_semaphore()

    def greet(dev):
        pl.semaphore_signal(barrier, inc=1, device_id=dev, device_id_type=MESH)

    greet(core_dev)
    greet(x_dev)
    greet(y_dev)

    @pl.when(zz > 0)
    def _():
        greet(down_dev)

    @pl.when(zz < 3)
    def _():
        greet(up_dev)

    @pl.when((blk == 1) & (dp < CHIPS - 1))
    def _():
        greet((dp + 1, 0))

    def project_cols(rows, at, bias):
        part = dot_nn(x_row[rows, :], wp[:, pl.ds(at, 256)])
        if bias is not None:
            part = part + bias
        return part.astype(LOW)

    load_x.wait()
    load_wp.wait()
    for tile in range(3):
        cols = slice(256 * tile, 256 * tile + 256)
        q_part = project_cols(own_rows, 256 * tile, query_bias[:, cols])
        q_own[:, cols] = q_part * jnp.asarray(HEAD_DIM ** (-0.5), LOW)
    for tile in range(3):
        cols = slice(256 * tile, 256 * tile + 256)
        k_row[own_rows, cols] = project_cols(own_rows, WIDTH + 256 * tile, None)
        v_row[own_rows, cols] = project_cols(
            own_rows, 2 * WIDTH + 256 * tile, value_bias[:, cols]
        )

    waits = 3 + (zz > 0).astype(jnp.int32) + (zz < 3).astype(jnp.int32)
    waits = waits + ((blk == 0) & (dp > 0)).astype(jnp.int32)
    pl.semaphore_wait(barrier, waits)

    def to_core(at, src, dst):
        copy = pltpu.make_async_remote_copy(
            src_ref=src,
            dst_ref=dst,
            send_sem=core_send.at[at],
            recv_sem=core_recv.at[at],
            device_id=core_dev,
            device_id_type=MESH,
        )
        copy.start()
        return copy

    core_copies = []
    send_x = to_core(0, x_row.at[own_rows], x_row.at[own_rows])
    core_copies.append(send_x)
    length = valid_length[0]
    key_at = lax.broadcasted_iota(jnp.int32, (1, ROW), 1)
    key_live = key_at < length
    token_at = blk * BLOCK + lax.broadcasted_iota(jnp.int32, (BLOCK, 1), 0)
    row_live = (token_at < length).astype(FULL)
    live_map[...] = jnp.where(key_live, 1.0 / ROW, 0.0) * row_live
    pltpu.make_async_remote_copy(
        src_ref=x_row.at[oth_rows],
        dst_ref=x_row.at[oth_rows],
        send_sem=core_send.at[0],
        recv_sem=core_recv.at[0],
        device_id=core_dev,
        device_id_type=MESH,
    ).wait_recv()
    for tile in range(3):
        cols = slice(256 * tile, 256 * tile + 256)
        k_row[oth_rows, cols] = project_cols(oth_rows, WIDTH + 256 * tile, None)
        v_row[oth_rows, cols] = project_cols(
            oth_rows, 2 * WIDTH + 256 * tile, value_bias[:, cols]
        )

    lane = lax.broadcasted_iota(jnp.int32, (1, LANES), 1)
    head_lanes = ((lane < HEAD_DIM).astype(LOW), (lane >= HEAD_DIM).astype(LOW))

    @pl.loop(0, HEADS // 2)
    def _(pair):
        cols = pl.ds(aligned(pair * LANES, LANES), LANES)
        q_pair = q_own[:, cols]
        k_pair = k_row[:, cols]
        v_pair = v_row[:, cols]
        gathered = None
        for side in range(2):
            scores = dot_nt(q_pair * head_lanes[side], k_pair)
            scores = jnp.where(key_live, scores, -1e30)
            peak = jnp.max(scores, axis=-1, keepdims=True)
            terms = jnp.exp(scores - peak)
            scale = 1.0 / jnp.sum(terms, axis=-1, keepdims=True)
            soft_low = (terms * scale).astype(LOW)
            soft[2 * pair + side] = soft_low
            part = dot_nn(soft_low, v_pair * head_lanes[side])
            gathered = part if gathered is None else gathered + part
        att_own[:, cols] = gathered.astype(LOW)

    core_copies.append(to_core(1, att_own, att_oth))

    load_wo.wait()
    branch = dot_nn(att_own[...], wo[...]) + output_bias[...]
    resid = x_row[own_rows, :].astype(FULL) + branch
    centre = resid - row_mean(resid)
    scale_one = lax.rsqrt(row_mean(centre * centre) + norm_eps)
    normal = centre * scale_one
    norm_one[...] = normal
    mix_own[...] = (normal * first_gain[...] + first_shift[...]).astype(LOW)
    core_copies.append(to_core(2, mix_own, mix_oth))

    load_we.wait()

    @pl.loop(0, 6)
    def _(at):
        cols = pl.ds(aligned(at * 512, 512), 512)
        expanded = dot_nn(mix_own[...], we[:, cols]) + expand_bias[:, cols]
        gate = 0.5 + 0.5 * lax.erf(expanded * (2.0**-0.5))
        bell = jnp.exp(expanded * expanded * -0.5) * ((2.0 * jnp.pi) ** -0.5)
        act_own[:, cols] = (expanded * gate).astype(LOW)
        slope[:, cols] = (gate + expanded * bell).astype(LOW)

    core_copies.append(to_core(3, act_own, act_oth))
    load_wr.wait()
    reduced = dot_nn(act_own[...], wr[...]) + reduce_bias[...]
    mixed = norm_one[...] * first_gain[...] + first_shift[...]
    resid = mixed + reduced
    centre = resid - row_mean(resid)
    scale_two = lax.rsqrt(row_mean(centre * centre) + norm_eps)
    normal = centre * scale_two
    layer_output[...] = (normal * second_gain[...] + second_shift[...]).astype(LOW)

    answered = answerable[0] > 0
    start_slot = jnp.where(answered, start_index[0], 0)
    end_slot = jnp.where(answered, end_index[0], 0)
    load_up.wait()
    cot = up[...].astype(FULL) * row_live
    cot = cot + (token_at == start_slot).astype(FULL) * start_vector[...]
    cot = cot + (token_at == end_slot).astype(FULL) * end_vector[...]

    def put_bias(first_row, vector):
        for at in range(vector.shape[1] // LANES):
            bias_sum[first_row + at : first_row + at + 1, :] = vector[
                :, at * LANES : (at + 1) * LANES
            ]

    put_bias(60, col_sum(cot * normal))
    put_bias(66, col_sum(cot))
    pulled = cot * second_gain[...]
    pulled = scale_two * (pulled - row_mean(pulled) - normal * row_mean(pulled * normal))
    resid_two[...] = pulled
    pulled_low = pulled.astype(LOW)
    gred_own[...] = pulled_low
    put_bias(54, col_sum(pulled_low.astype(FULL)))
    own_384 = pl.ds(aligned(blk * 384, 384), 384)
    oth_384 = pl.ds(aligned(oth * 384, 384), 384)
    core_copies.append(to_core(4, gred_own.at[:, oth_384], gred_oth))

    def send(src, dst, send_sem, recv_sem, dev):
        pltpu.make_async_remote_copy(
            src_ref=src,
            dst_ref=dst,
            send_sem=send_sem,
            recv_sem=recv_sem,
            device_id=dev,
            device_id_type=MESH,
        ).start()

    def wait_recv(dst, recv_sem):
        pltpu.make_async_remote_copy(
            src_ref=dst,
            dst_ref=dst,
            send_sem=recv_sem,
            recv_sem=recv_sem,
            device_id=core_dev,
            device_id_type=MESH,
        ).wait_recv()

    def wait_send(src, send_sem):
        pltpu.make_async_remote_copy(
            src_ref=src,
            dst_ref=src,
            send_sem=send_sem,
            recv_sem=send_sem,
            device_id=core_dev,
            device_id_type=MESH,
        ).wait_send()

    def base_of(plane, x_at, y_at):
        return 24 * plane + 6 * (2 * y_at + x_at)

    def first_sends(plane):
        return (
            (base_of(plane, 1 - xx, 1 - yy), 0, x_dev),
            (base_of(plane, 1 - xx, 1 - yy) + 3, 2, y_dev),
            (base_of(plane, 1 - xx, yy), 1, x_dev),
            (base_of(plane, xx, 1 - yy) + 3, 3, y_dev),
        )

    def step_one(plane):
        for first, slot, dev in first_sends(plane):
            send(
                grad.at[pl.ds(first, 3)],
                plane_in.at[plane, slot],
                s1_send.at[plane, slot],
                s1_recv.at[plane, slot],
                dev,
            )

    def second_sends(plane):
        return (
            (base_of(plane, xx, 1 - yy), 0, 0, y_dev),
            (base_of(plane, 1 - xx, yy) + 3, 2, 1, x_dev),
        )

    def add_units(first, arrays):
        @pl.loop(0, 3)
        def _(at):
            value = grad[first + at].astype(FULL)
            for array, index in arrays:
                value = value + array[index + (at,)].astype(FULL)
            grad[first + at] = value.astype(LOW)

    def step_two(plane):
        for first, slot, slot2, dev in second_sends(plane):
            wait_recv(plane_in.at[plane, slot], s1_recv.at[plane, slot])
            add_units(first, [(plane_in, (plane, slot))])
            send(
                grad.at[pl.ds(first, 3)],
                plane_in2.at[plane, slot2],
                s2_send.at[plane, slot2],
                s2_recv.at[plane, slot2],
                dev,
            )

    def step_three(plane):
        own = base_of(plane, xx, yy)
        for slot, slot2, first in ((1, 0, own), (3, 1, own + 3)):
            wait_recv(plane_in.at[plane, slot], s1_recv.at[plane, slot])
            wait_recv(plane_in2.at[plane, slot2], s2_recv.at[plane, slot2])
            add_units(first, [(plane_in, (plane, slot)), (plane_in2, (plane, slot2))])

    def chain(plane):
        own = base_of(plane, xx, yy)
        below = zz < plane
        way = jnp.where(below, 0, 1)

        @pl.when(zz != plane)
        def _():
            for half in range(2):
                first = own + 3 * half

                @pl.when((below & (zz > 0)) | (jnp.logical_not(below) & (zz < 3)))
                def _():
                    wait_recv(chain_in.at[way, plane, half], chain_recv.at[way, plane, half])
                    add_units(first, [(chain_in, (way, plane, half))])

                send(
                    grad.at[pl.ds(first, 3)],
                    chain_in.at[way, plane, half],
                    chain_send.at[plane, half],
                    chain_recv.at[way, plane, half],
                    (jnp.where(below, dp + 4, dp - 4), blk),
                )

        @pl.when(zz == plane)
        def _():
            for half in range(2):
                ways = ([0] if plane > 0 else []) + ([1] if plane < 3 else [])
                for one in ways:
                    wait_recv(chain_in.at[one, plane, half], chain_recv.at[one, plane, half])

                @pl.loop(0, 3)
                def _(at):
                    value = grad[own + 3 * half + at].astype(FULL)
                    for one in ways:
                        value = value + chain_in[one, plane, half, at].astype(FULL)
                    total[3 * half + at] = value

    core_copies[3].wait_recv()
    core_copies[4].wait_recv()

    def reduce_rows(at):
        cols = pl.ds(aligned(at * WIDTH, WIDTH), WIDTH)
        part = dot_tn(
            both(act_own[:, cols], act_oth[:, cols]), both(gred_own[:, own_384], gred_oth[...])
        )
        for unit in range(8):
            for tile in range(3):
                grad[64 + 8 * at + unit, 96 * tile : 96 * tile + 96, :] = part[
                    96 * unit : 96 * unit + 96, LANES * tile : LANES * tile + LANES
                ].astype(LOW)

    @pl.loop(1, 4)
    def _(at):
        reduce_rows(at)

    step_one(3)
    reduce_rows(0)

    @pl.loop(0, 6)
    def _(at):
        half = jnp.where(at < 3, oth, blk)
        part_at = lax.rem(at, 3) * 512
        cols = pl.ds(aligned(half * 1536 + part_at, 512), 512)
        grad_active = dot_nt(gred_own[...], wr[cols, :])
        grad_expanded = (grad_active * slope[:, cols].astype(FULL)).astype(LOW)
        gexp_own[half, :, pl.ds(aligned(part_at, 512), 512)] = grad_expanded
        sums = col_sum(grad_expanded.astype(FULL))
        for tile in range(4):
            bias_sum[pl.ds(30 + half * 12 + lax.rem(at, 3) * 4 + tile, 1), :] = sums[
                :, LANES * tile : LANES * tile + LANES
            ]

    core_copies.append(to_core(5, gexp_own.at[oth], gexp_oth))
    grad_mixed = resid_two[...]
    for half in range(2):
        grad_mixed = grad_mixed + dot_nt(
            gexp_own[half], we[:, 1536 * half : 1536 * half + 1536]
        )

    normal = norm_one[...]
    put_bias(18, col_sum(grad_mixed * normal))
    put_bias(24, col_sum(grad_mixed))
    pulled = grad_mixed * first_gain[...]
    pulled = scale_one * (pulled - row_mean(pulled) - normal * row_mean(pulled * normal))
    resid_one[...] = pulled
    pulled_low = pulled.astype(LOW)
    gbr_own[...] = pulled_low
    put_bias(12, col_sum(pulled_low.astype(FULL)))
    core_copies.append(to_core(6, gbr_own.at[:, oth_384], gbr_oth))

    core_copies[2].wait_recv()
    core_copies[5].wait_recv()

    @pl.loop(0, 6)
    def _(at):
        cols = pl.ds(aligned(at * 256, 256), 256)
        part = dot_tn(
            both(mix_own[...], mix_oth[...]), both(gexp_own[blk, :, cols], gexp_oth[:, cols])
        )
        rows = pl.ds(aligned(at * 48, 48), 48)
        for unit in range(32):
            piece = part[24 * unit : 24 * unit + 24, :]
            grad[32 + unit, rows, :] = both(piece[:, :LANES], piece[:, LANES:]).astype(LOW)

    step_one(2)

    gatt[...] = dot_nt(gbr_own[...], wo[...]).astype(LOW)
    core_copies[1].wait_recv()
    core_copies[6].wait_recv()
    part = dot_tn(both(att_own[...], att_oth[...]), both(gbr_own[:, own_384], gbr_oth[...]))
    for unit in range(8):
        for tile in range(3):
            grad[24 + unit, 96 * tile : 96 * tile + 96, :] = part[
                96 * unit : 96 * unit + 96, LANES * tile : LANES * tile + LANES
            ].astype(LOW)
    step_one(1)

    qt[...] = q_own[...].T
    gat[...] = gatt[...].T
    load_te.wait()

    def head_pair(pair):
        cols = pl.ds(aligned(pair * LANES, LANES), LANES)
        ga_pair = gatt[:, cols]
        k_pair = k_row[:, cols]
        v_pair = v_row[:, cols]
        grad_query = None
        for side in range(2):
            rows = pl.ds(aligned(pair * LANES + side * HEAD_DIM, HEAD_DIM), HEAD_DIM)
            soft_low = soft[2 * pair + side]
            grad_soft = dot_nt(ga_pair * head_lanes[side], v_pair)
            soft_full = soft_low.astype(FULL)
            taught = te[2 * pair + side].astype(FULL) * live_map[...]
            shift = jnp.sum(taught - grad_soft * soft_full, axis=-1, keepdims=True)
            grad_scores = (soft_full * (grad_soft + shift) - taught).astype(LOW)
            part = dot_nn(grad_scores, k_pair * head_lanes[side])
            grad_query = part if grad_query is None else grad_query + part
            slot = pl.ds(aligned(pair * ROW, ROW), ROW)
            at = side * HEAD_DIM
            slope[at : at + HEAD_DIM, slot] = dot_nn(qt[rows, :], grad_scores).astype(LOW)
            at = at + LANES
            slope[at : at + HEAD_DIM, slot] = dot_nn(gat[rows, :], soft_low).astype(LOW)
        gpj_own[:, cols] = (grad_query * HEAD_DIM ** (-0.5)).astype(LOW)

    @pl.loop(0, HEADS // 2)
    def _(pair):
        head_pair(pair)

    def turned(pair, block, first):
        lanes = pl.ds(aligned(pair * ROW + block * BLOCK, BLOCK), BLOCK)
        return slope[first : first + LANES, lanes].T

    for pair in range(HEADS // 2):
        for first in (0, LANES):
            at = pair * LANES + first * (WIDTH // LANES)
            dkv_out[:, at : at + LANES] = turned(pair, oth, first)
    core_copies.append(to_core(7, dkv_out, dkv_in))
    step_two(3)
    core_copies[7].wait_recv()
    for pair in range(HEADS // 2):
        for first in (0, LANES):
            at = pair * LANES + first * (WIDTH // LANES)
            gpj_own[:, WIDTH + at : WIDTH + at + LANES] = (
                turned(pair, blk, first).astype(FULL) + dkv_in[:, at : at + LANES].astype(FULL)
            ).astype(LOW)
    own_1152 = pl.ds(aligned(blk * 1152, 1152), 1152)
    oth_1152 = pl.ds(aligned(oth * 1152, 1152), 1152)
    core_copies.append(to_core(8, gpj_own.at[:, oth_1152], gpj_oth))
    put_bias(0, col_sum(gpj_own[:, :WIDTH].astype(FULL)))
    put_bias(6, col_sum(gpj_own[:, 2 * WIDTH :].astype(FULL)))
    input_gradient[...] = (resid_one[...] + dot_nt(gpj_own[...], wp[...])).astype(LOW)

    core_copies[8].wait_recv()

    @pl.loop(0, 3)
    def _(at):
        cols = pl.ds(aligned(at * 384, 384), 384)
        mine = pl.ds(aligned(blk * 1152 + at * 384, 384), 384)
        part = dot_tn(
            both(x_row[own_rows, :], x_row[oth_rows, :]), both(gpj_own[:, mine], gpj_oth[:, cols])
        )
        for unit in range(24):
            for tile in range(3):
                rows = pl.ds(aligned(at * 96 + 32 * tile, 32), 32)
                grad[unit, rows, :] = part[
                    32 * unit : 32 * unit + 32, LANES * tile : LANES * tile + LANES
                ].astype(LOW)

    step_one(0)

    def bias_hop(at, here, there, dev):
        @pl.when(here)
        def _():
            send(bias_sum, bias_in.at[at], bias_send.at[0], bias_recv.at[at], dev)

        @pl.when(there)
        def _():
            wait_recv(bias_in.at[at], bias_recv.at[at])
            bias_sum[...] += bias_in[at]

    bias_hop(0, xx == 0, xx == 1, x_dev)
    step_two(2)
    step_three(3)
    chain(3)
    bias_hop(1, (xx == 1) & (yy == 0), (xx == 1) & (yy == 1), y_dev)
    step_two(1)
    step_three(2)
    chain(2)
    corner = (xx == 1) & (yy == 1)

    @pl.when(corner & (zz > 0))
    def _():
        wait_recv(bias_in.at[2], bias_recv.at[2])
        bias_sum[...] += bias_in[2]

    @pl.when(corner & (zz < 3))
    def _():
        send(bias_sum, bias_in.at[2], bias_send.at[0], bias_recv.at[2], up_dev)

    step_two(0)
    step_three(1)
    chain(1)
    last = dp == CHIPS - 1

    @pl.when(last & (blk == 0))
    def _():
        send(bias_sum, bias_in.at[3], bias_send.at[0], bias_recv.at[3], core_dev)

    @pl.when(last & (blk == 1))
    def _():
        wait_recv(bias_in.at[3], bias_recv.at[3])
        flat[1728:1800, :] = bias_sum[...] + bias_in[3]

    step_three(0)
    chain(0)

    last_send = to_core(9, total.at[pl.ds(3 * oth, 3)], total_oth)
    core_copies.append(last_send)

    def lay_out(source, first, column_half):
        for unit in range(3):
            kind_at = 3 * device + unit
            kinds = (
                (kind_at < 24, 32, 9),
                (((kind_at >= 24) & (kind_at < 32)) | (kind_at >= 64), 96, 3),
                ((kind_at >= 32) & (kind_at < 64), 24, 12),
            )
            for fits, rows, tiles in kinds:

                @pl.when(fits)
                def _():
                    for tile in range(tiles):
                        for group in range(rows // 8):
                            at = rows * tile + 8 * group
                            to = 576 * unit + 16 * group * tiles + tile + column_half * tiles
                            flat[pl.ds(to, 8, stride=2 * tiles), :] = source[
                                first + unit, at : at + 8, :
                            ]

    lay_out(total, 3 * blk, blk)
    last_send.wait_recv()
    lay_out(total_oth, 0, oth)

    @pl.when(blk == 1)
    def _():
        send(flat.at[0:72], flat.at[1728:1800], fix_send.at[0], fix_recv.at[0], core_dev)

    @pl.when((blk == 0) & (dp > 0))
    def _():
        send(flat.at[0:72], flat.at[1728:1800], fix_send.at[0], fix_recv.at[0], (dp - 1, 1))

    @pl.when(device < 2 * CHIPS - 1)
    def _():
        wait_recv(flat.at[1728:1800], fix_recv.at[0])

    shift = 32 * lax.rem(device, 4)
    skip = (9 * device) // 4
    stays = lane < LANES - shift

    @pl.loop(0, 31)
    def _(at):
        rows = at * 56
        first = pltpu.roll(flat[pl.ds(rows + skip, 56), :], LANES - shift, 1)
        second = pltpu.roll(flat[pl.ds(rows + skip + 1, 56), :], LANES - shift, 1)
        grads[pl.ds(aligned(rows, 8), 56), :] = jnp.where(stays, first, second)

    for copy in core_copies:
        copy.wait_send()
    for plane in range(4):
        for slot in range(4):
            wait_send(plane_in.at[plane, slot], s1_send.at[plane, slot])
        for slot in range(2):
            wait_send(plane_in2.at[plane, slot], s2_send.at[plane, slot])

        @pl.when(zz != plane)
        def _():
            for half in range(2):
                wait_send(chain_in.at[0, plane, half], chain_send.at[plane, half])

    @pl.when(jnp.logical_not(last & (blk == 1)))
    def _():
        wait_send(bias_sum, bias_send.at[0])

    @pl.when(device > 0)
    def _():
        wait_send(flat.at[0:72], fix_send.at[0])


def fused_layer(
    hidden_in,
    project_weight,
    output_weight,
    expand_weight,
    reduce_weight,
    query_bias,
    value_bias,
    output_bias,
    first_gain,
    first_shift,
    expand_bias,
    reduce_bias,
    second_gain,
    second_shift,
    upstream,
    teacher_maps,
    start_vector,
    end_vector,
    valid_length,
    start_index,
    end_index,
    answerable,
):
    vectors = [
        vector.reshape(1, -1)
        for vector in (
            query_bias,
            value_bias,
            output_bias,
            first_gain,
            first_shift,
            expand_bias,
            reduce_bias,
            second_gain,
            second_shift,
            start_vector,
            end_vector,
        )
    ]
    scalars = [valid_length, start_index, end_index, answerable]
    anywhere = pl.BlockSpec(memory_space=pl.ANY)
    in_vmem = pl.BlockSpec(memory_space=pltpu.VMEM)
    in_smem = pl.BlockSpec(memory_space=pltpu.SMEM)

    def low(*shape):
        return pltpu.VMEM(shape, LOW)

    def full(*shape):
        return pltpu.VMEM(shape, FULL)

    dma = pltpu.SemaphoreType.DMA
    scratch = [
        low(WIDTH, 3 * WIDTH),
        low(WIDTH, WIDTH),
        low(WIDTH, FF),
        low(FF, WIDTH),
        low(HEADS, BLOCK, ROW),
        low(BLOCK, WIDTH),
        low(ROW, WIDTH),
        low(BLOCK, WIDTH),
        low(ROW, WIDTH),
        low(ROW, WIDTH),
        low(HEADS, BLOCK, ROW),
        low(BLOCK, WIDTH),
        low(BLOCK, WIDTH),
        low(BLOCK, WIDTH),
        low(BLOCK, WIDTH),
        low(BLOCK, FF),
        low(BLOCK, FF),
        low(BLOCK, FF),
        full(BLOCK, WIDTH),
        full(BLOCK, WIDTH),
        full(BLOCK, WIDTH),
        low(BLOCK, WIDTH),
        low(BLOCK, WIDTH // 2),
        low(2, BLOCK, FF // 2),
        low(BLOCK, FF // 2),
        low(BLOCK, WIDTH),
        low(BLOCK, WIDTH // 2),
        low(BLOCK, WIDTH),
        low(WIDTH, BLOCK),
        low(WIDTH, BLOCK),
        low(BLOCK, 2 * WIDTH),
        low(BLOCK, 2 * WIDTH),
        low(BLOCK, 3 * WIDTH),
        low(BLOCK, 3 * WIDTH // 2),
        full(BLOCK, ROW),
        low(96, UNIT, LANES),
        low(4, 4, 3, UNIT, LANES),
        low(4, 2, 3, UNIT, LANES),
        low(2, 4, 2, 3, UNIT, LANES),
        full(6, UNIT, LANES),
        full(3, UNIT, LANES),
        full(1816, LANES),
        full(72, LANES),
        full(4, 72, LANES),
        dma((7,)),
        dma((10,)),
        dma((10,)),
        dma((4, 4)),
        dma((4, 4)),
        dma((4, 2)),
        dma((4, 2)),
        dma((4, 2)),
        dma((2, 4, 2)),
        dma((1,)),
        dma((4,)),
        dma((1,)),
        dma((1,)),
    ]
    layer_output, input_gradient, grads = pl.pallas_call(
        layer_kernel,
        out_shape=(
            jax.ShapeDtypeStruct((BLOCK, WIDTH), LOW),
            jax.ShapeDtypeStruct((BLOCK, WIDTH), LOW),
            jax.ShapeDtypeStruct((1736, LANES), FULL),
        ),
        in_specs=[anywhere] * 7 + [in_vmem] * len(vectors) + [in_smem] * 4,
        out_specs=(in_vmem, in_vmem, in_vmem),
        scratch_shapes=scratch,
        compiler_params=pltpu.CompilerParams(
            collective_id=0, has_side_effects=True, vmem_limit_bytes=63 * 2**20
        ),
        name="encoder_layer",
    )(
        hidden_in.reshape(BLOCK, WIDTH),
        upstream.reshape(BLOCK, WIDTH),
        teacher_maps.reshape(HEADS, BLOCK, ROW),
        project_weight,
        output_weight,
        expand_weight,
        reduce_weight,
        *vectors,
        *scalars,
    )
    return (
        layer_output.reshape(1, BLOCK, WIDTH),
        input_gradient.reshape(1, BLOCK, WIDTH),
        grads.reshape(-1)[: 96 * 3 * 576 * LANES // 96 + 288],
    )


def layer_norm(field_in, gain_vec, shift_vec):
    centre = field_in - jnp.mean(field_in, axis=-1, keepdims=True)
    spread = jnp.mean(centre * centre, axis=-1, keepdims=True)
    return centre * lax.rsqrt(spread + norm_eps) * gain_vec + shift_vec


def gelu_exact(field_in):
    return jax.nn.gelu(field_in, approximate=False)


def outer_sum(left, right):
    return jnp.einsum("nd,ne->de", left, right, preferred_element_type=jnp.float32)


def column_sum(values_low):
    return jnp.sum(values_low.astype(jnp.float32), axis=0)


def plain_layer(
    hidden_in,
    project_weight,
    output_weight,
    expand_weight,
    reduce_weight,
    query_bias,
    value_bias,
    output_bias,
    first_gain,
    first_shift,
    expand_bias,
    reduce_bias,
    second_gain,
    second_shift,
    upstream,
    teacher_maps,
    start_vector,
    end_vector,
    valid_length,
    start_index,
    end_index,
    answerable,
):
    row_count, block_len, width = hidden_in.shape
    blocks = lax.axis_size("blk")
    length = block_len * blocks
    offset = lax.axis_index("blk") * block_len
    token_count = row_count * block_len
    positions = offset + jnp.arange(block_len, dtype=jnp.int32)
    key_live = jnp.arange(length, dtype=jnp.int32)[None, :] < valid_length[:, None]
    row_live = positions[None, :] < valid_length[:, None]
    score_scale = HEAD_DIM ** (-0.5)
    tokens = hidden_in.reshape(token_count, width)
    joined_bias = jnp.concatenate([query_bias, jnp.zeros_like(query_bias), value_bias])
    project = (
        jnp.dot(tokens, project_weight, preferred_element_type=jnp.float32) + joined_bias
    ).astype(jnp.bfloat16)
    queries = project[:, :width].reshape(row_count, block_len, HEADS, HEAD_DIM)
    keys_own = project[:, width : 2 * width].reshape(row_count, block_len, width)
    values_own = project[:, 2 * width :].reshape(row_count, block_len, width)
    keys_all, values_all = (
        lax.all_gather(keys_own, "blk", axis=1, tiled=True),
        lax.all_gather(values_own, "blk", axis=1, tiled=True),
    )

    def scores_of(keys_full):
        raw = (
            jnp.einsum(
                "rqhe,rkhe->rhqk",
                queries,
                keys_full.reshape(row_count, length, HEADS, HEAD_DIM),
                preferred_element_type=jnp.float32,
            )
            * score_scale
        )
        return jnp.where(key_live[:, None, None, :], raw, -1e30)

    scores = scores_of(keys_all)
    row_peak = jnp.max(scores, axis=-1, keepdims=True)
    expo_terms = jnp.exp(scores - row_peak)
    row_total = jnp.sum(expo_terms, axis=-1, keepdims=True)
    soft_low = (expo_terms / row_total).astype(jnp.bfloat16)
    log_total = row_peak + jnp.log(row_total)
    attended = (
        jnp.einsum(
            "rhqk,rkhe->rqhe",
            soft_low,
            values_all.reshape(row_count, length, HEADS, HEAD_DIM),
            preferred_element_type=jnp.float32,
        )
        .reshape(token_count, width)
        .astype(jnp.bfloat16)
    )
    branch = jnp.dot(attended, output_weight, preferred_element_type=jnp.float32) + output_bias
    resid_one = tokens.astype(jnp.float32) + branch
    mixed, first_pull = jax.vjp(layer_norm, resid_one, first_gain, first_shift)
    mixed_low = mixed.astype(jnp.bfloat16)
    expanded = jnp.dot(mixed_low, expand_weight, preferred_element_type=jnp.float32) + expand_bias
    active, gelu_pull = jax.vjp(gelu_exact, expanded)
    active_low = active.astype(jnp.bfloat16)
    reduced = jnp.dot(active_low, reduce_weight, preferred_element_type=jnp.float32) + reduce_bias
    result, second_pull = jax.vjp(layer_norm, mixed + reduced, second_gain, second_shift)
    layer_output = result.astype(jnp.bfloat16).reshape(row_count, block_len, width)
    start_slot = jnp.where(answerable > 0, start_index, 0)
    end_slot = jnp.where(answerable > 0, end_index, 0)
    cotangent = (
        upstream.astype(jnp.float32) * row_live[..., None].astype(jnp.float32)
        + (positions[None, :] == start_slot[:, None])[..., None].astype(jnp.float32) * start_vector
        + (positions[None, :] == end_slot[:, None])[..., None].astype(jnp.float32) * end_vector
    )
    grad_resid_two, grad_second_gain, grad_second_shift = second_pull(
        cotangent.reshape(token_count, width)
    )
    grad_reduced = grad_resid_two.astype(jnp.bfloat16)
    grad_active = jnp.einsum(
        "nd,fd->nf", grad_reduced, reduce_weight, preferred_element_type=jnp.float32
    )
    grad_expanded = gelu_pull(grad_active)[0].astype(jnp.bfloat16)
    grad_mixed = grad_resid_two + jnp.einsum(
        "nf,df->nd", grad_expanded, expand_weight, preferred_element_type=jnp.float32
    )
    grad_resid_one, grad_first_gain, grad_first_shift = first_pull(grad_mixed)
    grad_branch = grad_resid_one.astype(jnp.bfloat16)
    grad_attended = jnp.einsum(
        "ne,de->nd", grad_branch, output_weight, preferred_element_type=jnp.float32
    )
    grad_attended = grad_attended.astype(jnp.bfloat16).reshape(
        row_count, block_len, HEADS, HEAD_DIM
    )
    keys_back, values_back = (
        lax.all_gather(keys_own, "blk", axis=1, tiled=True),
        lax.all_gather(values_own, "blk", axis=1, tiled=True),
    )
    keys_heads = keys_back.reshape(row_count, length, HEADS, HEAD_DIM)
    values_heads = values_back.reshape(row_count, length, HEADS, HEAD_DIM)
    soft = jnp.exp(scores_of(keys_back) - log_total)
    both_live = row_live[:, None, :, None] & key_live[:, None, None, :]
    teacher_live = jnp.where(both_live, teacher_maps.astype(jnp.float32), 0.0)
    teacher_total = jnp.sum(teacher_live, axis=-1, keepdims=True)
    grad_soft = jnp.einsum(
        "rqhe,rkhe->rhqk", grad_attended, values_heads, preferred_element_type=jnp.float32
    )
    row_delta = jnp.sum(grad_soft * soft, axis=-1, keepdims=True)
    grad_scores = (
        soft * (grad_soft - row_delta) + (teacher_total * soft - teacher_live) / length
    ).astype(jnp.bfloat16)
    grad_query = (
        jnp.einsum("rhqk,rkhe->rqhe", grad_scores, keys_heads, preferred_element_type=jnp.float32)
        * score_scale
    )
    grad_keys = (
        jnp.einsum(
            "rhqk,rqhe->rkhe", grad_scores, queries, preferred_element_type=jnp.float32
        ).reshape(row_count, length, width)
        * score_scale
    )
    grad_values = jnp.einsum(
        "rhqk,rqhe->rkhe", soft_low, grad_attended, preferred_element_type=jnp.float32
    ).reshape(row_count, length, width)
    keys_grad_own, values_grad_own = (
        lax.psum_scatter(
            grad_keys.astype(jnp.bfloat16), "blk", scatter_dimension=1, tiled=True
        ).astype(jnp.float32),
        lax.psum_scatter(
            grad_values.astype(jnp.bfloat16), "blk", scatter_dimension=1, tiled=True
        ).astype(jnp.float32),
    )
    grad_project = jnp.concatenate(
        [
            grad_query.reshape(token_count, width),
            keys_grad_own.reshape(token_count, width),
            values_grad_own.reshape(token_count, width),
        ],
        axis=1,
    ).astype(jnp.bfloat16)
    grad_input = grad_resid_one + jnp.einsum(
        "ne,de->nd", grad_project, project_weight, preferred_element_type=jnp.float32
    )
    input_gradient = grad_input.astype(jnp.bfloat16).reshape(row_count, block_len, width)
    (
        tokens_both,
        project_both,
        attended_both,
        branch_both,
        mixed_both,
        expanded_both,
        active_both,
        reduced_both,
    ) = (
        lax.all_gather(tokens, "blk", axis=0, tiled=True),
        lax.all_gather(grad_project, "blk", axis=0, tiled=True),
        lax.all_gather(attended, "blk", axis=0, tiled=True),
        lax.all_gather(grad_branch, "blk", axis=0, tiled=True),
        lax.all_gather(mixed_low, "blk", axis=0, tiled=True),
        lax.all_gather(grad_expanded, "blk", axis=0, tiled=True),
        lax.all_gather(active_low, "blk", axis=0, tiled=True),
        lax.all_gather(grad_reduced, "blk", axis=0, tiled=True),
    )
    project_sums = column_sum(project_both)
    norm_grads = lax.psum(
        (grad_first_gain, grad_first_shift, grad_second_gain, grad_second_shift), "blk"
    )
    flat_grads = jnp.concatenate(
        [
            outer_sum(tokens_both, project_both).reshape(-1),
            outer_sum(attended_both, branch_both).reshape(-1),
            outer_sum(mixed_both, expanded_both).reshape(-1),
            outer_sum(active_both, reduced_both).reshape(-1),
            project_sums[:width],
            project_sums[2 * width :],
            column_sum(branch_both),
            norm_grads[0],
            norm_grads[1],
            column_sum(expanded_both),
            column_sum(reduced_both),
            norm_grads[2],
            norm_grads[3],
        ]
    )
    data_count = lax.axis_size("dp")
    piece_len = flat_grads.shape[0] // (data_count * blocks)
    mine = lax.dynamic_index_in_dim(
        flat_grads.reshape(data_count, blocks, piece_len), lax.axis_index("blk"), 1, keepdims=False
    )
    weight_gradients = lax.psum_scatter(mine, "dp", scatter_dimension=0, tiled=True).reshape(
        piece_len
    )
    return (layer_output, input_gradient, weight_gradients)


def solution(mesh):
    placed = (
        P("dp", "blk", None),
        P(),
        P(),
        P(),
        P(),
        P(),
        P(),
        P(),
        P(),
        P(),
        P(),
        P(),
        P(),
        P(),
        P("dp", "blk", None),
        P("dp", None, "blk", None),
        P(),
        P(),
        P("dp"),
        P("dp"),
        P("dp"),
        P("dp"),
    )
    fits = (mesh.shape["dp"], mesh.shape["blk"]) == (CHIPS, 2)
    layer = fused_layer if fits else plain_layer
    return jax.shard_map(
        layer,
        mesh=mesh,
        in_specs=placed,
        out_specs=(P("dp", "blk", None), P("dp", "blk", None), P(("dp", "blk"))),
        check_vma=False,
    )
```

```python
import jax
import jax.numpy as jnp
from jax import lax
from jax.experimental import pallas as pl
from jax.experimental.pallas import tpu as pltpu
from jax.sharding import PartitionSpec as P

HEADS = 12
HEAD_DIM = 64
WIDTH = 768
FF = 3072
BLOCK = 256
ROW = 512
UNIT = 288
CHIPS = 16
LANES = 128

MESH = pl.DeviceIdType.MESH
LOW = jnp.bfloat16
FULL = jnp.float32

norm_eps = 1e-12


def dot_nn(left, right):
    return jnp.dot(left, right, preferred_element_type=FULL)


def dot_nt(left, right):
    return lax.dot_general(left, right, (((1,), (1,)), ((), ())), preferred_element_type=FULL)


def dot_tn(left, right):
    return lax.dot_general(left, right, (((0,), (0,)), ((), ())), preferred_element_type=FULL)


def both(own, other):
    return jnp.concatenate([own, other], axis=0)


def col_sum(field):
    return jnp.sum(field, axis=0, keepdims=True)


def row_mean(field):
    return jnp.mean(field, axis=-1, keepdims=True)


SCHEDULE = {
    "reduce": (
        ("first", 3, 1),
    ),
    "slopes": (
        ("first", 3, 0),
    ),
    "norm": (
        ("second", 3, 1),
    ),
    "expand": (
        ("pair", 2, 2),
        ("pair", 3, 2),
        ("second", 3, 0),
    ),
    "output": (
        ("first", 1, 1),
    ),
    "heads0": (
        ("first", 1, 0),
    ),
    "heads2": (
        ("second", 1, 1),
        ("first", 2, 0),
    ),
    "keys": (
        ("pair", 1, 2),
    ),
    "project": (
        ("first", 0, 0),
        ("pair", 0, 2),
        ("add", 3, 2),
        ("second", 3, 2),
        ("second", 2, 0),
        ("third", 3, 1),
    ),
    "bias0": (
        ("second", 0, 0),
        ("first", 0, 1),
        ("third", 3, 0),
        ("second", 1, 0),
        ("third", 1, 1),
        ("add", 2, 2),
    ),
    "bias1": (
        ("third", 0, 0),
        ("second", 0, 1),
        ("third", 2, 0),
        ("add", 0, 2),
        ("first", 2, 1),
        ("third", 3, 2),
    ),
    "bias2": (
        ("third", 1, 0),
        ("third", 0, 1),
        ("second", 0, 2),
        ("second", 2, 1),
        ("add", 1, 2),
        ("second", 1, 2),
    ),
    "bias3": (
        ("third", 0, 2),
        ("third", 2, 1),
        ("second", 2, 2),
        ("third", 2, 2),
        ("third", 1, 2),
        ("finish", 0, 0),
        ("finish", 0, 1),
    ),
    "end1": (
        ("finish", 0, 2),
    ),
}


def aligned(start, step):
    return pl.multiple_of(start, step)


def layer_kernel(
    hidden,
    upstream,
    teacher,
    w_project,
    w_output,
    w_expand,
    w_reduce,
    vectors,
    scalars,
    layer_output,
    input_gradient,
    grads,
    wp,
    wo,
    we,
    wr,
    te,
    up,
    x_row,
    vector_at,
    q_own,
    k_row,
    v_row,
    soft,
    att_own,
    att_oth,
    mix_own,
    mix_oth,
    act_own,
    act_oth,
    slope,
    norm_one,
    resid_two,
    resid_one,
    gred_own,
    gred_oth,
    gexp_own,
    gexp_oth,
    gbr_own,
    gbr_oth,
    gatt,
    qt,
    gat,
    dkv_out,
    dkv_in,
    gpj_own,
    gpj_oth,
    live_map,
    out_own,
    gin_own,
    grad,
    pair_in,
    first_in,
    second_in,
    far_in,
    total,
    total_oth,
    flat,
    placed,
    bias_sum,
    bias_in,
    load_sem,
    vector_sem,
    core_send,
    core_recv,
    pair_send,
    pair_recv,
    first_send,
    first_recv,
    second_send,
    second_recv,
    far_send,
    far_recv,
    bias_send,
    bias_recv,
    fix_send,
    fix_recv,
    out_sem,
):
    dp = lax.axis_index("dp")
    blk = lax.axis_index("blk")
    oth = 1 - blk
    xx = dp % 2
    yy = (dp // 2) % 2
    zz = dp // 4
    column = dp % 4
    outer = (zz == 0) | (zz == 3)
    core_dev = (dp, oth)
    x_dev = (dp + 1 - 2 * xx, blk)
    y_dev = (dp + 2 - 4 * yy, blk)
    pair_dev = (jnp.where(zz % 2 == 0, dp + 4, dp - 4), blk)
    device = dp * 2 + blk

    def load(at, src, dst):
        copy = pltpu.make_async_copy(src, dst, load_sem.at[at])
        copy.start()
        return copy

    own_rows = pl.ds(aligned(blk * BLOCK, BLOCK), BLOCK)
    oth_rows = pl.ds(aligned(oth * BLOCK, BLOCK), BLOCK)
    load_x = load(0, hidden, x_row.at[own_rows])
    load_wp = load(1, w_project, wp)
    small = []
    for at, (src, dst) in enumerate(zip(vectors, vector_at)):
        small.append(pltpu.make_async_copy(src, dst.at[0], vector_sem.at[at]))
    for copy in small:
        copy.start()
    load_wo = load(2, w_output, wo)
    load_we = load(3, w_expand, we)
    load_wr = load(4, w_reduce, wr)
    load_up = load(5, upstream, up)
    load_te = load(6, teacher, te)
    (
        query_bias,
        value_bias,
        output_bias,
        first_gain,
        first_shift,
        expand_bias,
        reduce_bias,
        second_gain,
        second_shift,
        start_vector,
        end_vector,
    ) = vector_at

    barrier = pltpu.get_barrier_semaphore()

    def greet(dev):
        pl.semaphore_signal(barrier, inc=1, device_id=dev, device_id_type=MESH)

    greet(core_dev)
    greet(x_dev)
    greet(y_dev)
    for step in range(1, 4):
        greet((lax.rem(dp + 4 * step, CHIPS), blk))

    @pl.when((blk == 1) & (dp < CHIPS - 1))
    def _():
        greet((dp + 1, 0))

    def project_cols(rows, at, bias):
        part = dot_nn(x_row[rows, :], wp[:, pl.ds(at, 256)])
        if bias is not None:
            part = part + bias
        return part.astype(LOW)

    load_x.wait()
    load_wp.wait()
    for copy in small:
        copy.wait()
    for tile in range(3):
        cols = slice(256 * tile, 256 * tile + 256)
        q_part = project_cols(own_rows, 256 * tile, query_bias[:, cols])
        q_own[:, cols] = q_part * jnp.asarray(HEAD_DIM ** (-0.5), LOW)
    for tile in range(3):
        cols = slice(256 * tile, 256 * tile + 256)
        k_row[own_rows, cols] = project_cols(own_rows, WIDTH + 256 * tile, None)
        v_row[own_rows, cols] = project_cols(
            own_rows, 2 * WIDTH + 256 * tile, value_bias[:, cols]
        )

    pl.semaphore_wait(barrier, 6 + ((blk == 0) & (dp > 0)).astype(jnp.int32))

    def to_core(at, src, dst):
        copy = pltpu.make_async_remote_copy(
            src_ref=src,
            dst_ref=dst,
            send_sem=core_send.at[at],
            recv_sem=core_recv.at[at],
            device_id=core_dev,
            device_id_type=MESH,
        )
        copy.start()
        return copy

    core_copies = []
    send_x = to_core(0, x_row.at[own_rows], x_row.at[own_rows])
    core_copies.append(send_x)
    length, start_at, end_at, answered = (ref[...].reshape(1, 1) for ref in scalars)
    key_at = lax.broadcasted_iota(jnp.int32, (1, ROW), 1)
    key_live = key_at < length
    token_at = blk * BLOCK + lax.broadcasted_iota(jnp.int32, (BLOCK, 1), 0)
    row_live = (token_at < length).astype(FULL)
    live_map[...] = jnp.where(key_live, 1.0 / ROW, 0.0) * row_live
    pltpu.make_async_remote_copy(
        src_ref=x_row.at[oth_rows],
        dst_ref=x_row.at[oth_rows],
        send_sem=core_send.at[0],
        recv_sem=core_recv.at[0],
        device_id=core_dev,
        device_id_type=MESH,
    ).wait_recv()
    for tile in range(3):
        cols = slice(256 * tile, 256 * tile + 256)
        k_row[oth_rows, cols] = project_cols(oth_rows, WIDTH + 256 * tile, None)
        v_row[oth_rows, cols] = project_cols(
            oth_rows, 2 * WIDTH + 256 * tile, value_bias[:, cols]
        )

    lane = lax.broadcasted_iota(jnp.int32, (1, LANES), 1)
    head_lanes = ((lane < HEAD_DIM).astype(LOW), (lane >= HEAD_DIM).astype(LOW))

    @pl.loop(0, HEADS // 2)
    def _(pair):
        cols = pl.ds(aligned(pair * LANES, LANES), LANES)
        q_pair = q_own[:, cols]
        k_pair = k_row[:, cols]
        v_pair = v_row[:, cols]
        gathered = None
        for side in range(2):
            scores = dot_nt(q_pair * head_lanes[side], k_pair)
            scores = jnp.where(key_live, scores, -1e30)
            peak = jnp.max(scores, axis=-1, keepdims=True)
            terms = jnp.exp(scores - peak)
            scale = 1.0 / jnp.sum(terms, axis=-1, keepdims=True)
            soft_low = (terms * scale).astype(LOW)
            soft[2 * pair + side] = soft_low
            part = dot_nn(soft_low, v_pair * head_lanes[side])
            gathered = part if gathered is None else gathered + part
        att_own[:, cols] = gathered.astype(LOW)

    core_copies.append(to_core(1, att_own, att_oth))

    load_wo.wait()
    branch = dot_nn(att_own[...], wo[...]) + output_bias[...]
    resid = x_row[own_rows, :].astype(FULL) + branch
    centre = resid - row_mean(resid)
    scale_one = lax.rsqrt(row_mean(centre * centre) + norm_eps)
    normal = centre * scale_one
    norm_one[...] = normal
    mix_own[...] = (normal * first_gain[...] + first_shift[...]).astype(LOW)
    core_copies.append(to_core(2, mix_own, mix_oth))

    load_we.wait()

    @pl.loop(0, 6)
    def _(at):
        cols = pl.ds(aligned(at * 512, 512), 512)
        expanded = dot_nn(mix_own[...], we[:, cols]) + expand_bias[:, cols]
        gate = 0.5 + 0.5 * lax.erf(expanded * (2.0**-0.5))
        bell = jnp.exp(expanded * expanded * -0.5) * ((2.0 * jnp.pi) ** -0.5)
        act_own[:, cols] = (expanded * gate).astype(LOW)
        slope[:, cols] = (gate + expanded * bell).astype(LOW)

    core_copies.append(to_core(3, act_own, act_oth))
    load_wr.wait()
    reduced = dot_nn(act_own[...], wr[...]) + reduce_bias[...]
    mixed = norm_one[...] * first_gain[...] + first_shift[...]
    resid = mixed + reduced
    centre = resid - row_mean(resid)
    scale_two = lax.rsqrt(row_mean(centre * centre) + norm_eps)
    normal = centre * scale_two
    out_own[...] = (normal * second_gain[...] + second_shift[...]).astype(LOW)
    store_out = pltpu.make_async_copy(out_own, layer_output, out_sem.at[0])
    store_out.start()

    answered = answered > 0
    start_slot = jnp.where(answered, start_at, 0)
    end_slot = jnp.where(answered, end_at, 0)
    load_up.wait()
    cot = up[...].astype(FULL) * row_live
    cot = cot + (token_at == start_slot).astype(FULL) * start_vector[...]
    cot = cot + (token_at == end_slot).astype(FULL) * end_vector[...]

    def put_bias(first_row, vector):
        for at in range(vector.shape[1] // LANES):
            bias_sum[first_row + at : first_row + at + 1, :] = vector[
                :, at * LANES : (at + 1) * LANES
            ]

    put_bias(60, col_sum(cot * normal))
    put_bias(66, col_sum(cot))
    pulled = cot * second_gain[...]
    pulled = scale_two * (pulled - row_mean(pulled) - normal * row_mean(pulled * normal))
    resid_two[...] = pulled
    pulled_low = pulled.astype(LOW)
    gred_own[...] = pulled_low
    put_bias(54, col_sum(pulled_low.astype(FULL)))
    own_384 = pl.ds(aligned(blk * 384, 384), 384)
    oth_384 = pl.ds(aligned(oth * 384, 384), 384)
    core_copies.append(to_core(4, gred_own.at[:, oth_384], gred_oth))

    def send(src, dst, send_sem, recv_sem, dev):
        pltpu.make_async_remote_copy(
            src_ref=src,
            dst_ref=dst,
            send_sem=send_sem,
            recv_sem=recv_sem,
            device_id=dev,
            device_id_type=MESH,
        ).start()

    def wait_recv(dst, recv_sem):
        pltpu.make_async_remote_copy(
            src_ref=dst,
            dst_ref=dst,
            send_sem=recv_sem,
            recv_sem=recv_sem,
            device_id=core_dev,
            device_id_type=MESH,
        ).wait_recv()

    def wait_send(src, send_sem):
        pltpu.make_async_remote_copy(
            src_ref=src,
            dst_ref=src,
            send_sem=send_sem,
            recv_sem=send_sem,
            device_id=core_dev,
            device_id_type=MESH,
        ).wait_send()

    def owner(plane, x_at, y_at):
        return 4 * plane + 2 * y_at + x_at

    def add_unit(chip, unit, arrivals):
        value = grad[chip, unit].astype(FULL)
        for arrival in arrivals:
            value = value + arrival.astype(FULL)
        grad[chip, unit] = value.astype(LOW)

    def kept(plane):
        return outer if plane in (0, 3) else jnp.logical_not(outer)

    def taking_part(plane, third, step):
        if third == 2:
            pl.when(kept(plane))(step)
        else:
            step()

    def pair_copy(plane):
        return pltpu.make_async_remote_copy(
            src_ref=grad.at[pl.ds(4 * plane, 4), pl.ds(4, 2)],
            dst_ref=pair_in.at[plane // 2],
            send_sem=pair_send.at[plane],
            recv_sem=pair_recv.at[plane],
            device_id=pair_dev,
            device_id_type=MESH,
        )

    def first_copies(plane, third, slots=range(4)):
        one, two = 2 * third, 2 * third + 1
        return [
            pltpu.make_async_remote_copy(
                src_ref=grad.at[chip, unit],
                dst_ref=first_in.at[plane, third, slot],
                send_sem=first_send.at[plane, third, slot],
                recv_sem=first_recv.at[plane, third, slot],
                device_id=dev,
                device_id_type=MESH,
            )
            for chip, unit, slot, dev in (
                (owner(plane, 1 - xx, 1 - yy), one, 0, x_dev),
                (owner(plane, 1 - xx, 1 - yy), two, 1, y_dev),
                (owner(plane, 1 - xx, yy), one, 2, x_dev),
                (owner(plane, xx, 1 - yy), two, 3, y_dev),
            )
            if slot in slots
        ]

    def second_copies(plane, third):
        one, two = 2 * third, 2 * third + 1
        return [
            pltpu.make_async_remote_copy(
                src_ref=grad.at[chip, unit],
                dst_ref=second_in.at[plane, third, slot],
                send_sem=second_send.at[plane, third, slot],
                recv_sem=second_recv.at[plane, third, slot],
                device_id=dev,
                device_id_type=MESH,
            )
            for chip, unit, slot, dev in (
                (owner(plane, xx, 1 - yy), one, 0, y_dev),
                (owner(plane, 1 - xx, yy), two, 1, x_dev),
            )
        ]

    def far_copy(plane, third):
        slot = 6 if third == 2 else 3 * third + jnp.where(zz < plane, zz, zz - 1)
        return pltpu.make_async_remote_copy(
            src_ref=grad.at[owner(plane, xx, yy), pl.ds(2 * third, 2)],
            dst_ref=far_in.at[slot],
            send_sem=far_send.at[plane, third],
            recv_sem=far_recv.at[slot],
            device_id=(owner(plane, xx, yy), blk),
            device_id_type=MESH,
        )

    def pair_step(plane, third):
        @pl.when(jnp.logical_not(kept(plane)))
        def _():
            pair_copy(plane).start()

    def pair_add(plane, third):
        @pl.when(kept(plane))
        def _():
            pair_copy(plane).wait_recv()

            @pl.loop(0, 4)
            def _(chip):
                for unit in range(2):
                    add_unit(4 * plane + chip, 4 + unit, [pair_in[plane // 2, chip, unit]])

            for copy in first_copies(plane, third):
                copy.start()

    def first_step(plane, third):
        for copy in first_copies(plane, third):
            copy.start()

    def second_step(plane, third):
        def step():
            firsts = first_copies(plane, third, (0, 1))
            seconds = second_copies(plane, third)
            for way in range(2):
                chip = (owner(plane, xx, 1 - yy), owner(plane, 1 - xx, yy))[way]
                firsts[way].wait_recv()
                add_unit(chip, 2 * third + way, [first_in[plane, third, way]])
                seconds[way].start()

        taking_part(plane, third, step)

    def third_step(plane, third):
        def step():
            firsts = first_copies(plane, third, (2, 3))
            seconds = second_copies(plane, third)
            for way in range(2):
                firsts[way].wait_recv()
                seconds[way].wait_recv()
                add_unit(
                    owner(plane, xx, yy),
                    2 * third + way,
                    [first_in[plane, third, 2 + way], second_in[plane, third, way]],
                )

            @pl.when(zz != plane)
            def _():
                far_copy(plane, third).start()

        taking_part(plane, third, step)

    def finish_step(_, third):
        slots = (6,) if third == 2 else (3 * third, 3 * third + 1, 3 * third + 2)
        for slot in slots:
            wait_recv(far_in.at[slot], far_recv.at[slot])
        for way in range(2):
            value = grad[dp, 2 * third + way].astype(FULL)
            for slot in slots:
                value = value + far_in[slot, way].astype(FULL)
            total[2 * third + way] = value

    steps = {
        "pair": pair_step,
        "add": pair_add,
        "first": first_step,
        "second": second_step,
        "third": third_step,
        "finish": finish_step,
    }

    def serve(after):
        for what, plane, third in SCHEDULE.get(after, ()):
            steps[what](plane, third)

    def put_unit(at, rows, values):
        chip, unit = (at // 6, at % 6) if isinstance(at, int) else (lax.div(at, 6), lax.rem(at, 6))
        grad[chip, unit, rows, :] = values.astype(LOW)

    core_copies[3].wait_recv()
    core_copies[4].wait_recv()

    def reduce_rows(at):
        cols = pl.ds(aligned(at * WIDTH, WIDTH), WIDTH)
        part = dot_tn(
            both(act_own[:, cols], act_oth[:, cols]), both(gred_own[:, own_384], gred_oth[...])
        )
        for unit in range(8):
            for tile in range(3):
                put_unit(64 + 8 * at + unit, slice(96 * tile, 96 * tile + 96), part[
                    96 * unit : 96 * unit + 96, LANES * tile : LANES * tile + LANES
                ])

    @pl.loop(1, 4)
    def _(at):
        reduce_rows(at)

    serve("reduce")
    reduce_rows(0)

    @pl.loop(0, 6)
    def _(at):
        half = jnp.where(at < 3, oth, blk)
        part_at = lax.rem(at, 3) * 512
        cols = pl.ds(aligned(half * 1536 + part_at, 512), 512)
        grad_active = dot_nt(gred_own[...], wr[cols, :])
        grad_expanded = (grad_active * slope[:, cols].astype(FULL)).astype(LOW)
        gexp_own[half, :, pl.ds(aligned(part_at, 512), 512)] = grad_expanded
        sums = col_sum(grad_expanded.astype(FULL))
        for tile in range(4):
            bias_sum[pl.ds(30 + half * 12 + lax.rem(at, 3) * 4 + tile, 1), :] = sums[
                :, LANES * tile : LANES * tile + LANES
            ]

    core_copies.append(to_core(5, gexp_own.at[oth], gexp_oth))
    serve("slopes")
    grad_mixed = resid_two[...]
    for half in range(2):
        grad_mixed = grad_mixed + dot_nt(
            gexp_own[half], we[:, 1536 * half : 1536 * half + 1536]
        )

    normal = norm_one[...]
    put_bias(18, col_sum(grad_mixed * normal))
    put_bias(24, col_sum(grad_mixed))
    pulled = grad_mixed * first_gain[...]
    pulled = scale_one * (pulled - row_mean(pulled) - normal * row_mean(pulled * normal))
    resid_one[...] = pulled
    pulled_low = pulled.astype(LOW)
    gbr_own[...] = pulled_low
    put_bias(12, col_sum(pulled_low.astype(FULL)))
    core_copies.append(to_core(6, gbr_own.at[:, oth_384], gbr_oth))

    serve("norm")

    core_copies[2].wait_recv()
    core_copies[5].wait_recv()

    @pl.loop(0, 6)
    def _(at):
        cols = pl.ds(aligned(at * 256, 256), 256)
        part = dot_tn(
            both(mix_own[...], mix_oth[...]), both(gexp_own[blk, :, cols], gexp_oth[:, cols])
        )
        rows = pl.ds(aligned(at * 48, 48), 48)
        for unit in range(32):
            piece = part[24 * unit : 24 * unit + 24, :]
            put_unit(32 + unit, rows, both(piece[:, :LANES], piece[:, LANES:]))

    serve("expand")
    gatt[...] = dot_nt(gbr_own[...], wo[...]).astype(LOW)
    core_copies[1].wait_recv()
    core_copies[6].wait_recv()
    part = dot_tn(both(att_own[...], att_oth[...]), both(gbr_own[:, own_384], gbr_oth[...]))
    for unit in range(8):
        for tile in range(3):
            put_unit(24 + unit, slice(96 * tile, 96 * tile + 96), part[
                96 * unit : 96 * unit + 96, LANES * tile : LANES * tile + LANES
            ])
    serve("output")

    qt[...] = q_own[...].T
    gat[...] = gatt[...].T
    load_te.wait()

    def head_pair(pair):
        cols = pl.ds(aligned(pair * LANES, LANES), LANES)
        ga_pair = gatt[:, cols]
        k_pair = k_row[:, cols]
        v_pair = v_row[:, cols]
        grad_query = None
        for side in range(2):
            rows = pl.ds(aligned(pair * LANES + side * HEAD_DIM, HEAD_DIM), HEAD_DIM)
            soft_low = soft[2 * pair + side]
            grad_soft = dot_nt(ga_pair * head_lanes[side], v_pair)
            soft_full = soft_low.astype(FULL)
            taught = te[2 * pair + side].astype(FULL) * live_map[...]
            shift = jnp.sum(taught - grad_soft * soft_full, axis=-1, keepdims=True)
            grad_scores = (soft_full * (grad_soft + shift) - taught).astype(LOW)
            part = dot_nn(grad_scores, k_pair * head_lanes[side])
            grad_query = part if grad_query is None else grad_query + part
            slot = pl.ds(aligned(pair * ROW, ROW), ROW)
            at = side * HEAD_DIM
            slope[at : at + HEAD_DIM, slot] = dot_nn(qt[rows, :], grad_scores).astype(LOW)
            at = at + LANES
            slope[at : at + HEAD_DIM, slot] = dot_nn(gat[rows, :], soft_low).astype(LOW)
        gpj_own[:, cols] = (grad_query * HEAD_DIM ** (-0.5)).astype(LOW)

    for part in range(3):

        @pl.loop(2 * part, 2 * part + 2)
        def _(pair):
            head_pair(pair)

        serve("heads" + str(part))

    def turned(pair, block, first):
        lanes = pl.ds(aligned(pair * ROW + block * BLOCK, BLOCK), BLOCK)
        return slope[first : first + LANES, lanes].T

    for pair in range(HEADS // 2):
        for first in (0, LANES):
            at = pair * LANES + first * (WIDTH // LANES)
            dkv_out[:, at : at + LANES] = turned(pair, oth, first)
    core_copies.append(to_core(7, dkv_out, dkv_in))
    core_copies[7].wait_recv()
    for pair in range(HEADS // 2):
        for first in (0, LANES):
            at = pair * LANES + first * (WIDTH // LANES)
            gpj_own[:, WIDTH + at : WIDTH + at + LANES] = (
                turned(pair, blk, first).astype(FULL) + dkv_in[:, at : at + LANES].astype(FULL)
            ).astype(LOW)
    serve("keys")
    own_1152 = pl.ds(aligned(blk * 1152, 1152), 1152)
    oth_1152 = pl.ds(aligned(oth * 1152, 1152), 1152)
    core_copies.append(to_core(8, gpj_own.at[:, oth_1152], gpj_oth))
    put_bias(0, col_sum(gpj_own[:, :WIDTH].astype(FULL)))
    put_bias(6, col_sum(gpj_own[:, 2 * WIDTH :].astype(FULL)))

    def input_gradient_part():
        gin_own[...] = (resid_one[...] + dot_nt(gpj_own[...], wp[...])).astype(LOW)
        pltpu.make_async_copy(gin_own, input_gradient, out_sem.at[1]).start()

    core_copies[8].wait_recv()

    @pl.loop(0, 3)
    def _(at):
        cols = pl.ds(aligned(at * 384, 384), 384)
        mine = pl.ds(aligned(blk * 1152 + at * 384, 384), 384)
        part = dot_tn(
            both(x_row[own_rows, :], x_row[oth_rows, :]), both(gpj_own[:, mine], gpj_oth[:, cols])
        )
        for unit in range(24):
            for tile in range(3):
                rows = pl.ds(aligned(at * 96 + 32 * tile, 32), 32)
                put_unit(unit, rows, part[
                    32 * unit : 32 * unit + 32, LANES * tile : LANES * tile + LANES
                ])

    serve("project")
    input_gradient_part()
    serve("input")

    def bias_leaves(at, here, dev):
        @pl.when(here)
        def _():
            send(bias_sum, bias_in.at[at], bias_send.at[0], bias_recv.at[at], dev)

    def bias_comes(at, there):
        @pl.when(there)
        def _():
            wait_recv(bias_in.at[at], bias_recv.at[at])
            bias_sum[...] += bias_in[at]

    corner = (xx == 1) & (yy == 1)
    last = dp == CHIPS - 1
    bias_leaves(0, xx == 0, x_dev)
    serve("bias0")
    bias_comes(0, xx == 1)
    bias_leaves(1, (xx == 1) & (yy == 0), y_dev)
    serve("bias1")
    bias_comes(1, corner)

    @pl.when(corner & (zz < 3))
    def _():
        send(
            bias_sum,
            bias_in.at[2 + zz],
            bias_send.at[0],
            bias_recv.at[2 + zz],
            (CHIPS - 1, blk),
        )

    serve("bias2")

    @pl.when(last)
    def _():
        for at in range(2, 5):
            wait_recv(bias_in.at[at], bias_recv.at[at])
            bias_sum[...] += bias_in[at]

    @pl.when(last & (blk == 0))
    def _():
        send(bias_sum, bias_in.at[5], bias_send.at[0], bias_recv.at[5], core_dev)

    serve("bias3")

    @pl.when(last & (blk == 1))
    def _():
        wait_recv(bias_in.at[5], bias_recv.at[5])
        flat[1728:1800, :] = bias_sum[...] + bias_in[5]

    def lay_out(source, first, column_half, unit):
        kind_at = 3 * device + unit
        kinds = (
            (kind_at < 24, 32, 9),
            (((kind_at >= 24) & (kind_at < 32)) | (kind_at >= 64), 96, 3),
            ((kind_at >= 32) & (kind_at < 64), 24, 12),
        )
        for fits, rows, tiles in kinds:

            @pl.when(fits)
            def _():
                for tile in range(tiles):
                    for group in range(rows // 8):
                        at = rows * tile + 8 * group
                        to = 576 * unit + 16 * group * tiles + tile + column_half * tiles
                        flat[pl.ds(to, 8, stride=2 * tiles), :] = source[
                            first + unit, at : at + 8, :
                        ]

    def to_core_when(at, here, src, dst):
        @pl.when(here)
        def _():
            send(src, dst, core_send.at[at], core_recv.at[at], core_dev)

    serve("end0")
    to_core_when(9, blk == 1, total.at[pl.ds(0, 3)], total_oth)
    to_core_when(10, blk == 0, total.at[pl.ds(3, 1)], total_oth.at[pl.ds(0, 1)])

    @pl.when(blk == 1)
    def _():
        lay_out(total, 3, 1, 0)
        wait_recv(total_oth.at[pl.ds(0, 1)], core_recv.at[10])
        lay_out(total_oth, 0, 0, 0)
        send(flat.at[0:72], flat.at[1728:1800], fix_send.at[0], fix_recv.at[0], core_dev)

    @pl.when(blk == 0)
    def _():
        for unit in range(3):
            lay_out(total, 0, 0, unit)
        wait_recv(total_oth, core_recv.at[9])
        for unit in range(3):
            lay_out(total_oth, 0, 1, unit)

        @pl.when(dp > 0)
        def _():
            send(flat.at[0:72], flat.at[1728:1800], fix_send.at[0], fix_recv.at[0], (dp - 1, 1))

    serve("end1")
    to_core_when(11, blk == 0, total.at[pl.ds(4, 2)], total_oth.at[pl.ds(1, 2)])

    @pl.when(blk == 1)
    def _():
        for unit in range(1, 3):
            lay_out(total, 3, 1, unit)
        wait_recv(total_oth.at[pl.ds(1, 2)], core_recv.at[11])
        for unit in range(1, 3):
            lay_out(total_oth, 0, 0, unit)

    @pl.when(device < 2 * CHIPS - 1)
    def _():
        wait_recv(flat.at[1728:1800], fix_recv.at[0])

    shift = 32 * lax.rem(device, 4)
    skip = (9 * device) // 4
    stays = lane < LANES - shift

    @pl.loop(0, 31)
    def _(at):
        rows = at * 56
        first = pltpu.roll(flat[pl.ds(rows + skip, 56), :], LANES - shift, 1)
        second = pltpu.roll(flat[pl.ds(rows + skip + 1, 56), :], LANES - shift, 1)
        placed[pl.ds(aligned(rows, 8), 56), :] = jnp.where(stays, first, second)

    store_grads = pltpu.make_async_copy(placed, grads, out_sem.at[2])
    store_grads.start()

    for copy in core_copies:
        copy.wait_send()

    @pl.when(blk == 1)
    def _():
        wait_send(total.at[pl.ds(0, 3)], core_send.at[9])

    @pl.when(blk == 0)
    def _():
        wait_send(total.at[pl.ds(3, 1)], core_send.at[10])
        wait_send(total.at[pl.ds(4, 2)], core_send.at[11])

    for plane in range(4):

        @pl.when(jnp.logical_not(kept(plane)))
        def _():
            pair_copy(plane).wait_send()

        for third in range(3):

            def sent():
                for copy in first_copies(plane, third) + second_copies(plane, third):
                    copy.wait_send()

                @pl.when(zz != plane)
                def _():
                    far_copy(plane, third).wait_send()

            taking_part(plane, third, sent)

    @pl.when(jnp.logical_not(last & (blk == 1)))
    def _():
        wait_send(bias_sum, bias_send.at[0])

    @pl.when(device > 0)
    def _():
        wait_send(flat.at[0:72], fix_send.at[0])

    store_out.wait()
    pltpu.make_async_copy(gin_own, input_gradient, out_sem.at[1]).wait()
    store_grads.wait()


def hand_over(*refs):
    sources, targets, held, sems = refs[:3], refs[3:6], refs[6:9], refs[9]
    reads = [pltpu.make_async_copy(*pair, sems.at[at]) for at, pair in enumerate(zip(sources, held))]
    writes = [
        pltpu.make_async_copy(*pair, sems.at[3 + at]) for at, pair in enumerate(zip(held, targets))
    ]
    for read in reads:
        read.start()
    for read, write in zip(reads, writes):
        read.wait()
        write.start()
    for write in writes:
        write.wait()


def fused_layer(
    hidden_in,
    project_weight,
    output_weight,
    expand_weight,
    reduce_weight,
    query_bias,
    value_bias,
    output_bias,
    first_gain,
    first_shift,
    expand_bias,
    reduce_bias,
    second_gain,
    second_shift,
    upstream,
    teacher_maps,
    start_vector,
    end_vector,
    valid_length,
    start_index,
    end_index,
    answerable,
):
    vectors = (
        query_bias,
        value_bias,
        output_bias,
        first_gain,
        first_shift,
        expand_bias,
        reduce_bias,
        second_gain,
        second_shift,
        start_vector,
        end_vector,
    )
    scalars = (valid_length, start_index, end_index, answerable)
    anywhere = pl.BlockSpec(memory_space=pl.ANY)
    in_vmem = pl.BlockSpec(memory_space=pltpu.VMEM)

    def low(*shape):
        return pltpu.VMEM(shape, LOW)

    def full(*shape):
        return pltpu.VMEM(shape, FULL)

    dma = pltpu.SemaphoreType.DMA
    scratch = [
        low(WIDTH, 3 * WIDTH),
        low(WIDTH, WIDTH),
        low(WIDTH, FF),
        low(FF, WIDTH),
        low(HEADS, BLOCK, ROW),
        low(BLOCK, WIDTH),
        low(ROW, WIDTH),
        tuple(full(1, vector.shape[0]) for vector in vectors),
        low(BLOCK, WIDTH),
        low(ROW, WIDTH),
        low(ROW, WIDTH),
        low(HEADS, BLOCK, ROW),
        low(BLOCK, WIDTH),
        low(BLOCK, WIDTH),
        low(BLOCK, WIDTH),
        low(BLOCK, WIDTH),
        low(BLOCK, FF),
        low(BLOCK, FF),
        low(BLOCK, FF),
        full(BLOCK, WIDTH),
        full(BLOCK, WIDTH),
        full(BLOCK, WIDTH),
        low(BLOCK, WIDTH),
        low(BLOCK, WIDTH // 2),
        low(2, BLOCK, FF // 2),
        low(BLOCK, FF // 2),
        low(BLOCK, WIDTH),
        low(BLOCK, WIDTH // 2),
        low(BLOCK, WIDTH),
        low(WIDTH, BLOCK),
        low(WIDTH, BLOCK),
        low(BLOCK, 2 * WIDTH),
        low(BLOCK, 2 * WIDTH),
        low(BLOCK, 3 * WIDTH),
        low(BLOCK, 3 * WIDTH // 2),
        full(BLOCK, ROW),
        low(BLOCK, WIDTH),
        low(BLOCK, WIDTH),
        low(CHIPS, 6, UNIT, LANES),
        low(2, 4, 2, UNIT, LANES),
        low(4, 3, 4, UNIT, LANES),
        low(4, 3, 2, UNIT, LANES),
        low(7, 2, UNIT, LANES),
        full(6, UNIT, LANES),
        full(3, UNIT, LANES),
        full(1816, LANES),
        full(1736, LANES),
        full(72, LANES),
        full(6, 72, LANES),
        dma((7,)),
        dma((len(vectors),)),
        dma((12,)),
        dma((12,)),
        dma((4,)),
        dma((4,)),
        dma((4, 3, 4)),
        dma((4, 3, 4)),
        dma((4, 3, 2)),
        dma((4, 3, 2)),
        dma((4, 3)),
        dma((7,)),
        dma((1,)),
        dma((6,)),
        dma((1,)),
        dma((1,)),
        dma((3,)),
    ]
    results = (
        jax.ShapeDtypeStruct((BLOCK, WIDTH), LOW),
        jax.ShapeDtypeStruct((BLOCK, WIDTH), LOW),
        jax.ShapeDtypeStruct((1736, LANES), FULL),
    )
    made = pl.pallas_call(
        layer_kernel,
        out_shape=results,
        in_specs=[anywhere] * 7 + [(anywhere,) * len(vectors), (in_vmem,) * len(scalars)],
        out_specs=(anywhere,) * 3,
        scratch_shapes=scratch,
        compiler_params=pltpu.CompilerParams(
            collective_id=0, has_side_effects=True, vmem_limit_bytes=63 * 2**20
        ),
        name="encoder_layer",
    )(
        hidden_in.reshape(BLOCK, WIDTH),
        upstream.reshape(BLOCK, WIDTH),
        teacher_maps.reshape(HEADS, BLOCK, ROW),
        project_weight,
        output_weight,
        expand_weight,
        reduce_weight,
        vectors,
        scalars,
    )
    layer_output, input_gradient, grads = pl.pallas_call(
        hand_over,
        out_shape=results,
        in_specs=[anywhere] * 3,
        out_specs=(anywhere,) * 3,
        scratch_shapes=[pltpu.VMEM(result.shape, result.dtype) for result in results] + [dma((6,))],
        name="hand_over",
    )(*made)
    return (
        layer_output.reshape(1, BLOCK, WIDTH),
        input_gradient.reshape(1, BLOCK, WIDTH),
        grads.reshape(-1)[: 3 * 2 * UNIT * LANES + UNIT],
    )


def layer_norm(field_in, gain_vec, shift_vec):
    centre = field_in - jnp.mean(field_in, axis=-1, keepdims=True)
    spread = jnp.mean(centre * centre, axis=-1, keepdims=True)
    return centre * lax.rsqrt(spread + norm_eps) * gain_vec + shift_vec


def gelu_exact(field_in):
    return jax.nn.gelu(field_in, approximate=False)


def outer_sum(left, right):
    return jnp.einsum("nd,ne->de", left, right, preferred_element_type=jnp.float32)


def column_sum(values_low):
    return jnp.sum(values_low.astype(jnp.float32), axis=0)


def plain_layer(
    hidden_in,
    project_weight,
    output_weight,
    expand_weight,
    reduce_weight,
    query_bias,
    value_bias,
    output_bias,
    first_gain,
    first_shift,
    expand_bias,
    reduce_bias,
    second_gain,
    second_shift,
    upstream,
    teacher_maps,
    start_vector,
    end_vector,
    valid_length,
    start_index,
    end_index,
    answerable,
):
    row_count, block_len, width = hidden_in.shape
    blocks = lax.axis_size("blk")
    length = block_len * blocks
    offset = lax.axis_index("blk") * block_len
    token_count = row_count * block_len
    positions = offset + jnp.arange(block_len, dtype=jnp.int32)
    key_live = jnp.arange(length, dtype=jnp.int32)[None, :] < valid_length[:, None]
    row_live = positions[None, :] < valid_length[:, None]
    score_scale = HEAD_DIM ** (-0.5)
    tokens = hidden_in.reshape(token_count, width)
    joined_bias = jnp.concatenate([query_bias, jnp.zeros_like(query_bias), value_bias])
    project = (
        jnp.dot(tokens, project_weight, preferred_element_type=jnp.float32) + joined_bias
    ).astype(jnp.bfloat16)
    queries = project[:, :width].reshape(row_count, block_len, HEADS, HEAD_DIM)
    keys_own = project[:, width : 2 * width].reshape(row_count, block_len, width)
    values_own = project[:, 2 * width :].reshape(row_count, block_len, width)
    keys_all, values_all = (
        lax.all_gather(keys_own, "blk", axis=1, tiled=True),
        lax.all_gather(values_own, "blk", axis=1, tiled=True),
    )

    def scores_of(keys_full):
        raw = (
            jnp.einsum(
                "rqhe,rkhe->rhqk",
                queries,
                keys_full.reshape(row_count, length, HEADS, HEAD_DIM),
                preferred_element_type=jnp.float32,
            )
            * score_scale
        )
        return jnp.where(key_live[:, None, None, :], raw, -1e30)

    scores = scores_of(keys_all)
    row_peak = jnp.max(scores, axis=-1, keepdims=True)
    expo_terms = jnp.exp(scores - row_peak)
    row_total = jnp.sum(expo_terms, axis=-1, keepdims=True)
    soft_low = (expo_terms / row_total).astype(jnp.bfloat16)
    log_total = row_peak + jnp.log(row_total)
    attended = (
        jnp.einsum(
            "rhqk,rkhe->rqhe",
            soft_low,
            values_all.reshape(row_count, length, HEADS, HEAD_DIM),
            preferred_element_type=jnp.float32,
        )
        .reshape(token_count, width)
        .astype(jnp.bfloat16)
    )
    branch = jnp.dot(attended, output_weight, preferred_element_type=jnp.float32) + output_bias
    resid_one = tokens.astype(jnp.float32) + branch
    mixed, first_pull = jax.vjp(layer_norm, resid_one, first_gain, first_shift)
    mixed_low = mixed.astype(jnp.bfloat16)
    expanded = jnp.dot(mixed_low, expand_weight, preferred_element_type=jnp.float32) + expand_bias
    active, gelu_pull = jax.vjp(gelu_exact, expanded)
    active_low = active.astype(jnp.bfloat16)
    reduced = jnp.dot(active_low, reduce_weight, preferred_element_type=jnp.float32) + reduce_bias
    result, second_pull = jax.vjp(layer_norm, mixed + reduced, second_gain, second_shift)
    layer_output = result.astype(jnp.bfloat16).reshape(row_count, block_len, width)
    start_slot = jnp.where(answerable > 0, start_index, 0)
    end_slot = jnp.where(answerable > 0, end_index, 0)
    cotangent = (
        upstream.astype(jnp.float32) * row_live[..., None].astype(jnp.float32)
        + (positions[None, :] == start_slot[:, None])[..., None].astype(jnp.float32) * start_vector
        + (positions[None, :] == end_slot[:, None])[..., None].astype(jnp.float32) * end_vector
    )
    grad_resid_two, grad_second_gain, grad_second_shift = second_pull(
        cotangent.reshape(token_count, width)
    )
    grad_reduced = grad_resid_two.astype(jnp.bfloat16)
    grad_active = jnp.einsum(
        "nd,fd->nf", grad_reduced, reduce_weight, preferred_element_type=jnp.float32
    )
    grad_expanded = gelu_pull(grad_active)[0].astype(jnp.bfloat16)
    grad_mixed = grad_resid_two + jnp.einsum(
        "nf,df->nd", grad_expanded, expand_weight, preferred_element_type=jnp.float32
    )
    grad_resid_one, grad_first_gain, grad_first_shift = first_pull(grad_mixed)
    grad_branch = grad_resid_one.astype(jnp.bfloat16)
    grad_attended = jnp.einsum(
        "ne,de->nd", grad_branch, output_weight, preferred_element_type=jnp.float32
    )
    grad_attended = grad_attended.astype(jnp.bfloat16).reshape(
        row_count, block_len, HEADS, HEAD_DIM
    )
    keys_back, values_back = (
        lax.all_gather(keys_own, "blk", axis=1, tiled=True),
        lax.all_gather(values_own, "blk", axis=1, tiled=True),
    )
    keys_heads = keys_back.reshape(row_count, length, HEADS, HEAD_DIM)
    values_heads = values_back.reshape(row_count, length, HEADS, HEAD_DIM)
    soft = jnp.exp(scores_of(keys_back) - log_total)
    both_live = row_live[:, None, :, None] & key_live[:, None, None, :]
    teacher_live = jnp.where(both_live, teacher_maps.astype(jnp.float32), 0.0)
    teacher_total = jnp.sum(teacher_live, axis=-1, keepdims=True)
    grad_soft = jnp.einsum(
        "rqhe,rkhe->rhqk", grad_attended, values_heads, preferred_element_type=jnp.float32
    )
    row_delta = jnp.sum(grad_soft * soft, axis=-1, keepdims=True)
    grad_scores = (
        soft * (grad_soft - row_delta) + (teacher_total * soft - teacher_live) / length
    ).astype(jnp.bfloat16)
    grad_query = (
        jnp.einsum("rhqk,rkhe->rqhe", grad_scores, keys_heads, preferred_element_type=jnp.float32)
        * score_scale
    )
    grad_keys = (
        jnp.einsum(
            "rhqk,rqhe->rkhe", grad_scores, queries, preferred_element_type=jnp.float32
        ).reshape(row_count, length, width)
        * score_scale
    )
    grad_values = jnp.einsum(
        "rhqk,rqhe->rkhe", soft_low, grad_attended, preferred_element_type=jnp.float32
    ).reshape(row_count, length, width)
    keys_grad_own, values_grad_own = (
        lax.psum_scatter(
            grad_keys.astype(jnp.bfloat16), "blk", scatter_dimension=1, tiled=True
        ).astype(jnp.float32),
        lax.psum_scatter(
            grad_values.astype(jnp.bfloat16), "blk", scatter_dimension=1, tiled=True
        ).astype(jnp.float32),
    )
    grad_project = jnp.concatenate(
        [
            grad_query.reshape(token_count, width),
            keys_grad_own.reshape(token_count, width),
            values_grad_own.reshape(token_count, width),
        ],
        axis=1,
    ).astype(jnp.bfloat16)
    grad_input = grad_resid_one + jnp.einsum(
        "ne,de->nd", grad_project, project_weight, preferred_element_type=jnp.float32
    )
    input_gradient = grad_input.astype(jnp.bfloat16).reshape(row_count, block_len, width)
    (
        tokens_both,
        project_both,
        attended_both,
        branch_both,
        mixed_both,
        expanded_both,
        active_both,
        reduced_both,
    ) = (
        lax.all_gather(tokens, "blk", axis=0, tiled=True),
        lax.all_gather(grad_project, "blk", axis=0, tiled=True),
        lax.all_gather(attended, "blk", axis=0, tiled=True),
        lax.all_gather(grad_branch, "blk", axis=0, tiled=True),
        lax.all_gather(mixed_low, "blk", axis=0, tiled=True),
        lax.all_gather(grad_expanded, "blk", axis=0, tiled=True),
        lax.all_gather(active_low, "blk", axis=0, tiled=True),
        lax.all_gather(grad_reduced, "blk", axis=0, tiled=True),
    )
    project_sums = column_sum(project_both)
    norm_grads = lax.psum(
        (grad_first_gain, grad_first_shift, grad_second_gain, grad_second_shift), "blk"
    )
    flat_grads = jnp.concatenate(
        [
            outer_sum(tokens_both, project_both).reshape(-1),
            outer_sum(attended_both, branch_both).reshape(-1),
            outer_sum(mixed_both, expanded_both).reshape(-1),
            outer_sum(active_both, reduced_both).reshape(-1),
            project_sums[:width],
            project_sums[2 * width :],
            column_sum(branch_both),
            norm_grads[0],
            norm_grads[1],
            column_sum(expanded_both),
            column_sum(reduced_both),
            norm_grads[2],
            norm_grads[3],
        ]
    )
    data_count = lax.axis_size("dp")
    piece_len = flat_grads.shape[0] // (data_count * blocks)
    mine = lax.dynamic_index_in_dim(
        flat_grads.reshape(data_count, blocks, piece_len), lax.axis_index("blk"), 1, keepdims=False
    )
    weight_gradients = lax.psum_scatter(mine, "dp", scatter_dimension=0, tiled=True).reshape(
        piece_len
    )
    return (layer_output, input_gradient, weight_gradients)


def solution(mesh):
    placed = (
        P("dp", "blk", None),
        P(),
        P(),
        P(),
        P(),
        P(),
        P(),
        P(),
        P(),
        P(),
        P(),
        P(),
        P(),
        P(),
        P("dp", "blk", None),
        P("dp", None, "blk", None),
        P(),
        P(),
        P("dp"),
        P("dp"),
        P("dp"),
        P("dp"),
    )
    fits = (mesh.shape["dp"], mesh.shape["blk"]) == (CHIPS, 2)
    layer = fused_layer if fits else plain_layer
    return jax.shard_map(
        layer,
        mesh=mesh,
        in_specs=placed,
        out_specs=(P("dp", "blk", None), P("dp", "blk", None), P(("dp", "blk"))),
        check_vma=False,
    )
```

```python
import jax
import jax.numpy as jnp
from jax import lax
from jax.experimental import pallas as pl
from jax.experimental.pallas import tpu as pltpu
from jax.sharding import PartitionSpec as P

HEADS = 12
HEAD_DIM = 64
WIDTH = 768
FF = 3072
BLOCK = 256
ROW = 512
UNIT = 288
CHIPS = 16
LANES = 128

MESH = pl.DeviceIdType.MESH
LOW = jnp.bfloat16
FULL = jnp.float32

norm_eps = 1e-12


def dot_nn(left, right):
    return jnp.dot(left, right, preferred_element_type=FULL)


def dot_nt(left, right):
    return lax.dot_general(left, right, (((1,), (1,)), ((), ())), preferred_element_type=FULL)


def dot_tn(left, right):
    return lax.dot_general(left, right, (((0,), (0,)), ((), ())), preferred_element_type=FULL)


def both(own, other):
    return jnp.concatenate([own, other], axis=0)


def col_sum(field):
    return jnp.sum(field, axis=0, keepdims=True)


def row_mean(field):
    return jnp.mean(field, axis=-1, keepdims=True)


SCHEDULE = {
    "reduce0": (
        ("first", 3, 0),
    ),
    "reduce1": (
        ("first", 3, 1),
    ),
    "reduce2": (
        ("pair", 3, 2),
    ),
    "slopes": (
        ("second", 3, 0),
    ),
    "norm": (
        ("second", 3, 1),
    ),
    "output": (
        ("pair", 1, 2),
        ("first", 1, 1),
    ),
    "heads0": (
        ("first", 1, 0),
    ),
    "heads1": (
        ("third", 3, 1),
        ("second", 1, 1),
        ("first", 2, 1),
    ),
    "heads2": (
        ("third", 3, 0),
        ("pair", 2, 2),
    ),
    "keys": (
        ("second", 1, 0),
    ),
    "project": (
        ("first", 0, 0),
        ("first", 0, 1),
    ),
    "input": (
        ("second", 0, 0),
    ),
    "bias0": (
        ("first", 0, 2),
        ("chain", 3, 1),
        ("second", 0, 1),
        ("third", 1, 1),
        ("add", 3, 2),
        ("second", 2, 1),
        ("chain", 3, 0),
        ("third", 0, 0),
        ("third", 1, 0),
    ),
    "bias1": (
        ("second", 0, 2),
        ("second", 3, 2),
        ("first", 2, 0),
    ),
    "bias2": (
        ("add", 1, 2),
        ("third", 0, 1),
        ("add", 2, 2),
        ("third", 2, 1),
        ("third", 0, 2),
        ("third", 3, 2),
        ("chain", 0, 0),
    ),
    "bias3": (
        ("second", 2, 0),
        ("second", 1, 2),
        ("second", 2, 2),
        ("chain", 0, 1),
        ("third", 2, 0),
        ("chain", 0, 2),
        ("third", 1, 2),
        ("third", 2, 2),
    ),
    "end0": (
        ("finish", 0, 0),
        ("finish", 0, 1),
    ),
    "end1": (
        ("finish", 0, 2),
    ),
}
PAIRED = (0, 1, 1, 1)
CHAINED = (True, False, False, True)


def aligned(start, step):
    return pl.multiple_of(start, step)


def layer_kernel(
    hidden,
    upstream,
    teacher,
    w_project,
    w_output,
    w_expand,
    w_reduce,
    vectors,
    scalars,
    layer_output,
    input_gradient,
    grads,
    wp,
    wo,
    we,
    wr,
    te,
    up,
    x_row,
    vector_at,
    q_own,
    k_row,
    v_row,
    soft,
    att_own,
    att_oth,
    mix_own,
    mix_oth,
    act_own,
    act_oth,
    slope,
    norm_one,
    resid_two,
    resid_one,
    gred_own,
    gred_oth,
    gexp_own,
    gexp_oth,
    gbr_own,
    gbr_oth,
    gatt,
    qt,
    gat,
    dkv_out,
    dkv_in,
    gpj_own,
    gpj_oth,
    live_map,
    out_own,
    gin_own,
    grad,
    pair_in,
    first_in,
    second_in,
    far_in,
    total,
    total_oth,
    flat,
    placed,
    bias_sum,
    bias_in,
    load_sem,
    vector_sem,
    core_send,
    core_recv,
    pair_send,
    pair_recv,
    first_send,
    first_recv,
    second_send,
    second_recv,
    far_send,
    far_recv,
    bias_send,
    bias_recv,
    fix_send,
    fix_recv,
    out_sem,
):
    dp = lax.axis_index("dp")
    blk = lax.axis_index("blk")
    oth = 1 - blk
    xx = dp % 2
    yy = (dp // 2) % 2
    zz = dp // 4
    column = dp % 4
    core_dev = (dp, oth)
    x_dev = (dp + 1 - 2 * xx, blk)
    y_dev = (dp + 2 - 4 * yy, blk)
    pair_dev = (jnp.where(zz % 2 == 0, dp + 4, dp - 4), blk)
    device = dp * 2 + blk

    def load(at, src, dst):
        copy = pltpu.make_async_copy(src, dst, load_sem.at[at])
        copy.start()
        return copy

    own_rows = pl.ds(aligned(blk * BLOCK, BLOCK), BLOCK)
    oth_rows = pl.ds(aligned(oth * BLOCK, BLOCK), BLOCK)
    load_x = load(0, hidden, x_row.at[own_rows])
    load_wp = [
        load(6 + part, w_project.at[:, part_cols], wp.at[:, part_cols])
        for part, part_cols in enumerate(pl.ds(WIDTH * part, WIDTH) for part in range(3))
    ]
    small = []
    for at, (src, dst) in enumerate(zip(vectors, vector_at)):
        small.append(pltpu.make_async_copy(src, dst.at[0], vector_sem.at[at]))
    for copy in small:
        copy.start()
    (
        query_bias,
        value_bias,
        output_bias,
        first_gain,
        first_shift,
        expand_bias,
        reduce_bias,
        second_gain,
        second_shift,
        start_vector,
        end_vector,
    ) = vector_at

    barrier = pltpu.get_barrier_semaphore()

    def greet(dev):
        pl.semaphore_signal(barrier, inc=1, device_id=dev, device_id_type=MESH)

    greet(core_dev)
    greet(x_dev)
    greet(y_dev)
    for step in range(1, 4):
        greet((lax.rem(dp + 4 * step, CHIPS), blk))

    @pl.when((blk == 1) & (dp < CHIPS - 1))
    def _():
        greet((dp + 1, 0))

    def to_core(at, src, dst):
        copy = pltpu.make_async_remote_copy(
            src_ref=src,
            dst_ref=dst,
            send_sem=core_send.at[at],
            recv_sem=core_recv.at[at],
            device_id=core_dev,
            device_id_type=MESH,
        )
        copy.start()
        return copy

    load_x.wait()
    pl.semaphore_wait(barrier, 6 + ((blk == 0) & (dp > 0)).astype(jnp.int32))
    core_copies = [to_core(0, x_row.at[own_rows], x_row.at[own_rows])]

    length, start_at, end_at, answered = (ref[...].reshape(1, 1) for ref in scalars)
    key_at = lax.broadcasted_iota(jnp.int32, (1, ROW), 1)
    key_live = key_at < length
    token_at = blk * BLOCK + lax.broadcasted_iota(jnp.int32, (BLOCK, 1), 0)
    row_live = (token_at < length).astype(FULL)
    live_map[...] = jnp.where(key_live, 1.0 / ROW, 0.0) * row_live

    def project(rows, part):
        return dot_nn(x_row[rows, :], wp[:, WIDTH * part : WIDTH * part + WIDTH])

    load_wp[0].wait()
    for copy in small:
        copy.wait()
    own_queries = (project(own_rows, 0) + query_bias[...]).astype(LOW)
    q_own[...] = own_queries * jnp.asarray(HEAD_DIM ** (-0.5), LOW)
    load_wp[1].wait()
    load_wo = load(1, w_output, wo)
    load_we = load(2, w_expand, we)
    load_wr = load(3, w_reduce, wr)
    load_up = load(4, upstream, up)
    load_te = load(5, teacher, te)
    k_row[own_rows, :] = project(own_rows, 1).astype(LOW)
    load_wp[2].wait()
    v_row[own_rows, :] = (project(own_rows, 2) + value_bias[...]).astype(LOW)
    pltpu.make_async_remote_copy(
        src_ref=x_row.at[oth_rows],
        dst_ref=x_row.at[oth_rows],
        send_sem=core_send.at[0],
        recv_sem=core_recv.at[0],
        device_id=core_dev,
        device_id_type=MESH,
    ).wait_recv()
    k_row[oth_rows, :] = project(oth_rows, 1).astype(LOW)
    v_row[oth_rows, :] = (project(oth_rows, 2) + value_bias[...]).astype(LOW)

    lane = lax.broadcasted_iota(jnp.int32, (1, LANES), 1)
    head_lanes = ((lane < HEAD_DIM).astype(LOW), (lane >= HEAD_DIM).astype(LOW))

    def pair_cols(head):
        return slice(LANES * (head // 2), LANES * (head // 2) + LANES)

    def head_scores(head):
        cols = pair_cols(head)
        scores = dot_nt(q_own[:, cols] * head_lanes[head % 2], k_row[:, cols])
        return jnp.where(key_live, scores, -1e30)

    def head_soft(scores):
        peak = jnp.max(scores, axis=-1, keepdims=True)
        terms = jnp.exp(scores - peak)
        scale = 1.0 / jnp.sum(terms, axis=-1, keepdims=True)
        return (terms * scale).astype(LOW)

    gathered = {}

    def head_gather(head):
        cols = pair_cols(head)
        gathered[head] = dot_nn(soft[head], v_row[:, cols] * head_lanes[head % 2])
        if head % 2 == 1:
            att_own[:, cols] = (gathered[head - 1] + gathered[head]).astype(LOW)

    ahead = head_scores(0)
    for head in range(HEADS):
        scores = ahead
        if head + 1 < HEADS:
            ahead = head_scores(head + 1)
        if head > 0:
            head_gather(head - 1)
        soft[head] = head_soft(scores)
    head_gather(HEADS - 1)
    core_copies.append(to_core(1, att_own, att_oth))

    load_wo.wait()
    branch = dot_nn(att_own[...], wo[...]) + output_bias[...]
    resid = x_row[own_rows, :].astype(FULL) + branch
    centre = resid - row_mean(resid)
    scale_one = lax.rsqrt(row_mean(centre * centre) + norm_eps)
    normal = centre * scale_one
    norm_one[...] = normal
    mix_own[...] = (normal * first_gain[...] + first_shift[...]).astype(LOW)
    core_copies.append(to_core(2, mix_own, mix_oth))

    load_we.wait()

    @pl.loop(0, 6, unroll=6)
    def _(at):
        cols = pl.ds(aligned(at * 512, 512), 512)
        expanded = dot_nn(mix_own[...], we[:, cols]) + expand_bias[:, cols]
        gate = 0.5 + 0.5 * lax.erf(expanded * (2.0**-0.5))
        bell = jnp.exp(expanded * expanded * -0.5) * ((2.0 * jnp.pi) ** -0.5)
        act_own[:, cols] = (expanded * gate).astype(LOW)
        slope[:, cols] = (gate + expanded * bell).astype(LOW)

    core_copies.append(to_core(3, act_own, act_oth))
    load_wr.wait()
    reduced = dot_nn(act_own[...], wr[...]) + reduce_bias[...]
    mixed = norm_one[...] * first_gain[...] + first_shift[...]
    resid = mixed + reduced
    centre = resid - row_mean(resid)
    scale_two = lax.rsqrt(row_mean(centre * centre) + norm_eps)
    normal = centre * scale_two
    out_own[...] = (normal * second_gain[...] + second_shift[...]).astype(LOW)
    store_out = pltpu.make_async_copy(out_own, layer_output, out_sem.at[0])
    store_out.start()

    answered = answered > 0
    start_slot = jnp.where(answered, start_at, 0)
    end_slot = jnp.where(answered, end_at, 0)
    load_up.wait()
    cot = up[...].astype(FULL) * row_live
    cot = cot + (token_at == start_slot).astype(FULL) * start_vector[...]
    cot = cot + (token_at == end_slot).astype(FULL) * end_vector[...]

    def put_bias(first_row, vector):
        for at in range(vector.shape[1] // LANES):
            bias_sum[first_row + at : first_row + at + 1, :] = vector[
                :, at * LANES : (at + 1) * LANES
            ]

    put_bias(60, col_sum(cot * normal))
    put_bias(66, col_sum(cot))
    pulled = cot * second_gain[...]
    pulled = scale_two * (pulled - row_mean(pulled) - normal * row_mean(pulled * normal))
    resid_two[...] = pulled
    pulled_low = pulled.astype(LOW)
    gred_own[...] = pulled_low
    put_bias(54, col_sum(pulled_low.astype(FULL)))
    own_384 = pl.ds(aligned(blk * 384, 384), 384)
    oth_384 = pl.ds(aligned(oth * 384, 384), 384)
    core_copies.append(to_core(4, gred_own.at[:, oth_384], gred_oth))

    def send(src, dst, send_sem, recv_sem, dev):
        pltpu.make_async_remote_copy(
            src_ref=src,
            dst_ref=dst,
            send_sem=send_sem,
            recv_sem=recv_sem,
            device_id=dev,
            device_id_type=MESH,
        ).start()

    def wait_recv(dst, recv_sem):
        pltpu.make_async_remote_copy(
            src_ref=dst,
            dst_ref=dst,
            send_sem=recv_sem,
            recv_sem=recv_sem,
            device_id=core_dev,
            device_id_type=MESH,
        ).wait_recv()

    def wait_send(src, send_sem):
        pltpu.make_async_remote_copy(
            src_ref=src,
            dst_ref=src,
            send_sem=send_sem,
            recv_sem=send_sem,
            device_id=core_dev,
            device_id_type=MESH,
        ).wait_send()

    def owner(plane, x_at, y_at):
        return 4 * plane + 2 * y_at + x_at

    def add_unit(chip, unit, arrivals):
        value = grad[chip, unit].astype(FULL)
        for arrival in arrivals:
            value = value + arrival.astype(FULL)
        grad[chip, unit] = value.astype(LOW)

    def paired(plane, third):
        return third >= 3 - PAIRED[plane]

    def kept(plane):
        return (lax.rem(zz, 2) == 0) if plane < 2 else (lax.rem(zz, 2) == 1)

    def taking_part(plane, third, step):
        if paired(plane, third):
            pl.when(kept(plane))(step)
        else:
            step()

    def pair_copy(plane, third):
        return pltpu.make_async_remote_copy(
            src_ref=grad.at[pl.ds(4 * plane, 4), pl.ds(2 * third, 2)],
            dst_ref=pair_in.at[plane % 2, 2 - third],
            send_sem=pair_send.at[plane, third],
            recv_sem=pair_recv.at[plane, third],
            device_id=pair_dev,
            device_id_type=MESH,
        )

    def first_copies(plane, third, slots=range(4)):
        one, two = 2 * third, 2 * third + 1
        return [
            pltpu.make_async_remote_copy(
                src_ref=grad.at[chip, unit],
                dst_ref=first_in.at[plane, third, slot],
                send_sem=first_send.at[plane, third, slot],
                recv_sem=first_recv.at[plane, third, slot],
                device_id=dev,
                device_id_type=MESH,
            )
            for chip, unit, slot, dev in (
                (owner(plane, 1 - xx, 1 - yy), one, 0, x_dev),
                (owner(plane, 1 - xx, 1 - yy), two, 1, y_dev),
                (owner(plane, 1 - xx, yy), one, 2, x_dev),
                (owner(plane, xx, 1 - yy), two, 3, y_dev),
            )
            if slot in slots
        ]

    def second_copies(plane, third):
        one, two = 2 * third, 2 * third + 1
        return [
            pltpu.make_async_remote_copy(
                src_ref=grad.at[chip, unit],
                dst_ref=second_in.at[plane, third, slot],
                send_sem=second_send.at[plane, third, slot],
                recv_sem=second_recv.at[plane, third, slot],
                device_id=dev,
                device_id_type=MESH,
            )
            for chip, unit, slot, dev in (
                (owner(plane, xx, 1 - yy), one, 0, y_dev),
                (owner(plane, 1 - xx, yy), two, 1, x_dev),
            )
        ]

    def chained(plane, third):
        return CHAINED[plane] and not paired(plane, third)

    def last_slot(third, source, way):
        return 6 * third + 2 * source + way

    def passing_slot(plane, third, way):
        return 18 + 6 * sum(CHAINED[:plane]) + 2 * third + way

    def far_copy(plane, third, way):
        below = zz < plane
        if chained(plane, third):
            target = jnp.where(below, dp + 4, dp - 4)
            ends = jnp.where(below, zz + 1, zz - 1) == plane
            passing = passing_slot(plane, third, way)
            slot = jnp.where(ends, last_slot(third, jnp.where(below, 0, 1), way), passing)
        else:
            target = owner(plane, xx, yy)
            slot = last_slot(third, jnp.where(below, zz, zz - 1), way)
        return pltpu.make_async_remote_copy(
            src_ref=grad.at[owner(plane, xx, yy), 2 * third + way],
            dst_ref=far_in.at[slot],
            send_sem=far_send.at[plane, third, way],
            recv_sem=far_recv.at[slot],
            device_id=(target, blk),
            device_id_type=MESH,
        )

    def pair_step(plane, third):
        @pl.when(jnp.logical_not(kept(plane)))
        def _():
            pair_copy(plane, third).start()

    def pair_add(plane, third):
        @pl.when(kept(plane))
        def _():
            pair_copy(plane, third).wait_recv()

            @pl.loop(0, 4)
            def _(chip):
                for way in range(2):
                    add_unit(
                        4 * plane + chip,
                        2 * third + way,
                        [pair_in[plane % 2, 2 - third, chip, way]],
                    )

            for copy in first_copies(plane, third):
                copy.start()

    def first_step(plane, third):
        for copy in first_copies(plane, third):
            copy.start()

    def second_step(plane, third):
        def step():
            firsts = first_copies(plane, third, (0, 1))
            seconds = second_copies(plane, third)
            for way in range(2):
                chip = (owner(plane, xx, 1 - yy), owner(plane, 1 - xx, yy))[way]
                firsts[way].wait_recv()
                add_unit(chip, 2 * third + way, [first_in[plane, third, way]])
                seconds[way].start()

        taking_part(plane, third, step)

    def third_step(plane, third):
        def step():
            firsts = first_copies(plane, third, (2, 3))
            seconds = second_copies(plane, third)
            for way in range(2):
                firsts[way].wait_recv()
                seconds[way].wait_recv()
                add_unit(
                    owner(plane, xx, yy),
                    2 * third + way,
                    [first_in[plane, third, 2 + way], second_in[plane, third, way]],
                )
                leaves = (zz == 0) | (zz == 3) if chained(plane, third) else zz >= 0

                @pl.when((zz != plane) & leaves)
                def _():
                    far_copy(plane, third, way).start()

        taking_part(plane, third, step)

    def chain_step(plane, third):
        @pl.when((zz != plane) & (zz > 0) & (zz < 3))
        def _():
            for way in range(2):
                slot = passing_slot(plane, third, way)
                wait_recv(far_in.at[slot], far_recv.at[slot])
                add_unit(owner(plane, xx, yy), 2 * third + way, [far_in[slot]])
                far_copy(plane, third, way).start()

    def finish_step(_, third):
        for plane in range(4):
            if paired(plane, third):
                sources = [z for z in range(4) if z != plane and (z % 2 == 0) == (plane < 2)]
                sources = [z if z < plane else z - 1 for z in sources]
            elif CHAINED[plane]:
                sources = ([0] if plane > 0 else []) + ([1] if plane < 3 else [])
            else:
                sources = [0, 1, 2]

            @pl.when(zz == plane)
            def _():
                for way in range(2):
                    slots = [last_slot(third, source, way) for source in sources]
                    for slot in slots:
                        wait_recv(far_in.at[slot], far_recv.at[slot])
                    gave = paired(plane, third) and (plane % 2 == 0) != (plane < 2)
                    terms = [far_in[slot].astype(FULL) for slot in slots]
                    if not gave:
                        terms.append(grad[dp, 2 * third + way].astype(FULL))
                    total[2 * third + way] = sum(terms[1:], terms[0])

    steps = {
        "pair": pair_step,
        "add": pair_add,
        "first": first_step,
        "second": second_step,
        "third": third_step,
        "chain": chain_step,
        "finish": finish_step,
    }

    def serve(after):
        for what, plane, third in SCHEDULE.get(after, ()):
            steps[what](plane, third)

    def put_unit(at, rows, values):
        chip, unit = (at // 6, at % 6) if isinstance(at, int) else (lax.div(at, 6), lax.rem(at, 6))
        grad[chip, unit, rows, :] = values.astype(LOW)

    core_copies[3].wait_recv()
    core_copies[4].wait_recv()

    reduced_both = both(gred_own[:, own_384], gred_oth[...])

    def reduce_rows(first, count, before=0):
        cols = slice(96 * (first - 64) - before, 96 * (first - 64 + count))
        part = dot_tn(both(act_own[:, cols], act_oth[:, cols]), reduced_both)
        for unit in range(count):
            for tile in range(3):
                put_unit(
                    first + unit,
                    slice(96 * tile, 96 * tile + 96),
                    part[
                        before + 96 * unit : before + 96 * unit + 96,
                        LANES * tile : LANES * tile + LANES,
                    ],
                )

    for third in range(3):
        for chip in range(12, CHIPS):
            first = 6 * chip + 2 * third
            reduce_rows(first, 2, before=96 * (first - 64) % LANES)
        serve("reduce" + str(third))
    reduce_rows(64, 8)
    serve("reduce3")

    @pl.loop(0, 6)
    def _(at):
        half = jnp.where(at < 3, oth, blk)
        part_at = lax.rem(at, 3) * 512
        cols = pl.ds(aligned(half * 1536 + part_at, 512), 512)
        grad_active = dot_nt(gred_own[...], wr[cols, :])
        grad_expanded = (grad_active * slope[:, cols].astype(FULL)).astype(LOW)
        gexp_own[half, :, pl.ds(aligned(part_at, 512), 512)] = grad_expanded
        sums = col_sum(grad_expanded.astype(FULL))
        for tile in range(4):
            bias_sum[pl.ds(30 + half * 12 + lax.rem(at, 3) * 4 + tile, 1), :] = sums[
                :, LANES * tile : LANES * tile + LANES
            ]

    core_copies.append(to_core(5, gexp_own.at[oth], gexp_oth))
    serve("slopes")
    grad_mixed = resid_two[...]
    for half in range(2):
        grad_mixed = grad_mixed + dot_nt(
            gexp_own[half], we[:, 1536 * half : 1536 * half + 1536]
        )

    normal = norm_one[...]
    put_bias(18, col_sum(grad_mixed * normal))
    put_bias(24, col_sum(grad_mixed))
    pulled = grad_mixed * first_gain[...]
    pulled = scale_one * (pulled - row_mean(pulled) - normal * row_mean(pulled * normal))
    resid_one[...] = pulled
    pulled_low = pulled.astype(LOW)
    gbr_own[...] = pulled_low
    put_bias(12, col_sum(pulled_low.astype(FULL)))
    core_copies.append(to_core(6, gbr_own.at[:, oth_384], gbr_oth))

    serve("norm")

    core_copies[2].wait_recv()
    core_copies[5].wait_recv()

    @pl.loop(0, 6)
    def _(at):
        cols = pl.ds(aligned(at * 256, 256), 256)
        part = dot_tn(
            both(mix_own[...], mix_oth[...]), both(gexp_own[blk, :, cols], gexp_oth[:, cols])
        )
        rows = pl.ds(aligned(at * 48, 48), 48)
        for unit in range(32):
            piece = part[24 * unit : 24 * unit + 24, :]
            put_unit(32 + unit, rows, both(piece[:, :LANES], piece[:, LANES:]))

    serve("expand")
    gatt[...] = dot_nt(gbr_own[...], wo[...]).astype(LOW)
    core_copies[1].wait_recv()
    core_copies[6].wait_recv()
    part = dot_tn(both(att_own[...], att_oth[...]), both(gbr_own[:, own_384], gbr_oth[...]))
    for unit in range(8):
        for tile in range(3):
            put_unit(24 + unit, slice(96 * tile, 96 * tile + 96), part[
                96 * unit : 96 * unit + 96, LANES * tile : LANES * tile + LANES
            ])
    serve("output")

    qt[...] = q_own[...].T
    gat[...] = gatt[...].T
    load_te.wait()

    def head_pair(pair):
        cols = pl.ds(aligned(pair * LANES, LANES), LANES)
        ga_pair = gatt[:, cols]
        k_pair = k_row[:, cols]
        v_pair = v_row[:, cols]
        grad_query = None
        for side in range(2):
            rows = pl.ds(aligned(pair * LANES + side * HEAD_DIM, HEAD_DIM), HEAD_DIM)
            soft_low = soft[2 * pair + side]
            grad_soft = dot_nt(ga_pair * head_lanes[side], v_pair)
            soft_full = soft_low.astype(FULL)
            taught = te[2 * pair + side].astype(FULL) * live_map[...]
            shift = jnp.sum(taught - grad_soft * soft_full, axis=-1, keepdims=True)
            grad_scores = (soft_full * (grad_soft + shift) - taught).astype(LOW)
            part = dot_nn(grad_scores, k_pair * head_lanes[side])
            grad_query = part if grad_query is None else grad_query + part
            slot = pl.ds(aligned(pair * ROW, ROW), ROW)
            at = side * HEAD_DIM
            slope[at : at + HEAD_DIM, slot] = dot_nn(qt[rows, :], grad_scores).astype(LOW)
            at = at + LANES
            slope[at : at + HEAD_DIM, slot] = dot_nn(gat[rows, :], soft_low).astype(LOW)
        gpj_own[:, cols] = (grad_query * HEAD_DIM ** (-0.5)).astype(LOW)

    for part in range(3):

        @pl.loop(2 * part, 2 * part + 2)
        def _(pair):
            head_pair(pair)

        serve("heads" + str(part))

    def turned(pair, block, first):
        lanes = pl.ds(aligned(pair * ROW + block * BLOCK, BLOCK), BLOCK)
        return slope[first : first + LANES, lanes].T

    for pair in range(HEADS // 2):
        for first in (0, LANES):
            at = pair * LANES + first * (WIDTH // LANES)
            dkv_out[:, at : at + LANES] = turned(pair, oth, first)
    core_copies.append(to_core(7, dkv_out, dkv_in))
    core_copies[7].wait_recv()
    for pair in range(HEADS // 2):
        for first in (0, LANES):
            at = pair * LANES + first * (WIDTH // LANES)
            gpj_own[:, WIDTH + at : WIDTH + at + LANES] = (
                turned(pair, blk, first).astype(FULL) + dkv_in[:, at : at + LANES].astype(FULL)
            ).astype(LOW)
    serve("keys")
    own_1152 = pl.ds(aligned(blk * 1152, 1152), 1152)
    oth_1152 = pl.ds(aligned(oth * 1152, 1152), 1152)
    core_copies.append(to_core(8, gpj_own.at[:, oth_1152], gpj_oth))
    put_bias(0, col_sum(gpj_own[:, :WIDTH].astype(FULL)))
    put_bias(6, col_sum(gpj_own[:, 2 * WIDTH :].astype(FULL)))

    def input_gradient_part():
        gin_own[...] = (resid_one[...] + dot_nt(gpj_own[...], wp[...])).astype(LOW)
        pltpu.make_async_copy(gin_own, input_gradient, out_sem.at[1]).start()

    core_copies[8].wait_recv()

    @pl.loop(0, 3)
    def _(at):
        cols = pl.ds(aligned(at * 384, 384), 384)
        mine = pl.ds(aligned(blk * 1152 + at * 384, 384), 384)
        part = dot_tn(
            both(x_row[own_rows, :], x_row[oth_rows, :]), both(gpj_own[:, mine], gpj_oth[:, cols])
        )
        for unit in range(24):
            for tile in range(3):
                rows = pl.ds(aligned(at * 96 + 32 * tile, 32), 32)
                put_unit(unit, rows, part[
                    32 * unit : 32 * unit + 32, LANES * tile : LANES * tile + LANES
                ])

    serve("project")
    input_gradient_part()
    serve("input")

    def bias_leaves(at, here, dev):
        @pl.when(here)
        def _():
            send(bias_sum, bias_in.at[at], bias_send.at[0], bias_recv.at[at], dev)

    def bias_comes(at, there):
        @pl.when(there)
        def _():
            wait_recv(bias_in.at[at], bias_recv.at[at])
            bias_sum[...] += bias_in[at]

    corner = (xx == 1) & (yy == 1)
    last = dp == CHIPS - 1
    bias_leaves(0, xx == 0, x_dev)
    serve("bias0")
    bias_comes(0, xx == 1)
    bias_leaves(1, (xx == 1) & (yy == 0), y_dev)
    serve("bias1")
    bias_comes(1, corner)

    @pl.when(corner & (zz < 3))
    def _():
        send(
            bias_sum,
            bias_in.at[2 + zz],
            bias_send.at[0],
            bias_recv.at[2 + zz],
            (CHIPS - 1, blk),
        )

    serve("bias2")

    @pl.when(last)
    def _():
        for at in range(2, 5):
            wait_recv(bias_in.at[at], bias_recv.at[at])
            bias_sum[...] += bias_in[at]

    @pl.when(last & (blk == 0))
    def _():
        send(bias_sum, bias_in.at[5], bias_send.at[0], bias_recv.at[5], core_dev)

    serve("bias3")

    @pl.when(last & (blk == 1))
    def _():
        wait_recv(bias_in.at[5], bias_recv.at[5])
        flat[1728:1800, :] = bias_sum[...] + bias_in[5]

    def lay_out(source, first, column_half, unit):
        kind_at = 3 * device + unit
        kinds = (
            (kind_at < 24, 32, 9),
            (((kind_at >= 24) & (kind_at < 32)) | (kind_at >= 64), 96, 3),
            ((kind_at >= 32) & (kind_at < 64), 24, 12),
        )
        for fits, rows, tiles in kinds:

            @pl.when(fits)
            def _():
                for tile in range(tiles):
                    for group in range(rows // 8):
                        at = rows * tile + 8 * group
                        to = 576 * unit + 16 * group * tiles + tile + column_half * tiles
                        flat[pl.ds(to, 8, stride=2 * tiles), :] = source[
                            first + unit, at : at + 8, :
                        ]

    def to_core_when(at, here, src, dst):
        @pl.when(here)
        def _():
            send(src, dst, core_send.at[at], core_recv.at[at], core_dev)

    serve("end0")
    to_core_when(9, blk == 1, total.at[pl.ds(0, 3)], total_oth)
    to_core_when(10, blk == 0, total.at[pl.ds(3, 1)], total_oth.at[pl.ds(0, 1)])

    @pl.when(blk == 1)
    def _():
        lay_out(total, 3, 1, 0)
        wait_recv(total_oth.at[pl.ds(0, 1)], core_recv.at[10])
        lay_out(total_oth, 0, 0, 0)
        send(flat.at[0:72], flat.at[1728:1800], fix_send.at[0], fix_recv.at[0], core_dev)

    @pl.when(blk == 0)
    def _():
        for unit in range(3):
            lay_out(total, 0, 0, unit)
        wait_recv(total_oth, core_recv.at[9])
        for unit in range(3):
            lay_out(total_oth, 0, 1, unit)

        @pl.when(dp > 0)
        def _():
            send(flat.at[0:72], flat.at[1728:1800], fix_send.at[0], fix_recv.at[0], (dp - 1, 1))

    serve("end1")
    to_core_when(11, blk == 0, total.at[pl.ds(4, 2)], total_oth.at[pl.ds(1, 2)])

    @pl.when(blk == 1)
    def _():
        for unit in range(1, 3):
            lay_out(total, 3, 1, unit)
        wait_recv(total_oth.at[pl.ds(1, 2)], core_recv.at[11])
        for unit in range(1, 3):
            lay_out(total_oth, 0, 0, unit)

    @pl.when(device < 2 * CHIPS - 1)
    def _():
        wait_recv(flat.at[1728:1800], fix_recv.at[0])

    shift = 32 * lax.rem(device, 4)
    skip = (9 * device) // 4
    stays = lane < LANES - shift

    @pl.loop(0, 31)
    def _(at):
        rows = at * 56
        first = pltpu.roll(flat[pl.ds(rows + skip, 56), :], LANES - shift, 1)
        second = pltpu.roll(flat[pl.ds(rows + skip + 1, 56), :], LANES - shift, 1)
        placed[pl.ds(aligned(rows, 8), 56), :] = jnp.where(stays, first, second)

    store_grads = pltpu.make_async_copy(placed, grads, out_sem.at[2])
    store_grads.start()

    for copy in core_copies:
        copy.wait_send()

    @pl.when(blk == 1)
    def _():
        wait_send(total.at[pl.ds(0, 3)], core_send.at[9])

    @pl.when(blk == 0)
    def _():
        wait_send(total.at[pl.ds(3, 1)], core_send.at[10])
        wait_send(total.at[pl.ds(4, 2)], core_send.at[11])

    for plane in range(4):
        for third in range(3):
            if paired(plane, third):

                @pl.when(jnp.logical_not(kept(plane)))
                def _():
                    pair_copy(plane, third).wait_send()

            def sent():
                for copy in first_copies(plane, third) + second_copies(plane, third):
                    copy.wait_send()

                @pl.when(zz != plane)
                def _():
                    for way in range(2):
                        far_copy(plane, third, way).wait_send()

            taking_part(plane, third, sent)

    @pl.when(jnp.logical_not(last & (blk == 1)))
    def _():
        wait_send(bias_sum, bias_send.at[0])

    @pl.when(device > 0)
    def _():
        wait_send(flat.at[0:72], fix_send.at[0])

    store_out.wait()
    pltpu.make_async_copy(gin_own, input_gradient, out_sem.at[1]).wait()
    store_grads.wait()


def hand_over(*refs):
    sources, targets, held, sems = refs[:3], refs[3:6], refs[6:9], refs[9]
    reads = [pltpu.make_async_copy(*pair, sems.at[at]) for at, pair in enumerate(zip(sources, held))]
    writes = [
        pltpu.make_async_copy(*pair, sems.at[3 + at]) for at, pair in enumerate(zip(held, targets))
    ]
    for read in reads:
        read.start()
    for read, write in zip(reads, writes):
        read.wait()
        write.start()
    for write in writes:
        write.wait()


def fused_layer(
    hidden_in,
    project_weight,
    output_weight,
    expand_weight,
    reduce_weight,
    query_bias,
    value_bias,
    output_bias,
    first_gain,
    first_shift,
    expand_bias,
    reduce_bias,
    second_gain,
    second_shift,
    upstream,
    teacher_maps,
    start_vector,
    end_vector,
    valid_length,
    start_index,
    end_index,
    answerable,
):
    vectors = (
        query_bias,
        value_bias,
        output_bias,
        first_gain,
        first_shift,
        expand_bias,
        reduce_bias,
        second_gain,
        second_shift,
        start_vector,
        end_vector,
    )
    scalars = (valid_length, start_index, end_index, answerable)
    anywhere = pl.BlockSpec(memory_space=pl.ANY)
    in_vmem = pl.BlockSpec(memory_space=pltpu.VMEM)

    def low(*shape):
        return pltpu.VMEM(shape, LOW)

    def full(*shape):
        return pltpu.VMEM(shape, FULL)

    dma = pltpu.SemaphoreType.DMA
    scratch = [
        low(WIDTH, 3 * WIDTH),
        low(WIDTH, WIDTH),
        low(WIDTH, FF),
        low(FF, WIDTH),
        low(HEADS, BLOCK, ROW),
        low(BLOCK, WIDTH),
        low(ROW, WIDTH),
        tuple(full(1, vector.shape[0]) for vector in vectors),
        low(BLOCK, WIDTH),
        low(ROW, WIDTH),
        low(ROW, WIDTH),
        low(HEADS, BLOCK, ROW),
        low(BLOCK, WIDTH),
        low(BLOCK, WIDTH),
        low(BLOCK, WIDTH),
        low(BLOCK, WIDTH),
        low(BLOCK, FF),
        low(BLOCK, FF),
        low(BLOCK, FF),
        full(BLOCK, WIDTH),
        full(BLOCK, WIDTH),
        full(BLOCK, WIDTH),
        low(BLOCK, WIDTH),
        low(BLOCK, WIDTH // 2),
        low(2, BLOCK, FF // 2),
        low(BLOCK, FF // 2),
        low(BLOCK, WIDTH),
        low(BLOCK, WIDTH // 2),
        low(BLOCK, WIDTH),
        low(WIDTH, BLOCK),
        low(WIDTH, BLOCK),
        low(BLOCK, 2 * WIDTH),
        low(BLOCK, 2 * WIDTH),
        low(BLOCK, 3 * WIDTH),
        low(BLOCK, 3 * WIDTH // 2),
        full(BLOCK, ROW),
        low(BLOCK, WIDTH),
        low(BLOCK, WIDTH),
        low(CHIPS, 6, UNIT, LANES),
        low(2, max(PAIRED), 4, 2, UNIT, LANES),
        low(4, 3, 4, UNIT, LANES),
        low(4, 3, 2, UNIT, LANES),
        low(18 + 6 * sum(CHAINED), UNIT, LANES),
        full(6, UNIT, LANES),
        full(3, UNIT, LANES),
        full(1816, LANES),
        full(1736, LANES),
        full(72, LANES),
        full(6, 72, LANES),
        dma((9,)),
        dma((len(vectors),)),
        dma((12,)),
        dma((12,)),
        dma((4, 3)),
        dma((4, 3)),
        dma((4, 3, 4)),
        dma((4, 3, 4)),
        dma((4, 3, 2)),
        dma((4, 3, 2)),
        dma((4, 3, 2)),
        dma((18 + 6 * sum(CHAINED),)),
        dma((1,)),
        dma((6,)),
        dma((1,)),
        dma((1,)),
        dma((3,)),
    ]
    results = (
        jax.ShapeDtypeStruct((BLOCK, WIDTH), LOW),
        jax.ShapeDtypeStruct((BLOCK, WIDTH), LOW),
        jax.ShapeDtypeStruct((1736, LANES), FULL),
    )
    made = pl.pallas_call(
        layer_kernel,
        out_shape=results,
        in_specs=[anywhere] * 7 + [(anywhere,) * len(vectors), (in_vmem,) * len(scalars)],
        out_specs=(anywhere,) * 3,
        scratch_shapes=scratch,
        compiler_params=pltpu.CompilerParams(
            collective_id=0, has_side_effects=True, vmem_limit_bytes=63 * 2**20
        ),
        name="encoder_layer",
    )(
        hidden_in.reshape(BLOCK, WIDTH),
        upstream.reshape(BLOCK, WIDTH),
        teacher_maps.reshape(HEADS, BLOCK, ROW),
        project_weight,
        output_weight,
        expand_weight,
        reduce_weight,
        vectors,
        scalars,
    )
    layer_output, input_gradient, grads = pl.pallas_call(
        hand_over,
        out_shape=results,
        in_specs=[anywhere] * 3,
        out_specs=(anywhere,) * 3,
        scratch_shapes=[pltpu.VMEM(result.shape, result.dtype) for result in results] + [dma((6,))],
        name="hand_over",
    )(*made)
    return (
        layer_output.reshape(1, BLOCK, WIDTH),
        input_gradient.reshape(1, BLOCK, WIDTH),
        grads.reshape(-1)[: 3 * 2 * UNIT * LANES + UNIT],
    )


def layer_norm(field_in, gain_vec, shift_vec):
    centre = field_in - jnp.mean(field_in, axis=-1, keepdims=True)
    spread = jnp.mean(centre * centre, axis=-1, keepdims=True)
    return centre * lax.rsqrt(spread + norm_eps) * gain_vec + shift_vec


def gelu_exact(field_in):
    return jax.nn.gelu(field_in, approximate=False)


def outer_sum(left, right):
    return jnp.einsum("nd,ne->de", left, right, preferred_element_type=jnp.float32)


def column_sum(values_low):
    return jnp.sum(values_low.astype(jnp.float32), axis=0)


def plain_layer(
    hidden_in,
    project_weight,
    output_weight,
    expand_weight,
    reduce_weight,
    query_bias,
    value_bias,
    output_bias,
    first_gain,
    first_shift,
    expand_bias,
    reduce_bias,
    second_gain,
    second_shift,
    upstream,
    teacher_maps,
    start_vector,
    end_vector,
    valid_length,
    start_index,
    end_index,
    answerable,
):
    row_count, block_len, width = hidden_in.shape
    blocks = lax.axis_size("blk")
    length = block_len * blocks
    offset = lax.axis_index("blk") * block_len
    token_count = row_count * block_len
    positions = offset + jnp.arange(block_len, dtype=jnp.int32)
    key_live = jnp.arange(length, dtype=jnp.int32)[None, :] < valid_length[:, None]
    row_live = positions[None, :] < valid_length[:, None]
    score_scale = HEAD_DIM ** (-0.5)
    tokens = hidden_in.reshape(token_count, width)
    joined_bias = jnp.concatenate([query_bias, jnp.zeros_like(query_bias), value_bias])
    project = (
        jnp.dot(tokens, project_weight, preferred_element_type=jnp.float32) + joined_bias
    ).astype(jnp.bfloat16)
    queries = project[:, :width].reshape(row_count, block_len, HEADS, HEAD_DIM)
    keys_own = project[:, width : 2 * width].reshape(row_count, block_len, width)
    values_own = project[:, 2 * width :].reshape(row_count, block_len, width)
    keys_all, values_all = (
        lax.all_gather(keys_own, "blk", axis=1, tiled=True),
        lax.all_gather(values_own, "blk", axis=1, tiled=True),
    )

    def scores_of(keys_full):
        raw = (
            jnp.einsum(
                "rqhe,rkhe->rhqk",
                queries,
                keys_full.reshape(row_count, length, HEADS, HEAD_DIM),
                preferred_element_type=jnp.float32,
            )
            * score_scale
        )
        return jnp.where(key_live[:, None, None, :], raw, -1e30)

    scores = scores_of(keys_all)
    row_peak = jnp.max(scores, axis=-1, keepdims=True)
    expo_terms = jnp.exp(scores - row_peak)
    row_total = jnp.sum(expo_terms, axis=-1, keepdims=True)
    soft_low = (expo_terms / row_total).astype(jnp.bfloat16)
    log_total = row_peak + jnp.log(row_total)
    attended = (
        jnp.einsum(
            "rhqk,rkhe->rqhe",
            soft_low,
            values_all.reshape(row_count, length, HEADS, HEAD_DIM),
            preferred_element_type=jnp.float32,
        )
        .reshape(token_count, width)
        .astype(jnp.bfloat16)
    )
    branch = jnp.dot(attended, output_weight, preferred_element_type=jnp.float32) + output_bias
    resid_one = tokens.astype(jnp.float32) + branch
    mixed, first_pull = jax.vjp(layer_norm, resid_one, first_gain, first_shift)
    mixed_low = mixed.astype(jnp.bfloat16)
    expanded = jnp.dot(mixed_low, expand_weight, preferred_element_type=jnp.float32) + expand_bias
    active, gelu_pull = jax.vjp(gelu_exact, expanded)
    active_low = active.astype(jnp.bfloat16)
    reduced = jnp.dot(active_low, reduce_weight, preferred_element_type=jnp.float32) + reduce_bias
    result, second_pull = jax.vjp(layer_norm, mixed + reduced, second_gain, second_shift)
    layer_output = result.astype(jnp.bfloat16).reshape(row_count, block_len, width)
    start_slot = jnp.where(answerable > 0, start_index, 0)
    end_slot = jnp.where(answerable > 0, end_index, 0)
    cotangent = (
        upstream.astype(jnp.float32) * row_live[..., None].astype(jnp.float32)
        + (positions[None, :] == start_slot[:, None])[..., None].astype(jnp.float32) * start_vector
        + (positions[None, :] == end_slot[:, None])[..., None].astype(jnp.float32) * end_vector
    )
    grad_resid_two, grad_second_gain, grad_second_shift = second_pull(
        cotangent.reshape(token_count, width)
    )
    grad_reduced = grad_resid_two.astype(jnp.bfloat16)
    grad_active = jnp.einsum(
        "nd,fd->nf", grad_reduced, reduce_weight, preferred_element_type=jnp.float32
    )
    grad_expanded = gelu_pull(grad_active)[0].astype(jnp.bfloat16)
    grad_mixed = grad_resid_two + jnp.einsum(
        "nf,df->nd", grad_expanded, expand_weight, preferred_element_type=jnp.float32
    )
    grad_resid_one, grad_first_gain, grad_first_shift = first_pull(grad_mixed)
    grad_branch = grad_resid_one.astype(jnp.bfloat16)
    grad_attended = jnp.einsum(
        "ne,de->nd", grad_branch, output_weight, preferred_element_type=jnp.float32
    )
    grad_attended = grad_attended.astype(jnp.bfloat16).reshape(
        row_count, block_len, HEADS, HEAD_DIM
    )
    keys_back, values_back = (
        lax.all_gather(keys_own, "blk", axis=1, tiled=True),
        lax.all_gather(values_own, "blk", axis=1, tiled=True),
    )
    keys_heads = keys_back.reshape(row_count, length, HEADS, HEAD_DIM)
    values_heads = values_back.reshape(row_count, length, HEADS, HEAD_DIM)
    soft = jnp.exp(scores_of(keys_back) - log_total)
    both_live = row_live[:, None, :, None] & key_live[:, None, None, :]
    teacher_live = jnp.where(both_live, teacher_maps.astype(jnp.float32), 0.0)
    teacher_total = jnp.sum(teacher_live, axis=-1, keepdims=True)
    grad_soft = jnp.einsum(
        "rqhe,rkhe->rhqk", grad_attended, values_heads, preferred_element_type=jnp.float32
    )
    row_delta = jnp.sum(grad_soft * soft, axis=-1, keepdims=True)
    grad_scores = (
        soft * (grad_soft - row_delta) + (teacher_total * soft - teacher_live) / length
    ).astype(jnp.bfloat16)
    grad_query = (
        jnp.einsum("rhqk,rkhe->rqhe", grad_scores, keys_heads, preferred_element_type=jnp.float32)
        * score_scale
    )
    grad_keys = (
        jnp.einsum(
            "rhqk,rqhe->rkhe", grad_scores, queries, preferred_element_type=jnp.float32
        ).reshape(row_count, length, width)
        * score_scale
    )
    grad_values = jnp.einsum(
        "rhqk,rqhe->rkhe", soft_low, grad_attended, preferred_element_type=jnp.float32
    ).reshape(row_count, length, width)
    keys_grad_own, values_grad_own = (
        lax.psum_scatter(
            grad_keys.astype(jnp.bfloat16), "blk", scatter_dimension=1, tiled=True
        ).astype(jnp.float32),
        lax.psum_scatter(
            grad_values.astype(jnp.bfloat16), "blk", scatter_dimension=1, tiled=True
        ).astype(jnp.float32),
    )
    grad_project = jnp.concatenate(
        [
            grad_query.reshape(token_count, width),
            keys_grad_own.reshape(token_count, width),
            values_grad_own.reshape(token_count, width),
        ],
        axis=1,
    ).astype(jnp.bfloat16)
    grad_input = grad_resid_one + jnp.einsum(
        "ne,de->nd", grad_project, project_weight, preferred_element_type=jnp.float32
    )
    input_gradient = grad_input.astype(jnp.bfloat16).reshape(row_count, block_len, width)
    (
        tokens_both,
        project_both,
        attended_both,
        branch_both,
        mixed_both,
        expanded_both,
        active_both,
        reduced_both,
    ) = (
        lax.all_gather(tokens, "blk", axis=0, tiled=True),
        lax.all_gather(grad_project, "blk", axis=0, tiled=True),
        lax.all_gather(attended, "blk", axis=0, tiled=True),
        lax.all_gather(grad_branch, "blk", axis=0, tiled=True),
        lax.all_gather(mixed_low, "blk", axis=0, tiled=True),
        lax.all_gather(grad_expanded, "blk", axis=0, tiled=True),
        lax.all_gather(active_low, "blk", axis=0, tiled=True),
        lax.all_gather(grad_reduced, "blk", axis=0, tiled=True),
    )
    project_sums = column_sum(project_both)
    norm_grads = lax.psum(
        (grad_first_gain, grad_first_shift, grad_second_gain, grad_second_shift), "blk"
    )
    flat_grads = jnp.concatenate(
        [
            outer_sum(tokens_both, project_both).reshape(-1),
            outer_sum(attended_both, branch_both).reshape(-1),
            outer_sum(mixed_both, expanded_both).reshape(-1),
            outer_sum(active_both, reduced_both).reshape(-1),
            project_sums[:width],
            project_sums[2 * width :],
            column_sum(branch_both),
            norm_grads[0],
            norm_grads[1],
            column_sum(expanded_both),
            column_sum(reduced_both),
            norm_grads[2],
            norm_grads[3],
        ]
    )
    data_count = lax.axis_size("dp")
    piece_len = flat_grads.shape[0] // (data_count * blocks)
    mine = lax.dynamic_index_in_dim(
        flat_grads.reshape(data_count, blocks, piece_len), lax.axis_index("blk"), 1, keepdims=False
    )
    weight_gradients = lax.psum_scatter(mine, "dp", scatter_dimension=0, tiled=True).reshape(
        piece_len
    )
    return (layer_output, input_gradient, weight_gradients)


def solution(mesh):
    placed = (
        P("dp", "blk", None),
        P(),
        P(),
        P(),
        P(),
        P(),
        P(),
        P(),
        P(),
        P(),
        P(),
        P(),
        P(),
        P(),
        P("dp", "blk", None),
        P("dp", None, "blk", None),
        P(),
        P(),
        P("dp"),
        P("dp"),
        P("dp"),
        P("dp"),
    )
    fits = (mesh.shape["dp"], mesh.shape["blk"]) == (CHIPS, 2)
    layer = fused_layer if fits else plain_layer
    return jax.shard_map(
        layer,
        mesh=mesh,
        in_specs=placed,
        out_specs=(P("dp", "blk", None), P("dp", "blk", None), P(("dp", "blk"))),
        check_vma=False,
    )
```

```python
import jax
import jax.numpy as jnp
from jax import lax
from jax.experimental import pallas as pl
from jax.experimental.pallas import tpu as pltpu
from jax.sharding import PartitionSpec as P

HEADS = 12
HEAD_DIM = 64
WIDTH = 768
FF = 3072
BLOCK = 256
ROW = 512
UNIT = 288
CHIPS = 16
LANES = 128

MESH = pl.DeviceIdType.MESH
LOW = jnp.bfloat16
FULL = jnp.float32

norm_eps = 1e-12


def dot_nn(left, right):
    return jnp.dot(left, right, preferred_element_type=FULL)


def dot_nt(left, right):
    return lax.dot_general(left, right, (((1,), (1,)), ((), ())), preferred_element_type=FULL)


def dot_tn(left, right):
    return lax.dot_general(left, right, (((0,), (0,)), ((), ())), preferred_element_type=FULL)


def both(own, other):
    return jnp.concatenate([own, other], axis=0)


def col_sum(field):
    return jnp.sum(field, axis=0, keepdims=True)


def row_mean(field):
    return jnp.mean(field, axis=-1, keepdims=True)


SCHEDULE = {
    "reduce0": (
        ("first", 3, 1),
        ("first", 3, 0),
    ),
    "reduce1": (
        ("first", 3, 2),
    ),
    "reduce2": (
        ("first", 3, 3),
        ("pair", 3, 4),
    ),
    "norm": (
        ("second", 3, 0),
        ("second", 3, 1),
    ),
    "expand": (
        ("first", 2, 3),
        ("first", 2, 2),
        ("pair", 3, 5),
    ),
    "output": (
        ("pair", 1, 4),
        ("first", 1, 1),
        ("first", 1, 0),
        ("first", 2, 1),
        ("first", 2, 0),
    ),
    "heads0": (
        ("third", 3, 0),
    ),
    "heads1": (
        ("second", 3, 3),
        ("first", 1, 3),
        ("pair", 1, 5),
        ("second", 2, 3),
        ("pair", 2, 5),
    ),
    "keys": (
        ("second", 2, 2),
        ("add", 3, 4),
        ("add", 1, 4),
    ),
    "project": (
        ("pair", 0, 5),
        ("first", 0, 0),
        ("second", 1, 1),
        ("first", 0, 3),
        ("second", 1, 3),
        ("second", 1, 0),
        ("pair", 2, 4),
        ("second", 1, 4),
        ("first", 0, 4),
        ("second", 2, 0),
        ("first", 0, 1),
        ("third", 2, 3),
        ("third", 2, 2),
        ("bias", 0, 0),
    ),
    "input": (
        ("third", 1, 1),
        ("third", 3, 1),
        ("second", 0, 3),
        ("first", 0, 2),
        ("second", 0, 4),
        ("third", 1, 0),
        ("second", 0, 0),
    ),
    "end": (
        ("third", 1, 3),
        ("bias", 1, 0),
        ("third", 2, 0),
        ("second", 3, 4),
        ("third", 3, 3),
        ("second", 0, 1),
        ("add", 2, 4),
        ("second", 2, 1),
        ("third", 0, 3),
        ("second", 0, 2),
        ("third", 1, 4),
        ("third", 0, 4),
        ("add", 3, 5),
        ("third", 3, 4),
        ("second", 3, 2),
        ("first", 1, 2),
        ("add", 1, 5),
        ("third", 0, 0),
        ("third", 0, 1),
        ("second", 2, 4),
        ("add", 2, 5),
        ("chain", 0, 3),
        ("add", 0, 5),
        ("bias", 2, 0),
        ("chain", 0, 4),
        ("third", 0, 2),
        ("third", 2, 1),
        ("third", 2, 4),
        ("second", 1, 2),
        ("second", 3, 5),
        ("second", 2, 5),
        ("chain", 0, 0),
        ("chain", 0, 1),
        ("third", 3, 2),
        ("second", 1, 5),
        ("chain", 0, 2),
        ("third", 1, 2),
        ("third", 3, 5),
        ("second", 0, 5),
        ("third", 1, 5),
        ("third", 0, 5),
        ("finish", 0, 0),
        ("place", 0, 0),
        ("finish", 0, 4),
        ("finish", 0, 1),
        ("third", 2, 5),
        ("finish", 0, 3),
        ("place", 0, 3),
        ("place", 0, 4),
        ("place", 0, 1),
        ("finish", 0, 2),
        ("place", 0, 2),
        ("finish", 0, 5),
        ("place", 0, 5),
    ),
}
PAIRED = (1, 2, 2, 2)
CHAINED = (True, False, False, False)


def aligned(start, step):
    return pl.multiple_of(start, step)


def layer_kernel(
    hidden,
    upstream,
    teacher,
    w_project,
    w_output,
    w_expand,
    w_reduce,
    vectors,
    scalars,
    layer_output,
    input_gradient,
    grads,
    wp,
    wo,
    we,
    wr,
    te,
    up,
    x_row,
    vector_at,
    q_own,
    k_row,
    v_row,
    soft,
    att_own,
    att_oth,
    mix_own,
    mix_oth,
    act_own,
    act_oth,
    slope,
    norm_one,
    resid_two,
    resid_one,
    gred_own,
    gred_oth,
    gexp_own,
    gexp_oth,
    gbr_own,
    gbr_oth,
    gatt,
    qt,
    gat,
    dkv_out,
    dkv_in,
    gpj_own,
    gpj_oth,
    live_map,
    out_own,
    gin_own,
    grad,
    pair_in,
    first_in,
    second_in,
    far_in,
    total,
    flat,
    placed,
    bias_sum,
    bias_in,
    load_sem,
    vector_sem,
    core_send,
    core_recv,
    pair_send,
    pair_recv,
    first_send,
    first_recv,
    second_send,
    second_recv,
    far_send,
    far_recv,
    beside_send,
    bias_send,
    bias_recv,
    fix_send,
    fix_recv,
    out_sem,
):
    dp = lax.axis_index("dp")
    blk = lax.axis_index("blk")
    oth = 1 - blk
    xx = dp % 2
    yy = (dp // 2) % 2
    zz = dp // 4
    column = dp % 4
    core_dev = (dp, oth)
    x_dev = (dp + 1 - 2 * xx, blk)
    y_dev = (dp + 2 - 4 * yy, blk)
    pair_dev = (jnp.where(zz % 2 == 0, dp + 4, dp - 4), blk)
    device = dp * 2 + blk

    def load(at, src, dst):
        copy = pltpu.make_async_copy(src, dst, load_sem.at[at])
        copy.start()
        return copy

    own_rows = pl.ds(aligned(blk * BLOCK, BLOCK), BLOCK)
    oth_rows = pl.ds(aligned(oth * BLOCK, BLOCK), BLOCK)
    load_x = load(0, hidden, x_row.at[own_rows])
    load_wp = [
        load(6 + part, w_project.at[:, part_cols], wp.at[:, part_cols])
        for part, part_cols in enumerate(pl.ds(WIDTH * part, WIDTH) for part in range(3))
    ]
    small = []
    for at, (src, dst) in enumerate(zip(vectors, vector_at)):
        small.append(pltpu.make_async_copy(src, dst.at[0], vector_sem.at[at]))
    for copy in small:
        copy.start()
    (
        query_bias,
        value_bias,
        output_bias,
        first_gain,
        first_shift,
        expand_bias,
        reduce_bias,
        second_gain,
        second_shift,
        start_vector,
        end_vector,
    ) = vector_at

    barrier = pltpu.get_barrier_semaphore()

    def greet(dev):
        pl.semaphore_signal(barrier, inc=1, device_id=dev, device_id_type=MESH)

    greet(core_dev)
    greet(x_dev)
    greet(y_dev)
    for step in range(1, 4):
        greet((lax.rem(dp + 4 * step, CHIPS), blk))
        greet((lax.rem(dp + 4 * step, CHIPS), oth))

    @pl.when((blk == 1) & (dp < CHIPS - 1))
    def _():
        greet((dp + 1, 0))

    def to_core(at, src, dst):
        copy = pltpu.make_async_remote_copy(
            src_ref=src,
            dst_ref=dst,
            send_sem=core_send.at[at],
            recv_sem=core_recv.at[at],
            device_id=core_dev,
            device_id_type=MESH,
        )
        copy.start()
        return copy

    pl.semaphore_wait(barrier, 9 + ((blk == 0) & (dp > 0)).astype(jnp.int32))
    core_copies = [to_core(0, hidden, x_row.at[own_rows])]

    length, start_at, end_at, answered = (ref[...].reshape(1, 1) for ref in scalars)
    key_at = lax.broadcasted_iota(jnp.int32, (1, ROW), 1)
    key_live = key_at < length
    token_at = blk * BLOCK + lax.broadcasted_iota(jnp.int32, (BLOCK, 1), 0)
    row_live = (token_at < length).astype(FULL)
    live_map[...] = jnp.where(key_live, 1.0 / ROW, 0.0) * row_live

    def project(rows, part):
        return dot_nn(x_row[rows, :], wp[:, WIDTH * part : WIDTH * part + WIDTH])

    load_x.wait()
    load_wp[0].wait()
    for copy in small:
        copy.wait()
    own_queries = (project(own_rows, 0) + query_bias[...]).astype(LOW)
    q_own[...] = own_queries * jnp.asarray(HEAD_DIM ** (-0.5), LOW)
    load_wp[1].wait()
    load_wo = load(1, w_output, wo)
    load_we = load(2, w_expand, we)
    load_wr = load(3, w_reduce, wr)
    load_up = load(4, upstream, up)
    load_te = load(5, teacher, te)
    k_row[own_rows, :] = project(own_rows, 1).astype(LOW)
    load_wp[2].wait()
    v_row[own_rows, :] = (project(own_rows, 2) + value_bias[...]).astype(LOW)
    pltpu.make_async_remote_copy(
        src_ref=x_row.at[oth_rows],
        dst_ref=x_row.at[oth_rows],
        send_sem=core_send.at[0],
        recv_sem=core_recv.at[0],
        device_id=core_dev,
        device_id_type=MESH,
    ).wait_recv()
    k_row[oth_rows, :] = project(oth_rows, 1).astype(LOW)
    v_row[oth_rows, :] = (project(oth_rows, 2) + value_bias[...]).astype(LOW)

    lane = lax.broadcasted_iota(jnp.int32, (1, LANES), 1)
    head_lanes = ((lane < HEAD_DIM).astype(LOW), (lane >= HEAD_DIM).astype(LOW))

    def pair_cols(head):
        return slice(LANES * (head // 2), LANES * (head // 2) + LANES)

    def score_part(head, part):
        cols = pair_cols(head)
        keys = slice(BLOCK * part, BLOCK * part + BLOCK)
        scores = dot_nt(q_own[:, cols] * head_lanes[head % 2], k_row[keys, cols])
        return jnp.where(key_live[:, keys], scores, -1e30)

    gathered = {}

    def head_gather(head):
        cols = pair_cols(head)
        gathered[head] = dot_nn(soft[head], v_row[:, cols] * head_lanes[head % 2])
        if head % 2 == 1:
            att_own[:, cols] = (gathered[head - 1] + gathered[head]).astype(LOW)

    def peak_of(part):
        return jnp.max(part, axis=-1, keepdims=True)

    def total_of(part):
        return jnp.sum(part, axis=-1, keepdims=True)

    ahead = [score_part(0, 0), score_part(0, 1)]
    for head in range(HEADS):
        scores = ahead
        ahead = []
        if head + 1 < HEADS:
            ahead.append(score_part(head + 1, 0))
        peak = jnp.maximum(peak_of(scores[0]), peak_of(scores[1]))
        if head + 1 < HEADS:
            ahead.append(score_part(head + 1, 1))
        terms = [jnp.exp(part - peak) for part in scores]
        if head > 0:
            head_gather(head - 1)
        scale = 1.0 / (total_of(terms[0]) + total_of(terms[1]))
        for part in range(2):
            keys = slice(BLOCK * part, BLOCK * part + BLOCK)
            soft[head, :, keys] = (terms[part] * scale).astype(LOW)
    head_gather(HEADS - 1)
    core_copies.append(to_core(1, att_own, att_oth))

    load_wo.wait()
    branch = dot_nn(att_own[...], wo[...]) + output_bias[...]
    resid = x_row[own_rows, :].astype(FULL) + branch
    centre = resid - row_mean(resid)
    scale_one = lax.rsqrt(row_mean(centre * centre) + norm_eps)
    normal = centre * scale_one
    norm_one[...] = normal
    mix_own[...] = (normal * first_gain[...] + first_shift[...]).astype(LOW)
    core_copies.append(to_core(2, mix_own, mix_oth))

    load_we.wait()

    act_copies = []
    for at in range(6):
        cols = slice(512 * at, 512 * at + 512)
        expanded = dot_nn(mix_own[...], we[:, cols]) + expand_bias[:, cols]
        gate = 0.5 + 0.5 * lax.erf(expanded * (2.0**-0.5))
        bell = jnp.exp(expanded * expanded * -0.5) * ((2.0 * jnp.pi) ** -0.5)
        act_own[:, cols] = (expanded * gate).astype(LOW)
        slope[:, cols] = (gate + expanded * bell).astype(LOW)
        if at % 2 == 1:
            piece = slice(512 * at - 512, 512 * at + 512)
            act_copies.append(
                to_core(9 + at // 2, act_own.at[:, piece], act_oth.at[:, piece])
            )

    load_wr.wait()
    reduced = dot_nn(act_own[...], wr[...]) + reduce_bias[...]
    mixed = norm_one[...] * first_gain[...] + first_shift[...]
    resid = mixed + reduced
    centre = resid - row_mean(resid)
    scale_two = lax.rsqrt(row_mean(centre * centre) + norm_eps)
    normal = centre * scale_two
    out_own[...] = (normal * second_gain[...] + second_shift[...]).astype(LOW)
    store_out = pltpu.make_async_copy(out_own, layer_output, out_sem.at[0])
    store_out.start()

    answered = answered > 0
    start_slot = jnp.where(answered, start_at, 0)
    end_slot = jnp.where(answered, end_at, 0)
    load_up.wait()
    cot = up[...].astype(FULL) * row_live
    cot = cot + (token_at == start_slot).astype(FULL) * start_vector[...]
    cot = cot + (token_at == end_slot).astype(FULL) * end_vector[...]

    def put_bias(first_row, vector):
        for at in range(vector.shape[1] // LANES):
            bias_sum[first_row + at : first_row + at + 1, :] = vector[
                :, at * LANES : (at + 1) * LANES
            ]

    put_bias(60, col_sum(cot * normal))
    put_bias(66, col_sum(cot))
    pulled = cot * second_gain[...]
    pulled = scale_two * (pulled - row_mean(pulled) - normal * row_mean(pulled * normal))
    resid_two[...] = pulled
    pulled_low = pulled.astype(LOW)
    gred_own[...] = pulled_low
    put_bias(54, col_sum(pulled_low.astype(FULL)))
    own_384 = pl.ds(aligned(blk * 384, 384), 384)
    oth_384 = pl.ds(aligned(oth * 384, 384), 384)
    core_copies.append(act_copies[0])
    core_copies.append(to_core(4, gred_own.at[:, oth_384], gred_oth))

    def send(src, dst, send_sem, recv_sem, dev):
        pltpu.make_async_remote_copy(
            src_ref=src,
            dst_ref=dst,
            send_sem=send_sem,
            recv_sem=recv_sem,
            device_id=dev,
            device_id_type=MESH,
        ).start()

    def wait_recv(dst, recv_sem):
        pltpu.make_async_remote_copy(
            src_ref=dst,
            dst_ref=dst,
            send_sem=recv_sem,
            recv_sem=recv_sem,
            device_id=core_dev,
            device_id_type=MESH,
        ).wait_recv()

    def wait_send(src, send_sem):
        pltpu.make_async_remote_copy(
            src_ref=src,
            dst_ref=src,
            send_sem=send_sem,
            recv_sem=send_sem,
            device_id=core_dev,
            device_id_type=MESH,
        ).wait_send()

    def owner(plane, x_at, y_at):
        return 4 * plane + 2 * y_at + x_at

    def add_unit(chip, unit, arrivals):
        value = grad[chip, unit].astype(FULL)
        for arrival in arrivals:
            value = value + arrival.astype(FULL)
        grad[chip, unit] = value.astype(LOW)

    def paired(plane, unit):
        return unit >= 6 - PAIRED[plane]

    def kept(plane):
        return (lax.rem(zz, 2) == 0) if plane < 2 else (lax.rem(zz, 2) == 1)

    def taking_part(plane, unit, step):
        if paired(plane, unit):
            pl.when(kept(plane))(step)
        else:
            step()

    def pair_copy(plane, unit):
        return pltpu.make_async_remote_copy(
            src_ref=grad.at[pl.ds(4 * plane, 4), unit],
            dst_ref=pair_in.at[plane % 2, 5 - unit],
            send_sem=pair_send.at[plane, unit],
            recv_sem=pair_recv.at[plane, unit],
            device_id=pair_dev,
            device_id_type=MESH,
        )

    def crossing(plane, unit):
        x_first = (plane + unit) % 2 == 0
        first_dev, second_dev = (x_dev, y_dev) if x_first else (y_dev, x_dev)
        beside = owner(plane, 1 - xx, yy) if x_first else owner(plane, xx, 1 - yy)
        behind = owner(plane, xx, 1 - yy) if x_first else owner(plane, 1 - xx, yy)
        return first_dev, second_dev, beside, behind

    def first_copies(plane, unit, slots=(0, 1)):
        first_dev, _, beside, _ = crossing(plane, unit)
        chips = (owner(plane, 1 - xx, 1 - yy), beside)
        return [
            pltpu.make_async_remote_copy(
                src_ref=grad.at[chips[slot], unit],
                dst_ref=first_in.at[plane, unit, slot],
                send_sem=first_send.at[plane, unit, slot],
                recv_sem=first_recv.at[plane, unit, slot],
                device_id=first_dev,
                device_id_type=MESH,
            )
            for slot in slots
        ]

    def second_copy(plane, unit):
        _, second_dev, _, behind = crossing(plane, unit)
        return pltpu.make_async_remote_copy(
            src_ref=grad.at[behind, unit],
            dst_ref=second_in.at[plane, unit],
            send_sem=second_send.at[plane, unit],
            recv_sem=second_recv.at[plane, unit],
            device_id=second_dev,
            device_id_type=MESH,
        )

    def chained(plane, unit):
        return CHAINED[plane] and not paired(plane, unit)

    def last_slot(unit, source):
        return jnp.where(blk == unit // 3, 0, 12) + 4 * (unit % 3) + source

    def passing_slot(plane, unit):
        return 24 + 6 * sum(CHAINED[:plane]) + unit

    def far_copy(plane, unit):
        below = zz < plane
        core = unit // 3
        if chained(plane, unit):
            chip = jnp.where(below, dp + 4, dp - 4)
            ends = jnp.where(below, zz + 1, zz - 1) == plane
            last = last_slot(unit, jnp.where(below, 0, 1))
            slot = jnp.where(ends, last, passing_slot(plane, unit))
            core = jnp.where(ends, core, blk)
        else:
            chip = owner(plane, xx, yy)
            slot = last_slot(unit, jnp.where(below, zz, zz - 1))
        return pltpu.make_async_remote_copy(
            src_ref=grad.at[owner(plane, xx, yy), unit],
            dst_ref=far_in.at[slot],
            send_sem=far_send.at[plane, unit],
            recv_sem=far_recv.at[slot],
            device_id=(chip, core),
            device_id_type=MESH,
        )

    def beside_copy(unit):
        slot = 12 + 4 * (unit % 3) + 3
        return pltpu.make_async_remote_copy(
            src_ref=grad.at[dp, unit],
            dst_ref=far_in.at[slot],
            send_sem=beside_send.at[unit % 3],
            recv_sem=far_recv.at[slot],
            device_id=core_dev,
            device_id_type=MESH,
        )

    def pair_step(plane, unit):
        @pl.when(jnp.logical_not(kept(plane)))
        def _():
            pair_copy(plane, unit).start()

    def pair_add(plane, unit):
        @pl.when(kept(plane))
        def _():
            pair_copy(plane, unit).wait_recv()

            @pl.loop(0, 4)
            def _(chip):
                add_unit(4 * plane + chip, unit, [pair_in[plane % 2, 5 - unit, chip]])

            for copy in first_copies(plane, unit):
                copy.start()

    def first_step(plane, unit):
        for copy in first_copies(plane, unit):
            copy.start()

    def second_step(plane, unit):
        def step():
            first_copies(plane, unit, (0,))[0].wait_recv()
            _, _, _, behind = crossing(plane, unit)
            add_unit(behind, unit, [first_in[plane, unit, 0]])
            second_copy(plane, unit).start()

        taking_part(plane, unit, step)

    def third_step(plane, unit):
        def step():
            first_copies(plane, unit, (1,))[0].wait_recv()
            second_copy(plane, unit).wait_recv()
            add_unit(
                owner(plane, xx, yy), unit, [first_in[plane, unit, 1], second_in[plane, unit]]
            )
            leaves = zz != plane
            if chained(plane, unit):
                leaves = leaves & ((zz == 0) | (zz == 3))

            @pl.when(leaves)
            def _():
                far_copy(plane, unit).start()

            @pl.when((zz == plane) & (blk != unit // 3))
            def _():
                beside_copy(unit).start()

        taking_part(plane, unit, step)

    def chain_step(plane, unit):
        @pl.when((zz != plane) & (zz > 0) & (zz < 3))
        def _():
            slot = passing_slot(plane, unit)
            wait_recv(far_in.at[slot], far_recv.at[slot])
            add_unit(owner(plane, xx, yy), unit, [far_in[slot]])
            far_copy(plane, unit).start()

    def finish_step(_, unit):
        for plane in range(4):
            if paired(plane, unit):
                sources = [z for z in range(4) if z != plane and (z % 2 == 0) == (plane < 2)]
                sources = [z if z < plane else z - 1 for z in sources]
            elif CHAINED[plane]:
                sources = ([0] if plane > 0 else []) + ([1] if plane < 3 else [])
            else:
                sources = [0, 1, 2]

            gave = paired(plane, unit) and (plane % 2 == 0) != (plane < 2)

            @pl.when((zz == plane) & (blk == unit // 3))
            def _():
                for half in range(2):
                    first = 12 * half + 4 * (unit % 3)
                    slots = [first + source for source in sources]
                    if half == 1 and not gave:
                        slots.append(first + 3)
                    for slot in slots:
                        wait_recv(far_in.at[slot], far_recv.at[slot])
                    terms = [far_in[slot].astype(FULL) for slot in slots]
                    if half == 0 and not gave:
                        terms.append(grad[dp, unit].astype(FULL))
                    total[half, unit % 3] = sum(terms[1:], terms[0])

    def place_step(_, unit):
        core, local = unit // 3, unit % 3

        @pl.when(blk == core)
        def _():
            lay_out(0, core, local)
            lay_out(1, 1 - core, local)
            if unit == 0:
                @pl.when(dp > 0)
                def _():
                    hand_back((dp - 1, 1))

            elif unit == 3:
                hand_back(core_dev)
            if local < 2:
                move_rows(*((0, 9), (9, 19))[local])

    def lay_out(half, column_half, local):
        kind_at = 3 * device + local
        kinds = (
            (kind_at < 24, 32, 9),
            (((kind_at >= 24) & (kind_at < 32)) | (kind_at >= 64), 96, 3),
            ((kind_at >= 32) & (kind_at < 64), 24, 12),
        )
        for fits, rows, tiles in kinds:

            @pl.when(fits)
            def _():
                for tile in range(tiles):
                    for group in range(rows // 8):
                        at = rows * tile + 8 * group
                        to = 576 * local + 16 * group * tiles + tile + column_half * tiles
                        flat[pl.ds(to, 8, stride=2 * tiles), :] = total[
                            half, local, at : at + 8, :
                        ]

    def hand_back(dev):
        send(flat.at[0:72], flat.at[1728:1800], fix_send.at[0], fix_recv.at[0], dev)

    shift = 32 * lax.rem(device, 4)
    skip = (9 * device) // 4
    stays = lane < LANES - shift

    def move_rows(first, last):
        @pl.loop(first, last)
        def _(at):
            rows = at * 56
            one = pltpu.roll(flat[pl.ds(rows + skip, 56), :], LANES - shift, 1)
            two = pltpu.roll(flat[pl.ds(rows + skip + 1, 56), :], LANES - shift, 1)
            placed[pl.ds(aligned(rows, 8), 56), :] = jnp.where(stays, one, two)

    corner = (xx == 1) & (yy == 1)
    last = dp == CHIPS - 1

    def bias_step(hop, _):
        def leaves(here, slot, dev):
            @pl.when(here)
            def _():
                send(bias_sum, bias_in.at[slot], bias_send.at[0], bias_recv.at[slot], dev)

        def comes(here, slot):
            @pl.when(here)
            def _():
                wait_recv(bias_in.at[slot], bias_recv.at[slot])
                bias_sum[...] += bias_in[slot]

        if hop == 0:
            leaves(xx == 0, 0, x_dev)
        elif hop == 1:
            comes(xx == 1, 0)
            leaves((xx == 1) & (yy == 0), 1, y_dev)
        else:
            comes(corner, 1)
            leaves(corner & (zz < 3), 2 + 2 * zz + blk, (CHIPS - 1, 1))
            leaves(last & (blk == 0), 8, core_dev)

    steps = {
        "bias": bias_step,
        "pair": pair_step,
        "add": pair_add,
        "first": first_step,
        "second": second_step,
        "third": third_step,
        "chain": chain_step,
        "finish": finish_step,
        "place": place_step,
    }

    def serve(after):
        for what, plane, unit in SCHEDULE.get(after, ()):
            steps[what](plane, unit)

    def put_unit(at, rows, values):
        chip, unit = (at // 6, at % 6) if isinstance(at, int) else (lax.div(at, 6), lax.rem(at, 6))
        grad[chip, unit, rows, :] = values.astype(LOW)

    for copy in act_copies:
        copy.wait_recv()
    core_copies[4].wait_recv()

    reduced_both = both(gred_own[:, own_384], gred_oth[...])

    def reduce_rows(first, count, before=0):
        cols = slice(96 * (first - 64) - before, 96 * (first - 64 + count))
        part = dot_tn(both(act_own[:, cols], act_oth[:, cols]), reduced_both)
        for unit in range(count):
            for tile in range(3):
                put_unit(
                    first + unit,
                    slice(96 * tile, 96 * tile + 96),
                    part[
                        before + 96 * unit : before + 96 * unit + 96,
                        LANES * tile : LANES * tile + LANES,
                    ],
                )

    for third in range(3):
        for chip in range(12, CHIPS):
            first = 6 * chip + 2 * third
            reduce_rows(first, 2, before=96 * (first - 64) % LANES)
        serve("reduce" + str(third))
    reduce_rows(64, 8)
    serve("reduce3")

    for at in range(6):
        half = oth if at < 3 else blk
        part_at = at % 3 * 512
        cols = pl.ds(aligned(half * 1536 + part_at, 512), 512)
        grad_active = dot_nt(gred_own[...], wr[cols, :])
        grad_expanded = (grad_active * slope[:, cols].astype(FULL)).astype(LOW)
        gexp_own[half, :, part_at : part_at + 512] = grad_expanded
        sums = col_sum(grad_expanded.astype(FULL))
        for tile in range(4):
            bias_sum[pl.ds(30 + half * 12 + at % 3 * 4 + tile, 1), :] = sums[
                :, LANES * tile : LANES * tile + LANES
            ]
        if at == 2:
            core_copies.append(to_core(5, gexp_own.at[oth], gexp_oth))

    serve("slopes")
    grad_mixed = resid_two[...]
    for half in range(2):
        grad_mixed = grad_mixed + dot_nt(
            gexp_own[half], we[:, 1536 * half : 1536 * half + 1536]
        )

    normal = norm_one[...]
    put_bias(18, col_sum(grad_mixed * normal))
    put_bias(24, col_sum(grad_mixed))
    pulled = grad_mixed * first_gain[...]
    pulled = scale_one * (pulled - row_mean(pulled) - normal * row_mean(pulled * normal))
    resid_one[...] = pulled
    pulled_low = pulled.astype(LOW)
    gbr_own[...] = pulled_low
    put_bias(12, col_sum(pulled_low.astype(FULL)))
    core_copies.append(to_core(6, gbr_own.at[:, oth_384], gbr_oth))

    serve("norm")

    core_copies[2].wait_recv()
    core_copies[5].wait_recv()

    @pl.loop(0, 6, unroll=3)
    def _(at):
        cols = pl.ds(aligned(at * 256, 256), 256)
        part = dot_tn(
            both(mix_own[...], mix_oth[...]), both(gexp_own[blk, :, cols], gexp_oth[:, cols])
        )
        rows = pl.ds(aligned(at * 48, 48), 48)
        for unit in range(32):
            piece = part[24 * unit : 24 * unit + 24, :]
            put_unit(32 + unit, rows, both(piece[:, :LANES], piece[:, LANES:]))

    serve("expand")
    gatt[...] = dot_nt(gbr_own[...], wo[...]).astype(LOW)
    core_copies[1].wait_recv()
    core_copies[6].wait_recv()
    part = dot_tn(both(att_own[...], att_oth[...]), both(gbr_own[:, own_384], gbr_oth[...]))
    for unit in range(8):
        for tile in range(3):
            put_unit(24 + unit, slice(96 * tile, 96 * tile + 96), part[
                96 * unit : 96 * unit + 96, LANES * tile : LANES * tile + LANES
            ])
    serve("output")

    qt[...] = q_own[...].T
    gat[...] = gatt[...].T
    load_te.wait()

    def head_pair(pair):
        cols = pl.ds(aligned(pair * LANES, LANES), LANES)
        ga_pair = gatt[:, cols]
        k_pair = k_row[:, cols]
        v_pair = v_row[:, cols]
        grad_query = None
        for side in range(2):
            rows = pl.ds(aligned(pair * LANES + side * HEAD_DIM, HEAD_DIM), HEAD_DIM)
            soft_low = soft[2 * pair + side]
            grad_soft = dot_nt(ga_pair * head_lanes[side], v_pair)
            soft_full = soft_low.astype(FULL)
            taught = te[2 * pair + side].astype(FULL) * live_map[...]
            shift = jnp.sum(taught - grad_soft * soft_full, axis=-1, keepdims=True)
            grad_scores = (soft_full * (grad_soft + shift) - taught).astype(LOW)
            part = dot_nn(grad_scores, k_pair * head_lanes[side])
            grad_query = part if grad_query is None else grad_query + part
            slot = pl.ds(aligned(pair * ROW, ROW), ROW)
            at = side * HEAD_DIM
            slope[at : at + HEAD_DIM, slot] = dot_nn(qt[rows, :], grad_scores).astype(LOW)
            at = at + LANES
            slope[at : at + HEAD_DIM, slot] = dot_nn(gat[rows, :], soft_low).astype(LOW)
        gpj_own[:, cols] = (grad_query * HEAD_DIM ** (-0.5)).astype(LOW)

    for part in range(3):

        @pl.loop(2 * part, 2 * part + 2)
        def _(pair):
            head_pair(pair)

        serve("heads" + str(part))

    def turned(pair, block, first):
        lanes = pl.ds(aligned(pair * ROW + block * BLOCK, BLOCK), BLOCK)
        return slope[first : first + LANES, lanes].T

    for pair in range(HEADS // 2):
        for first in (0, LANES):
            at = pair * LANES + first * (WIDTH // LANES)
            dkv_out[:, at : at + LANES] = turned(pair, oth, first)
    core_copies.append(to_core(7, dkv_out, dkv_in))
    core_copies[7].wait_recv()
    for pair in range(HEADS // 2):
        for first in (0, LANES):
            at = pair * LANES + first * (WIDTH // LANES)
            gpj_own[:, WIDTH + at : WIDTH + at + LANES] = (
                turned(pair, blk, first).astype(FULL) + dkv_in[:, at : at + LANES].astype(FULL)
            ).astype(LOW)
    serve("keys")
    own_1152 = pl.ds(aligned(blk * 1152, 1152), 1152)
    oth_1152 = pl.ds(aligned(oth * 1152, 1152), 1152)
    core_copies.append(to_core(8, gpj_own.at[:, oth_1152], gpj_oth))
    put_bias(0, col_sum(gpj_own[:, :WIDTH].astype(FULL)))
    put_bias(6, col_sum(gpj_own[:, 2 * WIDTH :].astype(FULL)))

    def input_gradient_part():
        gin_own[...] = (resid_one[...] + dot_nt(gpj_own[...], wp[...])).astype(LOW)
        pltpu.make_async_copy(gin_own, input_gradient, out_sem.at[1]).start()

    core_copies[8].wait_recv()

    @pl.loop(0, 3, unroll=3)
    def _(at):
        cols = pl.ds(aligned(at * 384, 384), 384)
        mine = pl.ds(aligned(blk * 1152 + at * 384, 384), 384)
        part = dot_tn(
            both(x_row[own_rows, :], x_row[oth_rows, :]), both(gpj_own[:, mine], gpj_oth[:, cols])
        )
        for unit in range(24):
            for tile in range(3):
                rows = pl.ds(aligned(at * 96 + 32 * tile, 32), 32)
                put_unit(unit, rows, part[
                    32 * unit : 32 * unit + 32, LANES * tile : LANES * tile + LANES
                ])

    serve("project")
    input_gradient_part()
    serve("input")

    serve("end")

    @pl.when(last & (blk == 1))
    def _():
        for at in range(2, 9):
            wait_recv(bias_in.at[at], bias_recv.at[at])
        flat[1728:1800, :] = sum((bias_in[at] for at in range(2, 9)), bias_sum[...])

    @pl.when(device < 2 * CHIPS - 1)
    def _():
        wait_recv(flat.at[1728:1800], fix_recv.at[0])

    early = pl.ds(0, 19 * 56)
    late = pl.ds(19 * 56, 12 * 56)
    stores = [
        pltpu.make_async_copy(placed.at[rows], grads.at[rows], out_sem.at[2 + at])
        for at, rows in enumerate((early, late))
    ]
    stores[0].start()
    move_rows(19, 31)
    stores[1].start()

    for copy in core_copies + act_copies[1:]:
        copy.wait_send()

    for plane in range(4):
        for unit in range(6):
            if paired(plane, unit):

                @pl.when(jnp.logical_not(kept(plane)))
                def _():
                    pair_copy(plane, unit).wait_send()

            def sent():
                for copy in first_copies(plane, unit):
                    copy.wait_send()
                second_copy(plane, unit).wait_send()

                @pl.when(zz != plane)
                def _():
                    far_copy(plane, unit).wait_send()

                @pl.when((zz == plane) & (blk != unit // 3))
                def _():
                    beside_copy(unit).wait_send()

            taking_part(plane, unit, sent)

    @pl.when(jnp.logical_not(last & (blk == 1)))
    def _():
        wait_send(bias_sum, bias_send.at[0])

    @pl.when(device > 0)
    def _():
        wait_send(flat.at[0:72], fix_send.at[0])

    store_out.wait()
    pltpu.make_async_copy(gin_own, input_gradient, out_sem.at[1]).wait()
    for store in stores:
        store.wait()


def hand_over(*refs):
    sources, targets, held, sems = refs[:3], refs[3:6], refs[6:9], refs[9]
    pieces = []
    for source, target, buffer in zip(sources, targets, held):
        rows = 248 if source.shape[0] % 248 == 0 else source.shape[0]
        for first in range(0, source.shape[0], rows):
            piece = pl.ds(first, rows)
            pieces.append((source.at[piece], buffer.at[piece], target.at[piece]))
    reads = []
    writes = []
    for at, (source, buffer, target) in enumerate(pieces):
        reads.append(pltpu.make_async_copy(source, buffer, sems.at[0, at]))
        writes.append(pltpu.make_async_copy(buffer, target, sems.at[1, at]))
    for read in reads:
        read.start()
    for read, write in zip(reads, writes):
        read.wait()
        write.start()
    for write in writes:
        write.wait()


def fused_layer(
    hidden_in,
    project_weight,
    output_weight,
    expand_weight,
    reduce_weight,
    query_bias,
    value_bias,
    output_bias,
    first_gain,
    first_shift,
    expand_bias,
    reduce_bias,
    second_gain,
    second_shift,
    upstream,
    teacher_maps,
    start_vector,
    end_vector,
    valid_length,
    start_index,
    end_index,
    answerable,
):
    vectors = (
        query_bias,
        value_bias,
        output_bias,
        first_gain,
        first_shift,
        expand_bias,
        reduce_bias,
        second_gain,
        second_shift,
        start_vector,
        end_vector,
    )
    scalars = (valid_length, start_index, end_index, answerable)
    anywhere = pl.BlockSpec(memory_space=pl.ANY)
    in_vmem = pl.BlockSpec(memory_space=pltpu.VMEM)

    def low(*shape):
        return pltpu.VMEM(shape, LOW)

    def full(*shape):
        return pltpu.VMEM(shape, FULL)

    dma = pltpu.SemaphoreType.DMA
    scratch = [
        low(WIDTH, 3 * WIDTH),
        low(WIDTH, WIDTH),
        low(WIDTH, FF),
        low(FF, WIDTH),
        low(HEADS, BLOCK, ROW),
        low(BLOCK, WIDTH),
        low(ROW, WIDTH),
        tuple(full(1, vector.shape[0]) for vector in vectors),
        low(BLOCK, WIDTH),
        low(ROW, WIDTH),
        low(ROW, WIDTH),
        low(HEADS, BLOCK, ROW),
        low(BLOCK, WIDTH),
        low(BLOCK, WIDTH),
        low(BLOCK, WIDTH),
        low(BLOCK, WIDTH),
        low(BLOCK, FF),
        low(BLOCK, FF),
        low(BLOCK, FF),
        full(BLOCK, WIDTH),
        full(BLOCK, WIDTH),
        full(BLOCK, WIDTH),
        low(BLOCK, WIDTH),
        low(BLOCK, WIDTH // 2),
        low(2, BLOCK, FF // 2),
        low(BLOCK, FF // 2),
        low(BLOCK, WIDTH),
        low(BLOCK, WIDTH // 2),
        low(BLOCK, WIDTH),
        low(WIDTH, BLOCK),
        low(WIDTH, BLOCK),
        low(BLOCK, 2 * WIDTH),
        low(BLOCK, 2 * WIDTH),
        low(BLOCK, 3 * WIDTH),
        low(BLOCK, 3 * WIDTH // 2),
        full(BLOCK, ROW),
        low(BLOCK, WIDTH),
        low(BLOCK, WIDTH),
        low(CHIPS, 6, UNIT, LANES),
        low(2, max(PAIRED), 4, UNIT, LANES),
        low(4, 6, 2, UNIT, LANES),
        low(4, 6, UNIT, LANES),
        low(24 + 6 * sum(CHAINED), UNIT, LANES),
        full(2, 3, UNIT, LANES),
        full(1816, LANES),
        full(1736, LANES),
        full(72, LANES),
        full(9, 72, LANES),
        dma((9,)),
        dma((len(vectors),)),
        dma((12,)),
        dma((12,)),
        dma((4, 6)),
        dma((4, 6)),
        dma((4, 6, 2)),
        dma((4, 6, 2)),
        dma((4, 6)),
        dma((4, 6)),
        dma((4, 6)),
        dma((24 + 6 * sum(CHAINED),)),
        dma((3,)),
        dma((1,)),
        dma((9,)),
        dma((1,)),
        dma((1,)),
        dma((4,)),
    ]
    results = (
        jax.ShapeDtypeStruct((BLOCK, WIDTH), LOW),
        jax.ShapeDtypeStruct((BLOCK, WIDTH), LOW),
        jax.ShapeDtypeStruct((1736, LANES), FULL),
    )
    made = pl.pallas_call(
        layer_kernel,
        out_shape=results,
        in_specs=[anywhere] * 7 + [(anywhere,) * len(vectors), (in_vmem,) * len(scalars)],
        out_specs=(anywhere,) * 3,
        scratch_shapes=scratch,
        compiler_params=pltpu.CompilerParams(
            collective_id=0, has_side_effects=True, vmem_limit_bytes=63 * 2**20
        ),
        name="encoder_layer",
    )(
        hidden_in.reshape(BLOCK, WIDTH),
        upstream.reshape(BLOCK, WIDTH),
        teacher_maps.reshape(HEADS, BLOCK, ROW),
        project_weight,
        output_weight,
        expand_weight,
        reduce_weight,
        vectors,
        scalars,
    )
    layer_output, input_gradient, grads = pl.pallas_call(
        hand_over,
        out_shape=results,
        in_specs=[anywhere] * 3,
        out_specs=(anywhere,) * 3,
        scratch_shapes=[pltpu.VMEM(result.shape, result.dtype) for result in results] + [dma((2, 9))],
        name="hand_over",
    )(*made)
    return (
        layer_output.reshape(1, BLOCK, WIDTH),
        input_gradient.reshape(1, BLOCK, WIDTH),
        grads.reshape(-1)[: 3 * 2 * UNIT * LANES + UNIT],
    )


def layer_norm(field_in, gain_vec, shift_vec):
    centre = field_in - jnp.mean(field_in, axis=-1, keepdims=True)
    spread = jnp.mean(centre * centre, axis=-1, keepdims=True)
    return centre * lax.rsqrt(spread + norm_eps) * gain_vec + shift_vec


def gelu_exact(field_in):
    return jax.nn.gelu(field_in, approximate=False)


def outer_sum(left, right):
    return jnp.einsum("nd,ne->de", left, right, preferred_element_type=jnp.float32)


def column_sum(values_low):
    return jnp.sum(values_low.astype(jnp.float32), axis=0)


def plain_layer(
    hidden_in,
    project_weight,
    output_weight,
    expand_weight,
    reduce_weight,
    query_bias,
    value_bias,
    output_bias,
    first_gain,
    first_shift,
    expand_bias,
    reduce_bias,
    second_gain,
    second_shift,
    upstream,
    teacher_maps,
    start_vector,
    end_vector,
    valid_length,
    start_index,
    end_index,
    answerable,
):
    row_count, block_len, width = hidden_in.shape
    blocks = lax.axis_size("blk")
    length = block_len * blocks
    offset = lax.axis_index("blk") * block_len
    token_count = row_count * block_len
    positions = offset + jnp.arange(block_len, dtype=jnp.int32)
    key_live = jnp.arange(length, dtype=jnp.int32)[None, :] < valid_length[:, None]
    row_live = positions[None, :] < valid_length[:, None]
    score_scale = HEAD_DIM ** (-0.5)
    tokens = hidden_in.reshape(token_count, width)
    joined_bias = jnp.concatenate([query_bias, jnp.zeros_like(query_bias), value_bias])
    project = (
        jnp.dot(tokens, project_weight, preferred_element_type=jnp.float32) + joined_bias
    ).astype(jnp.bfloat16)
    queries = project[:, :width].reshape(row_count, block_len, HEADS, HEAD_DIM)
    keys_own = project[:, width : 2 * width].reshape(row_count, block_len, width)
    values_own = project[:, 2 * width :].reshape(row_count, block_len, width)
    keys_all, values_all = (
        lax.all_gather(keys_own, "blk", axis=1, tiled=True),
        lax.all_gather(values_own, "blk", axis=1, tiled=True),
    )

    def scores_of(keys_full):
        raw = (
            jnp.einsum(
                "rqhe,rkhe->rhqk",
                queries,
                keys_full.reshape(row_count, length, HEADS, HEAD_DIM),
                preferred_element_type=jnp.float32,
            )
            * score_scale
        )
        return jnp.where(key_live[:, None, None, :], raw, -1e30)

    scores = scores_of(keys_all)
    row_peak = jnp.max(scores, axis=-1, keepdims=True)
    expo_terms = jnp.exp(scores - row_peak)
    row_total = jnp.sum(expo_terms, axis=-1, keepdims=True)
    soft_low = (expo_terms / row_total).astype(jnp.bfloat16)
    log_total = row_peak + jnp.log(row_total)
    attended = (
        jnp.einsum(
            "rhqk,rkhe->rqhe",
            soft_low,
            values_all.reshape(row_count, length, HEADS, HEAD_DIM),
            preferred_element_type=jnp.float32,
        )
        .reshape(token_count, width)
        .astype(jnp.bfloat16)
    )
    branch = jnp.dot(attended, output_weight, preferred_element_type=jnp.float32) + output_bias
    resid_one = tokens.astype(jnp.float32) + branch
    mixed, first_pull = jax.vjp(layer_norm, resid_one, first_gain, first_shift)
    mixed_low = mixed.astype(jnp.bfloat16)
    expanded = jnp.dot(mixed_low, expand_weight, preferred_element_type=jnp.float32) + expand_bias
    active, gelu_pull = jax.vjp(gelu_exact, expanded)
    active_low = active.astype(jnp.bfloat16)
    reduced = jnp.dot(active_low, reduce_weight, preferred_element_type=jnp.float32) + reduce_bias
    result, second_pull = jax.vjp(layer_norm, mixed + reduced, second_gain, second_shift)
    layer_output = result.astype(jnp.bfloat16).reshape(row_count, block_len, width)
    start_slot = jnp.where(answerable > 0, start_index, 0)
    end_slot = jnp.where(answerable > 0, end_index, 0)
    cotangent = (
        upstream.astype(jnp.float32) * row_live[..., None].astype(jnp.float32)
        + (positions[None, :] == start_slot[:, None])[..., None].astype(jnp.float32) * start_vector
        + (positions[None, :] == end_slot[:, None])[..., None].astype(jnp.float32) * end_vector
    )
    grad_resid_two, grad_second_gain, grad_second_shift = second_pull(
        cotangent.reshape(token_count, width)
    )
    grad_reduced = grad_resid_two.astype(jnp.bfloat16)
    grad_active = jnp.einsum(
        "nd,fd->nf", grad_reduced, reduce_weight, preferred_element_type=jnp.float32
    )
    grad_expanded = gelu_pull(grad_active)[0].astype(jnp.bfloat16)
    grad_mixed = grad_resid_two + jnp.einsum(
        "nf,df->nd", grad_expanded, expand_weight, preferred_element_type=jnp.float32
    )
    grad_resid_one, grad_first_gain, grad_first_shift = first_pull(grad_mixed)
    grad_branch = grad_resid_one.astype(jnp.bfloat16)
    grad_attended = jnp.einsum(
        "ne,de->nd", grad_branch, output_weight, preferred_element_type=jnp.float32
    )
    grad_attended = grad_attended.astype(jnp.bfloat16).reshape(
        row_count, block_len, HEADS, HEAD_DIM
    )
    keys_back, values_back = (
        lax.all_gather(keys_own, "blk", axis=1, tiled=True),
        lax.all_gather(values_own, "blk", axis=1, tiled=True),
    )
    keys_heads = keys_back.reshape(row_count, length, HEADS, HEAD_DIM)
    values_heads = values_back.reshape(row_count, length, HEADS, HEAD_DIM)
    soft = jnp.exp(scores_of(keys_back) - log_total)
    both_live = row_live[:, None, :, None] & key_live[:, None, None, :]
    teacher_live = jnp.where(both_live, teacher_maps.astype(jnp.float32), 0.0)
    teacher_total = jnp.sum(teacher_live, axis=-1, keepdims=True)
    grad_soft = jnp.einsum(
        "rqhe,rkhe->rhqk", grad_attended, values_heads, preferred_element_type=jnp.float32
    )
    row_delta = jnp.sum(grad_soft * soft, axis=-1, keepdims=True)
    grad_scores = (
        soft * (grad_soft - row_delta) + (teacher_total * soft - teacher_live) / length
    ).astype(jnp.bfloat16)
    grad_query = (
        jnp.einsum("rhqk,rkhe->rqhe", grad_scores, keys_heads, preferred_element_type=jnp.float32)
        * score_scale
    )
    grad_keys = (
        jnp.einsum(
            "rhqk,rqhe->rkhe", grad_scores, queries, preferred_element_type=jnp.float32
        ).reshape(row_count, length, width)
        * score_scale
    )
    grad_values = jnp.einsum(
        "rhqk,rqhe->rkhe", soft_low, grad_attended, preferred_element_type=jnp.float32
    ).reshape(row_count, length, width)
    keys_grad_own, values_grad_own = (
        lax.psum_scatter(
            grad_keys.astype(jnp.bfloat16), "blk", scatter_dimension=1, tiled=True
        ).astype(jnp.float32),
        lax.psum_scatter(
            grad_values.astype(jnp.bfloat16), "blk", scatter_dimension=1, tiled=True
        ).astype(jnp.float32),
    )
    grad_project = jnp.concatenate(
        [
            grad_query.reshape(token_count, width),
            keys_grad_own.reshape(token_count, width),
            values_grad_own.reshape(token_count, width),
        ],
        axis=1,
    ).astype(jnp.bfloat16)
    grad_input = grad_resid_one + jnp.einsum(
        "ne,de->nd", grad_project, project_weight, preferred_element_type=jnp.float32
    )
    input_gradient = grad_input.astype(jnp.bfloat16).reshape(row_count, block_len, width)
    (
        tokens_both,
        project_both,
        attended_both,
        branch_both,
        mixed_both,
        expanded_both,
        active_both,
        reduced_both,
    ) = (
        lax.all_gather(tokens, "blk", axis=0, tiled=True),
        lax.all_gather(grad_project, "blk", axis=0, tiled=True),
        lax.all_gather(attended, "blk", axis=0, tiled=True),
        lax.all_gather(grad_branch, "blk", axis=0, tiled=True),
        lax.all_gather(mixed_low, "blk", axis=0, tiled=True),
        lax.all_gather(grad_expanded, "blk", axis=0, tiled=True),
        lax.all_gather(active_low, "blk", axis=0, tiled=True),
        lax.all_gather(grad_reduced, "blk", axis=0, tiled=True),
    )
    project_sums = column_sum(project_both)
    norm_grads = lax.psum(
        (grad_first_gain, grad_first_shift, grad_second_gain, grad_second_shift), "blk"
    )
    flat_grads = jnp.concatenate(
        [
            outer_sum(tokens_both, project_both).reshape(-1),
            outer_sum(attended_both, branch_both).reshape(-1),
            outer_sum(mixed_both, expanded_both).reshape(-1),
            outer_sum(active_both, reduced_both).reshape(-1),
            project_sums[:width],
            project_sums[2 * width :],
            column_sum(branch_both),
            norm_grads[0],
            norm_grads[1],
            column_sum(expanded_both),
            column_sum(reduced_both),
            norm_grads[2],
            norm_grads[3],
        ]
    )
    data_count = lax.axis_size("dp")
    piece_len = flat_grads.shape[0] // (data_count * blocks)
    mine = lax.dynamic_index_in_dim(
        flat_grads.reshape(data_count, blocks, piece_len), lax.axis_index("blk"), 1, keepdims=False
    )
    weight_gradients = lax.psum_scatter(mine, "dp", scatter_dimension=0, tiled=True).reshape(
        piece_len
    )
    return (layer_output, input_gradient, weight_gradients)


def solution(mesh):
    placed = (
        P("dp", "blk", None),
        P(),
        P(),
        P(),
        P(),
        P(),
        P(),
        P(),
        P(),
        P(),
        P(),
        P(),
        P(),
        P(),
        P("dp", "blk", None),
        P("dp", None, "blk", None),
        P(),
        P(),
        P("dp"),
        P("dp"),
        P("dp"),
        P("dp"),
    )
    fits = (mesh.shape["dp"], mesh.shape["blk"]) == (CHIPS, 2)
    layer = fused_layer if fits else plain_layer
    return jax.shard_map(
        layer,
        mesh=mesh,
        in_specs=placed,
        out_specs=(P("dp", "blk", None), P("dp", "blk", None), P(("dp", "blk"))),
        check_vma=False,
    )
```

```python
import jax
import jax.numpy as jnp
from jax import lax
from jax.experimental import pallas as pl
from jax.experimental.pallas import tpu as pltpu
from jax.sharding import PartitionSpec as P

HEADS = 12
HEAD_DIM = 64
WIDTH = 768
FF = 3072
BLOCK = 256
ROW = 512
UNIT = 288
CHIPS = 16
LANES = 128

MESH = pl.DeviceIdType.MESH
LOW = jnp.bfloat16
FULL = jnp.float32

norm_eps = 1e-12


def dot_nn(left, right):
    return jnp.dot(left, right, preferred_element_type=FULL)


def dot_nt(left, right):
    return lax.dot_general(left, right, (((1,), (1,)), ((), ())), preferred_element_type=FULL)


def dot_tn(left, right):
    return lax.dot_general(left, right, (((0,), (0,)), ((), ())), preferred_element_type=FULL)


def both(own, other):
    return jnp.concatenate([own, other], axis=0)


def col_sum(field):
    return jnp.sum(field, axis=0, keepdims=True)


def row_mean(field):
    return jnp.mean(field, axis=-1, keepdims=True)


SCHEDULE = {
    "reduce0": (
        ("first", 3, 1),
        ("first", 3, 0),
    ),
    "reduce1": (
        ("first", 3, 3),
    ),
    "reduce2": (
        ("first", 3, 4),
        ("pair", 3, 5),
    ),
    "norm": (
        ("pair", 3, 2),
        ("second", 3, 0),
        ("second", 3, 1),
    ),
    "expand": (
        ("second", 3, 3),
        ("first", 2, 4),
    ),
    "output": (
        ("first", 1, 1),
        ("pair", 1, 5),
        ("first", 2, 1),
    ),
    "heads0": (
        ("first", 1, 0),
    ),
    "heads4": (
        ("second", 2, 1),
        ("pair", 1, 2),
        ("third", 3, 1),
    ),
    "heads5": (
        ("second", 1, 1),
        ("first", 2, 3),
        ("second", 2, 4),
        ("pair", 2, 2),
        ("first", 1, 3),
        ("first", 2, 0),
    ),
    "project": (
        ("pair", 0, 5),
        ("third", 2, 1),
        ("second", 1, 0),
        ("second", 1, 3),
        ("first", 0, 1),
        ("first", 0, 4),
        ("third", 1, 1),
        ("second", 2, 0),
        ("first", 0, 0),
        ("third", 3, 0),
        ("pair", 2, 5),
        ("third", 2, 4),
    ),
    "end": (
        ("first", 0, 3),
        ("second", 0, 1),
        ("third", 1, 3),
        ("first", 0, 2),
        ("second", 0, 0),
        ("second", 0, 4),
        ("second", 0, 3),
        ("third", 3, 3),
        ("third", 1, 0),
        ("third", 0, 1),
        ("bias", 0, 0),
        ("add", 2, 2),
        ("second", 3, 4),
        ("first", 1, 4),
        ("second", 2, 3),
        ("second", 0, 2),
        ("third", 0, 0),
        ("third", 0, 4),
        ("third", 2, 0),
        ("second", 1, 4),
        ("add", 3, 5),
        ("add", 2, 5),
        ("second", 2, 2),
        ("chain", 0, 1),
        ("add", 0, 5),
        ("add", 3, 2),
        ("third", 0, 3),
        ("add", 1, 5),
        ("bias", 1, 0),
        ("chain", 0, 0),
        ("third", 0, 2),
        ("third", 3, 4),
        ("chain", 0, 4),
        ("add", 1, 2),
        ("third", 2, 2),
        ("third", 2, 3),
        ("second", 2, 5),
        ("second", 3, 5),
        ("second", 3, 2),
        ("third", 1, 4),
        ("second", 0, 5),
        ("chain", 0, 3),
        ("bias", 2, 0),
        ("second", 1, 5),
        ("chain", 0, 2),
        ("third", 0, 5),
        ("third", 2, 5),
        ("finish", 0, 1),
        ("second", 1, 2),
        ("third", 3, 5),
        ("third", 1, 5),
        ("finish", 0, 0),
        ("third", 1, 2),
        ("third", 3, 2),
        ("finish", 0, 4),
        ("place", 0, 0),
        ("finish", 0, 3),
        ("place", 0, 3),
        ("place", 0, 1),
        ("place", 0, 4),
        ("finish", 0, 5),
        ("place", 0, 5),
        ("finish", 0, 2),
        ("place", 0, 2),
    ),
}
PAIRED = ((5,), (5, 2), (5, 2), (5, 2))
CHAINED = (True, False, False, False)


def aligned(start, step):
    return pl.multiple_of(start, step)


def layer_kernel(
    hidden,
    upstream,
    teacher,
    w_project,
    w_output,
    w_expand,
    w_reduce,
    vectors,
    scalars,
    layer_output,
    input_gradient,
    grads,
    wp,
    wo,
    we,
    wr,
    te,
    up,
    x_row,
    vector_at,
    q_own,
    k_row,
    v_row,
    soft,
    att_own,
    att_oth,
    mix_own,
    mix_oth,
    act_own,
    act_oth,
    slope,
    norm_one,
    resid_two,
    resid_one,
    gred_own,
    gred_oth,
    gexp_own,
    gexp_oth,
    gbr_own,
    gbr_oth,
    gatt,
    qt,
    gat,
    dkv_in,
    gpj_own,
    gpj_oth,
    live_map,
    out_own,
    gin_own,
    grad,
    pair_in,
    first_in,
    second_in,
    far_in,
    total,
    flat,
    placed,
    bias_sum,
    bias_in,
    load_sem,
    vector_sem,
    core_send,
    core_recv,
    pair_send,
    pair_recv,
    first_send,
    first_recv,
    second_send,
    second_recv,
    far_send,
    far_recv,
    beside_send,
    bias_send,
    bias_recv,
    fix_send,
    fix_recv,
    out_sem,
):
    dp = lax.axis_index("dp")
    blk = lax.axis_index("blk")
    oth = 1 - blk
    xx = dp % 2
    yy = (dp // 2) % 2
    zz = dp // 4
    column = dp % 4
    core_dev = (dp, oth)
    x_dev = (dp + 1 - 2 * xx, blk)
    y_dev = (dp + 2 - 4 * yy, blk)
    pair_dev = (jnp.where(zz % 2 == 0, dp + 4, dp - 4), blk)
    device = dp * 2 + blk

    def load(at, src, dst):
        copy = pltpu.make_async_copy(src, dst, load_sem.at[at])
        copy.start()
        return copy

    own_rows = pl.ds(aligned(blk * BLOCK, BLOCK), BLOCK)
    oth_rows = pl.ds(aligned(oth * BLOCK, BLOCK), BLOCK)
    load_x = load(0, hidden, x_row.at[own_rows])
    load_wp = [
        load(6 + part, w_project.at[:, part_cols], wp.at[:, part_cols])
        for part, part_cols in enumerate(pl.ds(WIDTH * part, WIDTH) for part in range(3))
    ]
    small = []
    for at, (src, dst) in enumerate(zip(vectors, vector_at)):
        small.append(pltpu.make_async_copy(src, dst.at[0], vector_sem.at[at]))
    for copy in small:
        copy.start()
    (
        query_bias,
        value_bias,
        output_bias,
        first_gain,
        first_shift,
        expand_bias,
        reduce_bias,
        second_gain,
        second_shift,
        start_vector,
        end_vector,
    ) = vector_at

    barrier = pltpu.get_barrier_semaphore()

    def greet(dev):
        pl.semaphore_signal(barrier, inc=1, device_id=dev, device_id_type=MESH)

    greet(core_dev)
    greet(x_dev)
    greet(y_dev)
    for step in range(1, 4):
        greet((lax.rem(dp + 4 * step, CHIPS), blk))
        greet((lax.rem(dp + 4 * step, CHIPS), oth))

    @pl.when((blk == 1) & (dp < CHIPS - 1))
    def _():
        greet((dp + 1, 0))

    def to_core(at, src, dst):
        copy = pltpu.make_async_remote_copy(
            src_ref=src,
            dst_ref=dst,
            send_sem=core_send.at[at],
            recv_sem=core_recv.at[at],
            device_id=core_dev,
            device_id_type=MESH,
        )
        copy.start()
        return copy

    pl.semaphore_wait(barrier, 9 + ((blk == 0) & (dp > 0)).astype(jnp.int32))
    core_copies = [to_core(0, hidden, x_row.at[own_rows])]

    length, start_at, end_at, answered = (ref[...].reshape(1, 1) for ref in scalars)
    key_at = lax.broadcasted_iota(jnp.int32, (1, ROW), 1)
    key_live = key_at < length
    token_at = blk * BLOCK + lax.broadcasted_iota(jnp.int32, (BLOCK, 1), 0)
    row_live = (token_at < length).astype(FULL)
    live_map[...] = jnp.where(key_live, 1.0 / ROW, 0.0) * row_live

    def project(rows, part):
        return dot_nn(x_row[rows, :], wp[:, WIDTH * part : WIDTH * part + WIDTH])

    load_x.wait()
    load_wp[0].wait()
    for copy in small:
        copy.wait()
    own_queries = (project(own_rows, 0) + query_bias[...]).astype(LOW)
    q_own[...] = own_queries * jnp.asarray(HEAD_DIM ** (-0.5), LOW)
    load_wp[1].wait()
    load_wo = load(1, w_output, wo)
    load_we = load(2, w_expand, we)
    load_wr = load(3, w_reduce, wr)
    load_up = load(4, upstream, up)
    load_te = load(5, teacher, te)
    k_row[own_rows, :] = project(own_rows, 1).astype(LOW)
    load_wp[2].wait()
    v_row[own_rows, :] = (project(own_rows, 2) + value_bias[...]).astype(LOW)
    pltpu.make_async_remote_copy(
        src_ref=x_row.at[oth_rows],
        dst_ref=x_row.at[oth_rows],
        send_sem=core_send.at[0],
        recv_sem=core_recv.at[0],
        device_id=core_dev,
        device_id_type=MESH,
    ).wait_recv()
    k_row[oth_rows, :] = project(oth_rows, 1).astype(LOW)
    v_row[oth_rows, :] = (project(oth_rows, 2) + value_bias[...]).astype(LOW)

    lane = lax.broadcasted_iota(jnp.int32, (1, LANES), 1)
    head_lanes = ((lane < HEAD_DIM).astype(LOW), (lane >= HEAD_DIM).astype(LOW))

    def pair_cols(head):
        return slice(LANES * (head // 2), LANES * (head // 2) + LANES)

    def score_part(head, part):
        cols = pair_cols(head)
        keys = slice(BLOCK * part, BLOCK * part + BLOCK)
        scores = dot_nt(q_own[:, cols] * head_lanes[head % 2], k_row[keys, cols])
        return jnp.where(key_live[:, keys], scores, -1e30) if part == 1 else scores

    gathered = {}

    def head_gather(head):
        cols = pair_cols(head)
        gathered[head] = dot_nn(soft[head], v_row[:, cols] * head_lanes[head % 2])
        if head % 2 == 1:
            att_own[:, cols] = (gathered[head - 1] + gathered[head]).astype(LOW)

    def peak_of(part):
        return jnp.max(part, axis=-1, keepdims=True)

    def total_of(part):
        return jnp.sum(part, axis=-1, keepdims=True)

    ahead = [score_part(0, 0), score_part(0, 1)]
    for head in range(HEADS):
        scores = ahead
        ahead = []
        if head + 1 < HEADS:
            ahead.append(score_part(head + 1, 0))
        peak = jnp.maximum(peak_of(scores[0]), peak_of(scores[1]))
        if head + 1 < HEADS:
            ahead.append(score_part(head + 1, 1))
        terms = [jnp.exp(part - peak) for part in scores]
        if head > 0:
            head_gather(head - 1)
        scale = 1.0 / (total_of(terms[0]) + total_of(terms[1]))
        for part in range(2):
            keys = slice(BLOCK * part, BLOCK * part + BLOCK)
            soft[head, :, keys] = (terms[part] * scale).astype(LOW)
    head_gather(HEADS - 1)
    core_copies.append(to_core(1, att_own, att_oth))

    load_wo.wait()
    branch = dot_nn(att_own[...], wo[...]) + output_bias[...]
    resid = x_row[own_rows, :].astype(FULL) + branch
    centre = resid - row_mean(resid)
    scale_one = lax.rsqrt(row_mean(centre * centre) + norm_eps)
    normal = centre * scale_one
    norm_one[...] = normal
    mix_own[...] = (normal * first_gain[...] + first_shift[...]).astype(LOW)
    core_copies.append(to_core(2, mix_own, mix_oth))

    load_we.wait()

    act_copies = []
    for at in range(6):
        cols = slice(512 * at, 512 * at + 512)
        expanded = dot_nn(mix_own[...], we[:, cols]) + expand_bias[:, cols]
        gate = 0.5 + 0.5 * lax.erf(expanded * (2.0**-0.5))
        bell = jnp.exp(expanded * expanded * -0.5) * ((2.0 * jnp.pi) ** -0.5)
        act_own[:, cols] = (expanded * gate).astype(LOW)
        slope[:, cols] = (gate + expanded * bell).astype(LOW)
        if at % 2 == 1:
            piece = slice(512 * at - 512, 512 * at + 512)
            act_copies.append(
                to_core(9 + at // 2, act_own.at[:, piece], act_oth.at[:, piece])
            )

    load_wr.wait()
    reduced = dot_nn(act_own[...], wr[...]) + reduce_bias[...]
    mixed = norm_one[...] * first_gain[...] + first_shift[...]
    resid = mixed + reduced
    centre = resid - row_mean(resid)
    scale_two = lax.rsqrt(row_mean(centre * centre) + norm_eps)
    normal = centre * scale_two
    out_own[...] = (normal * second_gain[...] + second_shift[...]).astype(LOW)
    store_out = pltpu.make_async_copy(out_own, layer_output, out_sem.at[0])
    store_out.start()

    answered = answered > 0
    start_slot = jnp.where(answered, start_at, 0)
    end_slot = jnp.where(answered, end_at, 0)
    load_up.wait()
    cot = up[...].astype(FULL) * row_live
    cot = cot + (token_at == start_slot).astype(FULL) * start_vector[...]
    cot = cot + (token_at == end_slot).astype(FULL) * end_vector[...]

    def put_bias(first_row, vector):
        for at in range(vector.shape[1] // LANES):
            bias_sum[first_row + at : first_row + at + 1, :] = vector[
                :, at * LANES : (at + 1) * LANES
            ]

    put_bias(60, col_sum(cot * normal))
    put_bias(66, col_sum(cot))
    pulled = cot * second_gain[...]
    pulled = scale_two * (pulled - row_mean(pulled) - normal * row_mean(pulled * normal))
    resid_two[...] = pulled
    pulled_low = pulled.astype(LOW)
    gred_own[...] = pulled_low
    put_bias(54, col_sum(pulled_low.astype(FULL)))
    own_384 = pl.ds(aligned(blk * 384, 384), 384)
    oth_384 = pl.ds(aligned(oth * 384, 384), 384)
    core_copies.append(None)
    core_copies.append(to_core(4, gred_own.at[:, oth_384], gred_oth))

    def send(src, dst, send_sem, recv_sem, dev):
        pltpu.make_async_remote_copy(
            src_ref=src,
            dst_ref=dst,
            send_sem=send_sem,
            recv_sem=recv_sem,
            device_id=dev,
            device_id_type=MESH,
        ).start()

    def wait_recv(dst, recv_sem):
        pltpu.make_async_remote_copy(
            src_ref=dst,
            dst_ref=dst,
            send_sem=recv_sem,
            recv_sem=recv_sem,
            device_id=core_dev,
            device_id_type=MESH,
        ).wait_recv()

    def wait_send(src, send_sem):
        pltpu.make_async_remote_copy(
            src_ref=src,
            dst_ref=src,
            send_sem=send_sem,
            recv_sem=send_sem,
            device_id=core_dev,
            device_id_type=MESH,
        ).wait_send()

    def owner(plane, x_at, y_at):
        return 4 * plane + 2 * y_at + x_at

    def add_unit(chip, unit, arrivals):
        value = grad[chip, unit].astype(FULL)
        for arrival in arrivals:
            value = value + arrival.astype(FULL)
        grad[chip, unit] = value.astype(LOW)

    def paired(plane, unit):
        return unit in PAIRED[plane]

    def kept(plane):
        return (lax.rem(zz, 2) == 0) if plane < 2 else (lax.rem(zz, 2) == 1)

    def taking_part(plane, unit, step):
        if paired(plane, unit):
            pl.when(kept(plane))(step)
        else:
            step()

    def pair_copy(plane, unit):
        return pltpu.make_async_remote_copy(
            src_ref=grad.at[pl.ds(4 * plane, 4), unit],
            dst_ref=pair_in.at[plane % 2, PAIRED[plane].index(unit)],
            send_sem=pair_send.at[plane, unit],
            recv_sem=pair_recv.at[plane, unit],
            device_id=pair_dev,
            device_id_type=MESH,
        )

    def crossing(plane, unit):
        x_first = (plane + unit) % 2 == 0
        first_dev, second_dev = (x_dev, y_dev) if x_first else (y_dev, x_dev)
        beside = owner(plane, 1 - xx, yy) if x_first else owner(plane, xx, 1 - yy)
        behind = owner(plane, xx, 1 - yy) if x_first else owner(plane, 1 - xx, yy)
        return first_dev, second_dev, beside, behind

    def first_copies(plane, unit, slots=(0, 1)):
        first_dev, _, beside, _ = crossing(plane, unit)
        chips = (owner(plane, 1 - xx, 1 - yy), beside)
        return [
            pltpu.make_async_remote_copy(
                src_ref=grad.at[chips[slot], unit],
                dst_ref=first_in.at[plane, unit, slot],
                send_sem=first_send.at[plane, unit, slot],
                recv_sem=first_recv.at[plane, unit, slot],
                device_id=first_dev,
                device_id_type=MESH,
            )
            for slot in slots
        ]

    def second_copy(plane, unit):
        _, second_dev, _, behind = crossing(plane, unit)
        return pltpu.make_async_remote_copy(
            src_ref=grad.at[behind, unit],
            dst_ref=second_in.at[plane, unit],
            send_sem=second_send.at[plane, unit],
            recv_sem=second_recv.at[plane, unit],
            device_id=second_dev,
            device_id_type=MESH,
        )

    def chained(plane, unit):
        return CHAINED[plane] and not paired(plane, unit)

    def last_slot(unit, source):
        return jnp.where(blk == unit // 3, 0, 12) + 4 * (unit % 3) + source

    def passing_slot(plane, unit):
        return 24 + 6 * sum(CHAINED[:plane]) + unit

    def far_copy(plane, unit):
        below = zz < plane
        core = unit // 3
        if chained(plane, unit):
            chip = jnp.where(below, dp + 4, dp - 4)
            ends = jnp.where(below, zz + 1, zz - 1) == plane
            last = last_slot(unit, jnp.where(below, 0, 1))
            slot = jnp.where(ends, last, passing_slot(plane, unit))
            core = jnp.where(ends, core, blk)
        else:
            chip = owner(plane, xx, yy)
            slot = last_slot(unit, jnp.where(below, zz, zz - 1))
        return pltpu.make_async_remote_copy(
            src_ref=grad.at[owner(plane, xx, yy), unit],
            dst_ref=far_in.at[slot],
            send_sem=far_send.at[plane, unit],
            recv_sem=far_recv.at[slot],
            device_id=(chip, core),
            device_id_type=MESH,
        )

    def beside_copy(unit):
        slot = 12 + 4 * (unit % 3) + 3
        return pltpu.make_async_remote_copy(
            src_ref=grad.at[dp, unit],
            dst_ref=far_in.at[slot],
            send_sem=beside_send.at[unit % 3],
            recv_sem=far_recv.at[slot],
            device_id=core_dev,
            device_id_type=MESH,
        )

    def pair_step(plane, unit):
        @pl.when(jnp.logical_not(kept(plane)))
        def _():
            pair_copy(plane, unit).start()

    def pair_add(plane, unit):
        @pl.when(kept(plane))
        def _():
            pair_copy(plane, unit).wait_recv()

            @pl.loop(0, 4)
            def _(chip):
                add_unit(4 * plane + chip, unit, [pair_in[plane % 2, PAIRED[plane].index(unit), chip]])

            for copy in first_copies(plane, unit):
                copy.start()

    def first_step(plane, unit):
        for copy in first_copies(plane, unit):
            copy.start()

    def second_step(plane, unit):
        def step():
            first_copies(plane, unit, (0,))[0].wait_recv()
            _, _, _, behind = crossing(plane, unit)
            add_unit(behind, unit, [first_in[plane, unit, 0]])
            second_copy(plane, unit).start()

        taking_part(plane, unit, step)

    def third_step(plane, unit):
        def step():
            first_copies(plane, unit, (1,))[0].wait_recv()
            second_copy(plane, unit).wait_recv()
            add_unit(
                owner(plane, xx, yy), unit, [first_in[plane, unit, 1], second_in[plane, unit]]
            )
            leaves = zz != plane
            if chained(plane, unit):
                leaves = leaves & ((zz == 0) | (zz == 3))

            @pl.when(leaves)
            def _():
                far_copy(plane, unit).start()

            @pl.when((zz == plane) & (blk != unit // 3))
            def _():
                beside_copy(unit).start()

        taking_part(plane, unit, step)

    def chain_step(plane, unit):
        @pl.when((zz != plane) & (zz > 0) & (zz < 3))
        def _():
            slot = passing_slot(plane, unit)
            wait_recv(far_in.at[slot], far_recv.at[slot])
            add_unit(owner(plane, xx, yy), unit, [far_in[slot]])
            far_copy(plane, unit).start()

    def finish_step(_, unit):
        for plane in range(4):
            if paired(plane, unit):
                sources = [z for z in range(4) if z != plane and (z % 2 == 0) == (plane < 2)]
                sources = [z if z < plane else z - 1 for z in sources]
            elif CHAINED[plane]:
                sources = ([0] if plane > 0 else []) + ([1] if plane < 3 else [])
            else:
                sources = [0, 1, 2]

            gave = paired(plane, unit) and (plane % 2 == 0) != (plane < 2)

            @pl.when((zz == plane) & (blk == unit // 3))
            def _():
                for half in range(2):
                    first = 12 * half + 4 * (unit % 3)
                    slots = [first + source for source in sources]
                    if half == 1 and not gave:
                        slots.append(first + 3)
                    for slot in slots:
                        wait_recv(far_in.at[slot], far_recv.at[slot])
                    terms = [far_in[slot].astype(FULL) for slot in slots]
                    if half == 0 and not gave:
                        terms.append(grad[dp, unit].astype(FULL))
                    total[half, unit % 3] = sum(terms[1:], terms[0])

    def place_step(_, unit):
        core, local = unit // 3, unit % 3

        @pl.when(blk == core)
        def _():
            lay_out(0, core, local)
            lay_out(1, 1 - core, local)
            if unit == 0:
                @pl.when(dp > 0)
                def _():
                    hand_back((dp - 1, 1))

            elif unit == 3:
                hand_back(core_dev)
            if local < 2:
                move_rows(*((0, 9), (9, 19))[local])

    def lay_out(half, column_half, local):
        kind_at = 3 * device + local
        kinds = (
            (kind_at < 24, 32, 9),
            (((kind_at >= 24) & (kind_at < 32)) | (kind_at >= 64), 96, 3),
            ((kind_at >= 32) & (kind_at < 64), 24, 12),
        )
        for fits, rows, tiles in kinds:

            @pl.when(fits)
            def _():
                for tile in range(tiles):
                    for group in range(rows // 8):
                        at = rows * tile + 8 * group
                        to = 576 * local + 16 * group * tiles + tile + column_half * tiles
                        flat[pl.ds(to, 8, stride=2 * tiles), :] = total[
                            half, local, at : at + 8, :
                        ]

    def hand_back(dev):
        send(flat.at[0:72], flat.at[1728:1800], fix_send.at[0], fix_recv.at[0], dev)

    shift = 32 * lax.rem(device, 4)
    skip = (9 * device) // 4
    stays = lane < LANES - shift

    def move_rows(first, last):
        @pl.loop(first, last)
        def _(at):
            rows = at * 56
            one = pltpu.roll(flat[pl.ds(rows + skip, 56), :], LANES - shift, 1)
            two = pltpu.roll(flat[pl.ds(rows + skip + 1, 56), :], LANES - shift, 1)
            placed[pl.ds(aligned(rows, 8), 56), :] = jnp.where(stays, one, two)

    corner = (xx == 1) & (yy == 1)
    last = dp == CHIPS - 1

    def bias_step(hop, _):
        def leaves(here, slot, dev):
            @pl.when(here)
            def _():
                send(bias_sum, bias_in.at[slot], bias_send.at[0], bias_recv.at[slot], dev)

        def comes(here, slot):
            @pl.when(here)
            def _():
                wait_recv(bias_in.at[slot], bias_recv.at[slot])
                bias_sum[...] += bias_in[slot]

        if hop == 0:
            leaves(xx == 0, 0, x_dev)
        elif hop == 1:
            comes(xx == 1, 0)
            leaves((xx == 1) & (yy == 0), 1, y_dev)
        else:
            comes(corner, 1)
            leaves(corner & (zz < 3), 2 + 2 * zz + blk, (CHIPS - 1, 1))
            leaves(last & (blk == 0), 8, core_dev)

    steps = {
        "bias": bias_step,
        "pair": pair_step,
        "add": pair_add,
        "first": first_step,
        "second": second_step,
        "third": third_step,
        "chain": chain_step,
        "finish": finish_step,
        "place": place_step,
    }

    def serve(after):
        for what, plane, unit in SCHEDULE.get(after, ()):
            steps[what](plane, unit)

    def put_unit(at, rows, values):
        chip, unit = (at // 6, at % 6) if isinstance(at, int) else (lax.div(at, 6), lax.rem(at, 6))
        grad[chip, unit, rows, :] = values.astype(LOW)

    def reduce_cols(first, count):
        before = 96 * (first - 64) % LANES
        return slice(96 * (first - 64) - before, 96 * (first - 64 + count)), before

    def put_reduced(first, count, before, part):
        for unit in range(count):
            for tile in range(3):
                put_unit(
                    first + unit,
                    slice(96 * tile, 96 * tile + 96),
                    part[
                        before + 96 * unit : before + 96 * unit + 96,
                        LANES * tile : LANES * tile + LANES,
                    ],
                )

    def slope_step(at):
        half = oth if at < 3 else blk
        part_at = at % 3 * 512
        cols = pl.ds(aligned(half * 1536 + part_at, 512), 512)
        grad_active = dot_nt(gred_own[...], wr[cols, :])
        grad_expanded = (grad_active * slope[:, cols].astype(FULL)).astype(LOW)
        gexp_own[half, :, part_at : part_at + 512] = grad_expanded
        sums = col_sum(grad_expanded.astype(FULL))
        for tile in range(4):
            bias_sum[pl.ds(30 + half * 12 + at % 3 * 4 + tile, 1), :] = sums[
                :, LANES * tile : LANES * tile + LANES
            ]

    reduced_own = gred_own[:, own_384]
    begun = {}
    for chip in range(12, CHIPS):
        cols, _ = reduce_cols(6 * chip, 2)
        begun[chip] = dot_tn(act_own[:, cols], reduced_own)
    slope_step(0)
    for copy in act_copies:
        copy.wait_recv()
    core_copies[4].wait_recv()
    reduced_both = both(reduced_own, gred_oth[...])

    for third in range(3):
        for chip in range(12, CHIPS):
            first = 6 * chip + 2 * third
            cols, before = reduce_cols(first, 2)
            if third == 0:
                part = begun[chip] + dot_tn(act_oth[:, cols], gred_oth[...])
            else:
                part = dot_tn(both(act_own[:, cols], act_oth[:, cols]), reduced_both)
            put_reduced(first, 2, before, part)
        serve("reduce" + str(third))
    cols, _ = reduce_cols(64, 8)
    put_reduced(64, 8, 0, dot_tn(both(act_own[:, cols], act_oth[:, cols]), reduced_both))
    serve("reduce3")

    for at in range(1, 6):
        slope_step(at)
        if at == 2:
            core_copies.append(to_core(5, gexp_own.at[oth], gexp_oth))
            serve("slopes0")

    serve("slopes")
    grad_mixed = resid_two[...]
    for half in range(2):
        grad_mixed = grad_mixed + dot_nt(
            gexp_own[half], we[:, 1536 * half : 1536 * half + 1536]
        )

    normal = norm_one[...]
    put_bias(18, col_sum(grad_mixed * normal))
    put_bias(24, col_sum(grad_mixed))
    pulled = grad_mixed * first_gain[...]
    pulled = scale_one * (pulled - row_mean(pulled) - normal * row_mean(pulled * normal))
    resid_one[...] = pulled
    pulled_low = pulled.astype(LOW)
    gbr_own[...] = pulled_low
    put_bias(12, col_sum(pulled_low.astype(FULL)))
    core_copies.append(to_core(6, gbr_own.at[:, oth_384], gbr_oth))

    serve("norm")

    core_copies[2].wait_recv()
    core_copies[5].wait_recv()

    @pl.loop(0, 6, unroll=3)
    def _(at):
        cols = pl.ds(aligned(at * 256, 256), 256)
        part = dot_tn(
            both(mix_own[...], mix_oth[...]), both(gexp_own[blk, :, cols], gexp_oth[:, cols])
        )
        rows = pl.ds(aligned(at * 48, 48), 48)
        for unit in range(32):
            piece = part[24 * unit : 24 * unit + 24, :]
            put_unit(32 + unit, rows, both(piece[:, :LANES], piece[:, LANES:]))

    serve("expand")
    gatt[...] = dot_nt(gbr_own[...], wo[...]).astype(LOW)
    core_copies[1].wait_recv()
    core_copies[6].wait_recv()
    part = dot_tn(both(att_own[...], att_oth[...]), both(gbr_own[:, own_384], gbr_oth[...]))
    for unit in range(8):
        for tile in range(3):
            put_unit(24 + unit, slice(96 * tile, 96 * tile + 96), part[
                96 * unit : 96 * unit + 96, LANES * tile : LANES * tile + LANES
            ])
    serve("output")

    qt[...] = q_own[...].T
    gat[...] = gatt[...].T
    load_te.wait()

    def head_pair(pair):
        cols = pl.ds(aligned(pair * LANES, LANES), LANES)
        ga_pair = gatt[:, cols]
        k_pair = k_row[:, cols]
        v_pair = v_row[:, cols]
        grad_query = None
        for side in range(2):
            rows = pl.ds(aligned(pair * LANES + side * HEAD_DIM, HEAD_DIM), HEAD_DIM)
            soft_low = soft[2 * pair + side]
            grad_soft = dot_nt(ga_pair * head_lanes[side], v_pair)
            soft_full = soft_low.astype(FULL)
            taught = te[2 * pair + side].astype(FULL) * live_map[...]
            shift = jnp.sum(taught - grad_soft * soft_full, axis=-1, keepdims=True)
            grad_scores = (soft_full * (grad_soft + shift) - taught).astype(LOW)
            part = dot_nn(grad_scores, k_pair * head_lanes[side])
            grad_query = part if grad_query is None else grad_query + part
            slot = pl.ds(aligned(pair * ROW, ROW), ROW)
            at = side * HEAD_DIM
            slope[at : at + HEAD_DIM, slot] = dot_nn(qt[rows, :], grad_scores).astype(LOW)
            at = at + LANES
            slope[at : at + HEAD_DIM, slot] = dot_nn(gat[rows, :], soft_low).astype(LOW)
        gpj_own[:, cols] = (grad_query * HEAD_DIM ** (-0.5)).astype(LOW)

    for pair in range(HEADS // 2):
        head_pair(pair)
        serve("heads" + str(pair))

    def turned(pair, block, first):
        lanes = pl.ds(aligned(pair * ROW + block * BLOCK, BLOCK), BLOCK)
        return slope[first : first + LANES, lanes].T

    for copy in act_copies:
        copy.wait_send()
    for pair in range(HEADS // 2):
        for first in (0, LANES):
            at = pair * LANES + first * (WIDTH // LANES)
            act_own[:, at : at + LANES] = turned(pair, oth, first)
    core_copies.append(to_core(7, act_own.at[:, : 2 * WIDTH], dkv_in))
    core_copies[7].wait_recv()
    for pair in range(HEADS // 2):
        for first in (0, LANES):
            at = pair * LANES + first * (WIDTH // LANES)
            gpj_own[:, WIDTH + at : WIDTH + at + LANES] = (
                turned(pair, blk, first).astype(FULL) + dkv_in[:, at : at + LANES].astype(FULL)
            ).astype(LOW)
    serve("keys")
    own_1152 = pl.ds(aligned(blk * 1152, 1152), 1152)
    oth_1152 = pl.ds(aligned(oth * 1152, 1152), 1152)
    core_copies.append(to_core(8, gpj_own.at[:, oth_1152], gpj_oth))
    put_bias(0, col_sum(gpj_own[:, :WIDTH].astype(FULL)))
    put_bias(6, col_sum(gpj_own[:, 2 * WIDTH :].astype(FULL)))

    def input_gradient_part():
        gin_own[...] = (resid_one[...] + dot_nt(gpj_own[...], wp[...])).astype(LOW)
        pltpu.make_async_copy(gin_own, input_gradient, out_sem.at[1]).start()

    input_gradient_part()
    serve("input")

    core_copies[8].wait_recv()

    @pl.loop(0, 3, unroll=3)
    def _(at):
        cols = pl.ds(aligned(at * 384, 384), 384)
        mine = pl.ds(aligned(blk * 1152 + at * 384, 384), 384)
        part = dot_tn(
            both(x_row[own_rows, :], x_row[oth_rows, :]), both(gpj_own[:, mine], gpj_oth[:, cols])
        )
        for unit in range(24):
            for tile in range(3):
                rows = pl.ds(aligned(at * 96 + 32 * tile, 32), 32)
                put_unit(unit, rows, part[
                    32 * unit : 32 * unit + 32, LANES * tile : LANES * tile + LANES
                ])

    serve("project")

    serve("end")

    @pl.when(last & (blk == 1))
    def _():
        for at in range(2, 9):
            wait_recv(bias_in.at[at], bias_recv.at[at])
        flat[1728:1800, :] = sum((bias_in[at] for at in range(2, 9)), bias_sum[...])

    @pl.when(device < 2 * CHIPS - 1)
    def _():
        wait_recv(flat.at[1728:1800], fix_recv.at[0])

    early = pl.ds(0, 19 * 56)
    late = pl.ds(19 * 56, 12 * 56)
    stores = [
        pltpu.make_async_copy(placed.at[rows], grads.at[rows], out_sem.at[2 + at])
        for at, rows in enumerate((early, late))
    ]
    stores[0].start()
    move_rows(19, 31)
    stores[1].start()

    for copy in core_copies:
        if copy is not None:
            copy.wait_send()

    for plane in range(4):
        for unit in range(6):
            if paired(plane, unit):

                @pl.when(jnp.logical_not(kept(plane)))
                def _():
                    pair_copy(plane, unit).wait_send()

            def sent():
                for copy in first_copies(plane, unit):
                    copy.wait_send()
                second_copy(plane, unit).wait_send()

                @pl.when(zz != plane)
                def _():
                    far_copy(plane, unit).wait_send()

                @pl.when((zz == plane) & (blk != unit // 3))
                def _():
                    beside_copy(unit).wait_send()

            taking_part(plane, unit, sent)

    @pl.when(jnp.logical_not(last & (blk == 1)))
    def _():
        wait_send(bias_sum, bias_send.at[0])

    @pl.when(device > 0)
    def _():
        wait_send(flat.at[0:72], fix_send.at[0])

    store_out.wait()
    pltpu.make_async_copy(gin_own, input_gradient, out_sem.at[1]).wait()
    for store in stores:
        store.wait()


def hand_over(*refs):
    sources, targets, held, sems = refs[:3], refs[3:6], refs[6:9], refs[9]
    pieces = []
    for source, target, buffer in zip(sources, targets, held):
        rows = 248 if source.shape[0] % 248 == 0 else source.shape[0]
        for first in range(0, source.shape[0], rows):
            piece = pl.ds(first, rows)
            pieces.append((source.at[piece], buffer.at[piece], target.at[piece]))
    reads = []
    writes = []
    for at, (source, buffer, target) in enumerate(pieces):
        reads.append(pltpu.make_async_copy(source, buffer, sems.at[0, at]))
        writes.append(pltpu.make_async_copy(buffer, target, sems.at[1, at]))
    for read in reads:
        read.start()
    for read, write in zip(reads, writes):
        read.wait()
        write.start()
    for write in writes:
        write.wait()


def fused_layer(
    hidden_in,
    project_weight,
    output_weight,
    expand_weight,
    reduce_weight,
    query_bias,
    value_bias,
    output_bias,
    first_gain,
    first_shift,
    expand_bias,
    reduce_bias,
    second_gain,
    second_shift,
    upstream,
    teacher_maps,
    start_vector,
    end_vector,
    valid_length,
    start_index,
    end_index,
    answerable,
):
    vectors = (
        query_bias,
        value_bias,
        output_bias,
        first_gain,
        first_shift,
        expand_bias,
        reduce_bias,
        second_gain,
        second_shift,
        start_vector,
        end_vector,
    )
    scalars = (valid_length, start_index, end_index, answerable)
    anywhere = pl.BlockSpec(memory_space=pl.ANY)
    in_vmem = pl.BlockSpec(memory_space=pltpu.VMEM)

    def low(*shape):
        return pltpu.VMEM(shape, LOW)

    def full(*shape):
        return pltpu.VMEM(shape, FULL)

    dma = pltpu.SemaphoreType.DMA
    scratch = [
        low(WIDTH, 3 * WIDTH),
        low(WIDTH, WIDTH),
        low(WIDTH, FF),
        low(FF, WIDTH),
        low(HEADS, BLOCK, ROW),
        low(BLOCK, WIDTH),
        low(ROW, WIDTH),
        tuple(full(1, vector.shape[0]) for vector in vectors),
        low(BLOCK, WIDTH),
        low(ROW, WIDTH),
        low(ROW, WIDTH),
        low(HEADS, BLOCK, ROW),
        low(BLOCK, WIDTH),
        low(BLOCK, WIDTH),
        low(BLOCK, WIDTH),
        low(BLOCK, WIDTH),
        low(BLOCK, FF),
        low(BLOCK, FF),
        low(BLOCK, FF),
        full(BLOCK, WIDTH),
        full(BLOCK, WIDTH),
        full(BLOCK, WIDTH),
        low(BLOCK, WIDTH),
        low(BLOCK, WIDTH // 2),
        low(2, BLOCK, FF // 2),
        low(BLOCK, FF // 2),
        low(BLOCK, WIDTH),
        low(BLOCK, WIDTH // 2),
        low(BLOCK, WIDTH),
        low(WIDTH, BLOCK),
        low(WIDTH, BLOCK),
        low(BLOCK, 2 * WIDTH),
        low(BLOCK, 3 * WIDTH),
        low(BLOCK, 3 * WIDTH // 2),
        full(BLOCK, ROW),
        low(BLOCK, WIDTH),
        low(BLOCK, WIDTH),
        low(CHIPS, 6, UNIT, LANES),
        low(2, max(map(len, PAIRED)), 4, UNIT, LANES),
        low(4, 6, 2, UNIT, LANES),
        low(4, 6, UNIT, LANES),
        low(24 + 6 * sum(CHAINED), UNIT, LANES),
        full(2, 3, UNIT, LANES),
        full(1816, LANES),
        full(1736, LANES),
        full(72, LANES),
        full(9, 72, LANES),
        dma((9,)),
        dma((len(vectors),)),
        dma((12,)),
        dma((12,)),
        dma((4, 6)),
        dma((4, 6)),
        dma((4, 6, 2)),
        dma((4, 6, 2)),
        dma((4, 6)),
        dma((4, 6)),
        dma((4, 6)),
        dma((24 + 6 * sum(CHAINED),)),
        dma((3,)),
        dma((1,)),
        dma((9,)),
        dma((1,)),
        dma((1,)),
        dma((4,)),
    ]
    results = (
        jax.ShapeDtypeStruct((BLOCK, WIDTH), LOW),
        jax.ShapeDtypeStruct((BLOCK, WIDTH), LOW),
        jax.ShapeDtypeStruct((1736, LANES), FULL),
    )
    made = pl.pallas_call(
        layer_kernel,
        out_shape=results,
        in_specs=[anywhere] * 7 + [(anywhere,) * len(vectors), (in_vmem,) * len(scalars)],
        out_specs=(anywhere,) * 3,
        scratch_shapes=scratch,
        compiler_params=pltpu.CompilerParams(
            collective_id=0, has_side_effects=True, vmem_limit_bytes=63 * 2**20
        ),
        name="encoder_layer",
    )(
        hidden_in.reshape(BLOCK, WIDTH),
        upstream.reshape(BLOCK, WIDTH),
        teacher_maps.reshape(HEADS, BLOCK, ROW),
        project_weight,
        output_weight,
        expand_weight,
        reduce_weight,
        vectors,
        scalars,
    )
    layer_output, input_gradient, grads = pl.pallas_call(
        hand_over,
        out_shape=results,
        in_specs=[anywhere] * 3,
        out_specs=(anywhere,) * 3,
        scratch_shapes=[pltpu.VMEM(result.shape, result.dtype) for result in results] + [dma((2, 9))],
        name="hand_over",
    )(*made)
    return (
        layer_output.reshape(1, BLOCK, WIDTH),
        input_gradient.reshape(1, BLOCK, WIDTH),
        grads.reshape(-1)[: 3 * 2 * UNIT * LANES + UNIT],
    )


def layer_norm(field_in, gain_vec, shift_vec):
    centre = field_in - jnp.mean(field_in, axis=-1, keepdims=True)
    spread = jnp.mean(centre * centre, axis=-1, keepdims=True)
    return centre * lax.rsqrt(spread + norm_eps) * gain_vec + shift_vec


def gelu_exact(field_in):
    return jax.nn.gelu(field_in, approximate=False)


def outer_sum(left, right):
    return jnp.einsum("nd,ne->de", left, right, preferred_element_type=jnp.float32)


def column_sum(values_low):
    return jnp.sum(values_low.astype(jnp.float32), axis=0)


def plain_layer(
    hidden_in,
    project_weight,
    output_weight,
    expand_weight,
    reduce_weight,
    query_bias,
    value_bias,
    output_bias,
    first_gain,
    first_shift,
    expand_bias,
    reduce_bias,
    second_gain,
    second_shift,
    upstream,
    teacher_maps,
    start_vector,
    end_vector,
    valid_length,
    start_index,
    end_index,
    answerable,
):
    row_count, block_len, width = hidden_in.shape
    blocks = lax.axis_size("blk")
    length = block_len * blocks
    offset = lax.axis_index("blk") * block_len
    token_count = row_count * block_len
    positions = offset + jnp.arange(block_len, dtype=jnp.int32)
    key_live = jnp.arange(length, dtype=jnp.int32)[None, :] < valid_length[:, None]
    row_live = positions[None, :] < valid_length[:, None]
    score_scale = HEAD_DIM ** (-0.5)
    tokens = hidden_in.reshape(token_count, width)
    joined_bias = jnp.concatenate([query_bias, jnp.zeros_like(query_bias), value_bias])
    project = (
        jnp.dot(tokens, project_weight, preferred_element_type=jnp.float32) + joined_bias
    ).astype(jnp.bfloat16)
    queries = project[:, :width].reshape(row_count, block_len, HEADS, HEAD_DIM)
    keys_own = project[:, width : 2 * width].reshape(row_count, block_len, width)
    values_own = project[:, 2 * width :].reshape(row_count, block_len, width)
    keys_all, values_all = (
        lax.all_gather(keys_own, "blk", axis=1, tiled=True),
        lax.all_gather(values_own, "blk", axis=1, tiled=True),
    )

    def scores_of(keys_full):
        raw = (
            jnp.einsum(
                "rqhe,rkhe->rhqk",
                queries,
                keys_full.reshape(row_count, length, HEADS, HEAD_DIM),
                preferred_element_type=jnp.float32,
            )
            * score_scale
        )
        return jnp.where(key_live[:, None, None, :], raw, -1e30)

    scores = scores_of(keys_all)
    row_peak = jnp.max(scores, axis=-1, keepdims=True)
    expo_terms = jnp.exp(scores - row_peak)
    row_total = jnp.sum(expo_terms, axis=-1, keepdims=True)
    soft_low = (expo_terms / row_total).astype(jnp.bfloat16)
    log_total = row_peak + jnp.log(row_total)
    attended = (
        jnp.einsum(
            "rhqk,rkhe->rqhe",
            soft_low,
            values_all.reshape(row_count, length, HEADS, HEAD_DIM),
            preferred_element_type=jnp.float32,
        )
        .reshape(token_count, width)
        .astype(jnp.bfloat16)
    )
    branch = jnp.dot(attended, output_weight, preferred_element_type=jnp.float32) + output_bias
    resid_one = tokens.astype(jnp.float32) + branch
    mixed, first_pull = jax.vjp(layer_norm, resid_one, first_gain, first_shift)
    mixed_low = mixed.astype(jnp.bfloat16)
    expanded = jnp.dot(mixed_low, expand_weight, preferred_element_type=jnp.float32) + expand_bias
    active, gelu_pull = jax.vjp(gelu_exact, expanded)
    active_low = active.astype(jnp.bfloat16)
    reduced = jnp.dot(active_low, reduce_weight, preferred_element_type=jnp.float32) + reduce_bias
    result, second_pull = jax.vjp(layer_norm, mixed + reduced, second_gain, second_shift)
    layer_output = result.astype(jnp.bfloat16).reshape(row_count, block_len, width)
    start_slot = jnp.where(answerable > 0, start_index, 0)
    end_slot = jnp.where(answerable > 0, end_index, 0)
    cotangent = (
        upstream.astype(jnp.float32) * row_live[..., None].astype(jnp.float32)
        + (positions[None, :] == start_slot[:, None])[..., None].astype(jnp.float32) * start_vector
        + (positions[None, :] == end_slot[:, None])[..., None].astype(jnp.float32) * end_vector
    )
    grad_resid_two, grad_second_gain, grad_second_shift = second_pull(
        cotangent.reshape(token_count, width)
    )
    grad_reduced = grad_resid_two.astype(jnp.bfloat16)
    grad_active = jnp.einsum(
        "nd,fd->nf", grad_reduced, reduce_weight, preferred_element_type=jnp.float32
    )
    grad_expanded = gelu_pull(grad_active)[0].astype(jnp.bfloat16)
    grad_mixed = grad_resid_two + jnp.einsum(
        "nf,df->nd", grad_expanded, expand_weight, preferred_element_type=jnp.float32
    )
    grad_resid_one, grad_first_gain, grad_first_shift = first_pull(grad_mixed)
    grad_branch = grad_resid_one.astype(jnp.bfloat16)
    grad_attended = jnp.einsum(
        "ne,de->nd", grad_branch, output_weight, preferred_element_type=jnp.float32
    )
    grad_attended = grad_attended.astype(jnp.bfloat16).reshape(
        row_count, block_len, HEADS, HEAD_DIM
    )
    keys_back, values_back = (
        lax.all_gather(keys_own, "blk", axis=1, tiled=True),
        lax.all_gather(values_own, "blk", axis=1, tiled=True),
    )
    keys_heads = keys_back.reshape(row_count, length, HEADS, HEAD_DIM)
    values_heads = values_back.reshape(row_count, length, HEADS, HEAD_DIM)
    soft = jnp.exp(scores_of(keys_back) - log_total)
    both_live = row_live[:, None, :, None] & key_live[:, None, None, :]
    teacher_live = jnp.where(both_live, teacher_maps.astype(jnp.float32), 0.0)
    teacher_total = jnp.sum(teacher_live, axis=-1, keepdims=True)
    grad_soft = jnp.einsum(
        "rqhe,rkhe->rhqk", grad_attended, values_heads, preferred_element_type=jnp.float32
    )
    row_delta = jnp.sum(grad_soft * soft, axis=-1, keepdims=True)
    grad_scores = (
        soft * (grad_soft - row_delta) + (teacher_total * soft - teacher_live) / length
    ).astype(jnp.bfloat16)
    grad_query = (
        jnp.einsum("rhqk,rkhe->rqhe", grad_scores, keys_heads, preferred_element_type=jnp.float32)
        * score_scale
    )
    grad_keys = (
        jnp.einsum(
            "rhqk,rqhe->rkhe", grad_scores, queries, preferred_element_type=jnp.float32
        ).reshape(row_count, length, width)
        * score_scale
    )
    grad_values = jnp.einsum(
        "rhqk,rqhe->rkhe", soft_low, grad_attended, preferred_element_type=jnp.float32
    ).reshape(row_count, length, width)
    keys_grad_own, values_grad_own = (
        lax.psum_scatter(
            grad_keys.astype(jnp.bfloat16), "blk", scatter_dimension=1, tiled=True
        ).astype(jnp.float32),
        lax.psum_scatter(
            grad_values.astype(jnp.bfloat16), "blk", scatter_dimension=1, tiled=True
        ).astype(jnp.float32),
    )
    grad_project = jnp.concatenate(
        [
            grad_query.reshape(token_count, width),
            keys_grad_own.reshape(token_count, width),
            values_grad_own.reshape(token_count, width),
        ],
        axis=1,
    ).astype(jnp.bfloat16)
    grad_input = grad_resid_one + jnp.einsum(
        "ne,de->nd", grad_project, project_weight, preferred_element_type=jnp.float32
    )
    input_gradient = grad_input.astype(jnp.bfloat16).reshape(row_count, block_len, width)
    (
        tokens_both,
        project_both,
        attended_both,
        branch_both,
        mixed_both,
        expanded_both,
        active_both,
        reduced_both,
    ) = (
        lax.all_gather(tokens, "blk", axis=0, tiled=True),
        lax.all_gather(grad_project, "blk", axis=0, tiled=True),
        lax.all_gather(attended, "blk", axis=0, tiled=True),
        lax.all_gather(grad_branch, "blk", axis=0, tiled=True),
        lax.all_gather(mixed_low, "blk", axis=0, tiled=True),
        lax.all_gather(grad_expanded, "blk", axis=0, tiled=True),
        lax.all_gather(active_low, "blk", axis=0, tiled=True),
        lax.all_gather(grad_reduced, "blk", axis=0, tiled=True),
    )
    project_sums = column_sum(project_both)
    norm_grads = lax.psum(
        (grad_first_gain, grad_first_shift, grad_second_gain, grad_second_shift), "blk"
    )
    flat_grads = jnp.concatenate(
        [
            outer_sum(tokens_both, project_both).reshape(-1),
            outer_sum(attended_both, branch_both).reshape(-1),
            outer_sum(mixed_both, expanded_both).reshape(-1),
            outer_sum(active_both, reduced_both).reshape(-1),
            project_sums[:width],
            project_sums[2 * width :],
            column_sum(branch_both),
            norm_grads[0],
            norm_grads[1],
            column_sum(expanded_both),
            column_sum(reduced_both),
            norm_grads[2],
            norm_grads[3],
        ]
    )
    data_count = lax.axis_size("dp")
    piece_len = flat_grads.shape[0] // (data_count * blocks)
    mine = lax.dynamic_index_in_dim(
        flat_grads.reshape(data_count, blocks, piece_len), lax.axis_index("blk"), 1, keepdims=False
    )
    weight_gradients = lax.psum_scatter(mine, "dp", scatter_dimension=0, tiled=True).reshape(
        piece_len
    )
    return (layer_output, input_gradient, weight_gradients)


def solution(mesh):
    placed = (
        P("dp", "blk", None),
        P(),
        P(),
        P(),
        P(),
        P(),
        P(),
        P(),
        P(),
        P(),
        P(),
        P(),
        P(),
        P(),
        P("dp", "blk", None),
        P("dp", None, "blk", None),
        P(),
        P(),
        P("dp"),
        P("dp"),
        P("dp"),
        P("dp"),
    )
    fits = (mesh.shape["dp"], mesh.shape["blk"]) == (CHIPS, 2)
    layer = fused_layer if fits else plain_layer
    return jax.shard_map(
        layer,
        mesh=mesh,
        in_specs=placed,
        out_specs=(P("dp", "blk", None), P("dp", "blk", None), P(("dp", "blk"))),
        check_vma=False,
    )
```

```python
import jax
import jax.numpy as jnp
from jax import lax
from jax.experimental import pallas as pl
from jax.experimental.pallas import tpu as pltpu
from jax.sharding import PartitionSpec as P

HEADS = 12
HEAD_DIM = 64
WIDTH = 768
FF = 3072
BLOCK = 256
ROW = 512
UNIT = 288
CHIPS = 16
LANES = 128

MESH = pl.DeviceIdType.MESH
LOW = jnp.bfloat16
FULL = jnp.float32

norm_eps = 1e-12


def dot_nn(left, right):
    return jnp.dot(left, right, preferred_element_type=FULL)


def dot_nt(left, right):
    return lax.dot_general(left, right, (((1,), (1,)), ((), ())), preferred_element_type=FULL)


def dot_tn(left, right):
    return lax.dot_general(left, right, (((0,), (0,)), ((), ())), preferred_element_type=FULL)


def both(own, other):
    return jnp.concatenate([own, other], axis=0)


def col_sum(field):
    return jnp.sum(field, axis=0, keepdims=True)


def row_mean(field):
    return jnp.mean(field, axis=-1, keepdims=True)


SCHEDULE = {
    "reduce0": (
        ("first", 3, 1),
        ("first", 3, 0),
    ),
    "reduce1": (
        ("first", 3, 3),
    ),
    "reduce2": (
        ("first", 3, 4),
        ("pair", 3, 5),
    ),
    "norm": (
        ("pair", 3, 2),
        ("second", 3, 0),
        ("second", 3, 1),
    ),
    "expand": (
        ("second", 3, 3),
        ("first", 2, 4),
    ),
    "output": (
        ("first", 1, 1),
        ("pair", 1, 5),
        ("first", 2, 1),
    ),
    "heads0": (
        ("first", 1, 0),
    ),
    "heads4": (
        ("second", 2, 1),
        ("pair", 1, 2),
        ("third", 3, 1),
    ),
    "heads5": (
        ("second", 1, 1),
        ("first", 2, 3),
        ("second", 2, 4),
        ("pair", 2, 2),
        ("first", 1, 3),
        ("first", 2, 0),
    ),
    "project": (
        ("pair", 0, 5),
        ("third", 2, 1),
        ("second", 1, 0),
        ("second", 1, 3),
        ("first", 0, 1),
        ("first", 0, 4),
        ("third", 1, 1),
        ("second", 2, 0),
        ("first", 0, 0),
        ("third", 3, 0),
        ("pair", 2, 5),
        ("third", 2, 4),
    ),
    "end": (
        ("first", 0, 3),
        ("second", 0, 1),
        ("third", 1, 3),
        ("first", 0, 2),
        ("second", 0, 0),
        ("second", 0, 4),
        ("second", 0, 3),
        ("third", 3, 3),
        ("third", 1, 0),
        ("third", 0, 1),
        ("bias", 0, 0),
        ("add", 2, 2),
        ("second", 3, 4),
        ("first", 1, 4),
        ("second", 2, 3),
        ("second", 0, 2),
        ("third", 0, 0),
        ("third", 0, 4),
        ("third", 2, 0),
        ("second", 1, 4),
        ("add", 3, 5),
        ("add", 2, 5),
        ("second", 2, 2),
        ("chain", 0, 1),
        ("add", 0, 5),
        ("add", 3, 2),
        ("third", 0, 3),
        ("add", 1, 5),
        ("bias", 1, 0),
        ("chain", 0, 0),
        ("third", 0, 2),
        ("third", 3, 4),
        ("chain", 0, 4),
        ("add", 1, 2),
        ("third", 2, 2),
        ("third", 2, 3),
        ("second", 2, 5),
        ("second", 3, 5),
        ("second", 3, 2),
        ("third", 1, 4),
        ("second", 0, 5),
        ("chain", 0, 3),
        ("bias", 2, 0),
        ("second", 1, 5),
        ("chain", 0, 2),
        ("third", 0, 5),
        ("third", 2, 5),
        ("finish", 0, 1),
        ("second", 1, 2),
        ("third", 3, 5),
        ("third", 1, 5),
        ("finish", 0, 0),
        ("third", 1, 2),
        ("third", 3, 2),
        ("finish", 0, 4),
        ("place", 0, 0),
        ("finish", 0, 3),
        ("place", 0, 3),
        ("place", 0, 1),
        ("place", 0, 4),
        ("finish", 0, 5),
        ("place", 0, 5),
        ("finish", 0, 2),
        ("place", 0, 2),
    ),
}
PAIRED = ((5,), (5, 2), (5, 2), (5, 2))
CHAINED = (True, False, False, False)


def aligned(start, step):
    return pl.multiple_of(start, step)


def layer_kernel(
    hidden,
    upstream,
    teacher,
    w_project,
    w_output,
    w_expand,
    w_reduce,
    vectors,
    scalars,
    layer_output,
    input_gradient,
    grads,
    wp,
    wo,
    we,
    wr,
    te,
    up,
    x_row,
    vector_at,
    q_own,
    k_row,
    v_row,
    soft,
    att_own,
    att_oth,
    mix_own,
    mix_oth,
    act_own,
    act_oth,
    slope,
    norm_one,
    resid_two,
    resid_one,
    gred_own,
    gred_oth,
    gexp_own,
    gexp_oth,
    gbr_own,
    gbr_oth,
    gatt,
    qt,
    gat,
    dkv_in,
    gpj_own,
    gpj_oth,
    live_map,
    out_own,
    gin_own,
    grad,
    pair_in,
    first_in,
    second_in,
    far_in,
    total,
    flat,
    placed,
    bias_sum,
    bias_in,
    load_sem,
    vector_sem,
    core_send,
    core_recv,
    pair_send,
    pair_recv,
    first_send,
    first_recv,
    second_send,
    second_recv,
    far_send,
    far_recv,
    beside_send,
    bias_send,
    bias_recv,
    fix_send,
    fix_recv,
    out_sem,
):
    dp = lax.axis_index("dp")
    blk = lax.axis_index("blk")
    oth = 1 - blk
    xx = dp % 2
    yy = (dp // 2) % 2
    zz = dp // 4
    column = dp % 4
    core_dev = (dp, oth)
    x_dev = (dp + 1 - 2 * xx, blk)
    y_dev = (dp + 2 - 4 * yy, blk)
    pair_dev = (jnp.where(zz % 2 == 0, dp + 4, dp - 4), blk)
    device = dp * 2 + blk

    def load(at, src, dst):
        copy = pltpu.make_async_copy(src, dst, load_sem.at[at])
        copy.start()
        return copy

    own_rows = pl.ds(aligned(blk * BLOCK, BLOCK), BLOCK)
    oth_rows = pl.ds(aligned(oth * BLOCK, BLOCK), BLOCK)
    load_x = load(0, hidden, x_row.at[own_rows])
    load_wp = [
        load(6 + part, w_project.at[:, part_cols], wp.at[:, part_cols])
        for part, part_cols in enumerate(pl.ds(WIDTH * part, WIDTH) for part in range(3))
    ]
    barrier = pltpu.get_barrier_semaphore()

    def greet(dev):
        pl.semaphore_signal(barrier, inc=1, device_id=dev, device_id_type=MESH)

    greet(core_dev)
    greet(x_dev)
    greet(y_dev)
    for step in range(1, 4):
        greet((lax.rem(dp + 4 * step, CHIPS), blk))
        greet((lax.rem(dp + 4 * step, CHIPS), oth))

    @pl.when((blk == 1) & (dp < CHIPS - 1))
    def _():
        greet((dp + 1, 0))

    small = []
    for at, (src, dst) in enumerate(zip(vectors, vector_at)):
        small.append(pltpu.make_async_copy(src, dst.at[0], vector_sem.at[at]))
    for copy in small:
        copy.start()
    (
        query_bias,
        value_bias,
        output_bias,
        first_gain,
        first_shift,
        expand_bias,
        reduce_bias,
        second_gain,
        second_shift,
        start_vector,
        end_vector,
    ) = vector_at

    def to_core(at, src, dst):
        copy = pltpu.make_async_remote_copy(
            src_ref=src,
            dst_ref=dst,
            send_sem=core_send.at[at],
            recv_sem=core_recv.at[at],
            device_id=core_dev,
            device_id_type=MESH,
        )
        copy.start()
        return copy

    pl.semaphore_wait(barrier, 9 + ((blk == 0) & (dp > 0)).astype(jnp.int32))
    core_copies = [to_core(0, hidden, x_row.at[own_rows])]

    length, start_at, end_at, answered = (ref[...].reshape(1, 1) for ref in scalars)
    key_at = lax.broadcasted_iota(jnp.int32, (1, ROW), 1)
    key_live = key_at < length
    token_at = blk * BLOCK + lax.broadcasted_iota(jnp.int32, (BLOCK, 1), 0)
    row_live = (token_at < length).astype(FULL)
    live_map[...] = jnp.where(key_live, 1.0 / ROW, 0.0) * row_live

    def project(rows, part):
        return dot_nn(x_row[rows, :], wp[:, WIDTH * part : WIDTH * part + WIDTH])

    load_x.wait()
    load_wp[0].wait()
    for copy in small:
        copy.wait()
    own_queries = (project(own_rows, 0) + query_bias[...]).astype(LOW)
    q_own[...] = own_queries * jnp.asarray(HEAD_DIM ** (-0.5), LOW)
    load_wp[1].wait()
    load_wo = load(1, w_output, wo)
    load_we = load(2, w_expand, we)
    load_wr = load(3, w_reduce, wr)
    load_up = load(4, upstream, up)
    load_te = load(5, teacher, te)
    k_row[own_rows, :] = project(own_rows, 1).astype(LOW)
    load_wp[2].wait()
    v_row[own_rows, :] = (project(own_rows, 2) + value_bias[...]).astype(LOW)
    pltpu.make_async_remote_copy(
        src_ref=x_row.at[oth_rows],
        dst_ref=x_row.at[oth_rows],
        send_sem=core_send.at[0],
        recv_sem=core_recv.at[0],
        device_id=core_dev,
        device_id_type=MESH,
    ).wait_recv()
    k_row[oth_rows, :] = project(oth_rows, 1).astype(LOW)
    v_row[oth_rows, :] = (project(oth_rows, 2) + value_bias[...]).astype(LOW)

    lane = lax.broadcasted_iota(jnp.int32, (1, LANES), 1)
    head_lanes = ((lane < HEAD_DIM).astype(LOW), (lane >= HEAD_DIM).astype(LOW))

    def pair_cols(head):
        return slice(LANES * (head // 2), LANES * (head // 2) + LANES)

    def score_part(head, part):
        cols = pair_cols(head)
        keys = slice(BLOCK * part, BLOCK * part + BLOCK)
        scores = dot_nt(q_own[:, cols] * head_lanes[head % 2], k_row[keys, cols])
        return jnp.where(key_live[:, keys], scores, -1e30) if part == 1 else scores

    gathered = {}

    def head_gather(head):
        cols = pair_cols(head)
        gathered[head] = dot_nn(soft[head], v_row[:, cols] * head_lanes[head % 2])
        if head % 2 == 1:
            att_own[:, cols] = (gathered[head - 1] + gathered[head]).astype(LOW)

    def peak_of(part):
        return jnp.max(part, axis=-1, keepdims=True)

    def total_of(part):
        return jnp.sum(part, axis=-1, keepdims=True)

    ahead = [score_part(0, 0), score_part(0, 1)]
    for head in range(HEADS):
        scores = ahead
        ahead = []
        if head + 1 < HEADS:
            ahead.append(score_part(head + 1, 0))
        peak = jnp.maximum(peak_of(scores[0]), peak_of(scores[1]))
        if head + 1 < HEADS:
            ahead.append(score_part(head + 1, 1))
        terms = [jnp.exp(part - peak) for part in scores]
        if head > 0:
            head_gather(head - 1)
        scale = 1.0 / (total_of(terms[0]) + total_of(terms[1]))
        for part in range(2):
            keys = slice(BLOCK * part, BLOCK * part + BLOCK)
            soft[head, :, keys] = (terms[part] * scale).astype(LOW)
    head_gather(HEADS - 1)
    core_copies.append(to_core(1, att_own, att_oth))

    load_wo.wait()
    branch = dot_nn(att_own[...], wo[...]) + output_bias[...]
    resid = x_row[own_rows, :].astype(FULL) + branch
    centre = resid - row_mean(resid)
    scale_one = lax.rsqrt(row_mean(centre * centre) + norm_eps)
    normal = centre * scale_one
    norm_one[...] = normal
    mix_own[...] = (normal * first_gain[...] + first_shift[...]).astype(LOW)
    core_copies.append(to_core(2, mix_own, mix_oth))

    load_we.wait()

    act_copies = []
    for at in range(6):
        cols = slice(512 * at, 512 * at + 512)
        expanded = dot_nn(mix_own[...], we[:, cols]) + expand_bias[:, cols]
        gate = 0.5 + 0.5 * lax.erf(expanded * (2.0**-0.5))
        bell = jnp.exp(expanded * expanded * -0.5) * ((2.0 * jnp.pi) ** -0.5)
        act_own[:, cols] = (expanded * gate).astype(LOW)
        slope[:, cols] = (gate + expanded * bell).astype(LOW)
        if at % 2 == 1:
            piece = slice(512 * at - 512, 512 * at + 512)
            act_copies.append(
                to_core(9 + at // 2, act_own.at[:, piece], act_oth.at[:, piece])
            )

    load_wr.wait()
    reduced = dot_nn(act_own[...], wr[...]) + reduce_bias[...]
    mixed = norm_one[...] * first_gain[...] + first_shift[...]
    resid = mixed + reduced
    centre = resid - row_mean(resid)
    scale_two = lax.rsqrt(row_mean(centre * centre) + norm_eps)
    normal = centre * scale_two
    out_own[...] = (normal * second_gain[...] + second_shift[...]).astype(LOW)
    store_out = pltpu.make_async_copy(out_own, layer_output, out_sem.at[0])
    store_out.start()

    answered = answered > 0
    start_slot = jnp.where(answered, start_at, 0)
    end_slot = jnp.where(answered, end_at, 0)
    load_up.wait()
    cot = up[...].astype(FULL) * row_live
    cot = cot + (token_at == start_slot).astype(FULL) * start_vector[...]
    cot = cot + (token_at == end_slot).astype(FULL) * end_vector[...]

    def put_bias(first_row, vector):
        for at in range(vector.shape[1] // LANES):
            bias_sum[first_row + at : first_row + at + 1, :] = vector[
                :, at * LANES : (at + 1) * LANES
            ]

    put_bias(60, col_sum(cot * normal))
    put_bias(66, col_sum(cot))
    pulled = cot * second_gain[...]
    pulled = scale_two * (pulled - row_mean(pulled) - normal * row_mean(pulled * normal))
    resid_two[...] = pulled
    pulled_low = pulled.astype(LOW)
    gred_own[...] = pulled_low
    put_bias(54, col_sum(pulled_low.astype(FULL)))
    own_384 = pl.ds(aligned(blk * 384, 384), 384)
    oth_384 = pl.ds(aligned(oth * 384, 384), 384)
    core_copies.append(None)
    core_copies.append(to_core(4, gred_own.at[:, oth_384], gred_oth))

    def send(src, dst, send_sem, recv_sem, dev):
        pltpu.make_async_remote_copy(
            src_ref=src,
            dst_ref=dst,
            send_sem=send_sem,
            recv_sem=recv_sem,
            device_id=dev,
            device_id_type=MESH,
        ).start()

    def wait_recv(dst, recv_sem):
        pltpu.make_async_remote_copy(
            src_ref=dst,
            dst_ref=dst,
            send_sem=recv_sem,
            recv_sem=recv_sem,
            device_id=core_dev,
            device_id_type=MESH,
        ).wait_recv()

    def wait_send(src, send_sem):
        pltpu.make_async_remote_copy(
            src_ref=src,
            dst_ref=src,
            send_sem=send_sem,
            recv_sem=send_sem,
            device_id=core_dev,
            device_id_type=MESH,
        ).wait_send()

    def owner(plane, x_at, y_at):
        return 4 * plane + 2 * y_at + x_at

    def add_unit(chip, unit, arrivals):
        @pl.loop(0, 3)
        def _(at):
            rows = pl.ds(aligned(96 * at, 96), 96)
            value = grad[chip, unit, rows, :].astype(FULL)
            for arrival in arrivals:
                value = value + arrival[rows, :].astype(FULL)
            grad[chip, unit, rows, :] = value.astype(LOW)

    def paired(plane, unit):
        return unit in PAIRED[plane]

    def kept(plane):
        return (lax.rem(zz, 2) == 0) if plane < 2 else (lax.rem(zz, 2) == 1)

    def taking_part(plane, unit, step):
        if paired(plane, unit):
            pl.when(kept(plane))(step)
        else:
            step()

    def pair_copy(plane, unit):
        return pltpu.make_async_remote_copy(
            src_ref=grad.at[pl.ds(4 * plane, 4), unit],
            dst_ref=pair_in.at[plane % 2, PAIRED[plane].index(unit)],
            send_sem=pair_send.at[plane, unit],
            recv_sem=pair_recv.at[plane, unit],
            device_id=pair_dev,
            device_id_type=MESH,
        )

    def crossing(plane, unit):
        x_first = (plane + unit) % 2 == 0
        first_dev, second_dev = (x_dev, y_dev) if x_first else (y_dev, x_dev)
        beside = owner(plane, 1 - xx, yy) if x_first else owner(plane, xx, 1 - yy)
        behind = owner(plane, xx, 1 - yy) if x_first else owner(plane, 1 - xx, yy)
        return first_dev, second_dev, beside, behind

    def first_copies(plane, unit, slots=(0, 1)):
        first_dev, _, beside, _ = crossing(plane, unit)
        chips = (owner(plane, 1 - xx, 1 - yy), beside)
        return [
            pltpu.make_async_remote_copy(
                src_ref=grad.at[chips[slot], unit],
                dst_ref=first_in.at[plane, unit, slot],
                send_sem=first_send.at[plane, unit, slot],
                recv_sem=first_recv.at[plane, unit, slot],
                device_id=first_dev,
                device_id_type=MESH,
            )
            for slot in slots
        ]

    def second_copy(plane, unit):
        _, second_dev, _, behind = crossing(plane, unit)
        return pltpu.make_async_remote_copy(
            src_ref=grad.at[behind, unit],
            dst_ref=second_in.at[plane, unit],
            send_sem=second_send.at[plane, unit],
            recv_sem=second_recv.at[plane, unit],
            device_id=second_dev,
            device_id_type=MESH,
        )

    def chained(plane, unit):
        return CHAINED[plane] and not paired(plane, unit)

    def last_slot(unit, source):
        return jnp.where(blk == unit // 3, 0, 12) + 4 * (unit % 3) + source

    def passing_slot(plane, unit):
        return 24 + 6 * sum(CHAINED[:plane]) + unit

    def far_copy(plane, unit):
        below = zz < plane
        core = unit // 3
        if chained(plane, unit):
            chip = jnp.where(below, dp + 4, dp - 4)
            ends = jnp.where(below, zz + 1, zz - 1) == plane
            last = last_slot(unit, jnp.where(below, 0, 1))
            slot = jnp.where(ends, last, passing_slot(plane, unit))
            core = jnp.where(ends, core, blk)
        else:
            chip = owner(plane, xx, yy)
            slot = last_slot(unit, jnp.where(below, zz, zz - 1))
        return pltpu.make_async_remote_copy(
            src_ref=grad.at[owner(plane, xx, yy), unit],
            dst_ref=far_in.at[slot],
            send_sem=far_send.at[plane, unit],
            recv_sem=far_recv.at[slot],
            device_id=(chip, core),
            device_id_type=MESH,
        )

    def beside_copy(unit):
        slot = 12 + 4 * (unit % 3) + 3
        return pltpu.make_async_remote_copy(
            src_ref=grad.at[dp, unit],
            dst_ref=far_in.at[slot],
            send_sem=beside_send.at[unit % 3],
            recv_sem=far_recv.at[slot],
            device_id=core_dev,
            device_id_type=MESH,
        )

    def pair_step(plane, unit):
        @pl.when(jnp.logical_not(kept(plane)))
        def _():
            pair_copy(plane, unit).start()

    def pair_add(plane, unit):
        @pl.when(kept(plane))
        def _():
            pair_copy(plane, unit).wait_recv()

            @pl.loop(0, 4)
            def _(chip):
                add_unit(4 * plane + chip, unit, [pair_in.at[plane % 2, PAIRED[plane].index(unit), chip]])

            for copy in first_copies(plane, unit):
                copy.start()

    def first_step(plane, unit):
        for copy in first_copies(plane, unit):
            copy.start()

    def second_step(plane, unit):
        def step():
            first_copies(plane, unit, (0,))[0].wait_recv()
            _, _, _, behind = crossing(plane, unit)
            add_unit(behind, unit, [first_in.at[plane, unit, 0]])
            second_copy(plane, unit).start()

        taking_part(plane, unit, step)

    def third_step(plane, unit):
        def step():
            first_copies(plane, unit, (1,))[0].wait_recv()
            second_copy(plane, unit).wait_recv()
            add_unit(
                owner(plane, xx, yy), unit, [first_in.at[plane, unit, 1], second_in.at[plane, unit]]
            )
            leaves = zz != plane
            if chained(plane, unit):
                leaves = leaves & ((zz == 0) | (zz == 3))

            @pl.when(leaves)
            def _():
                far_copy(plane, unit).start()

            @pl.when((zz == plane) & (blk != unit // 3))
            def _():
                beside_copy(unit).start()

        taking_part(plane, unit, step)

    def chain_step(plane, unit):
        @pl.when((zz != plane) & (zz > 0) & (zz < 3))
        def _():
            slot = passing_slot(plane, unit)
            wait_recv(far_in.at[slot], far_recv.at[slot])
            add_unit(owner(plane, xx, yy), unit, [far_in.at[slot]])
            far_copy(plane, unit).start()

    def finish_step(_, unit):
        for plane in range(4):
            if paired(plane, unit):
                sources = [z for z in range(4) if z != plane and (z % 2 == 0) == (plane < 2)]
                sources = [z if z < plane else z - 1 for z in sources]
            elif CHAINED[plane]:
                sources = ([0] if plane > 0 else []) + ([1] if plane < 3 else [])
            else:
                sources = [0, 1, 2]

            gave = paired(plane, unit) and (plane % 2 == 0) != (plane < 2)

            @pl.when((zz == plane) & (blk == unit // 3))
            def _():
                for half in range(2):
                    first = 12 * half + 4 * (unit % 3)
                    slots = [first + source for source in sources]
                    if half == 1 and not gave:
                        slots.append(first + 3)
                    for slot in slots:
                        wait_recv(far_in.at[slot], far_recv.at[slot])
                    terms = [far_in[slot].astype(FULL) for slot in slots]
                    if half == 0 and not gave:
                        terms.append(grad[dp, unit].astype(FULL))
                    total[half, unit % 3] = sum(terms[1:], terms[0])

    def place_step(_, unit):
        core, local = unit // 3, unit % 3

        @pl.when(blk == core)
        def _():
            lay_out(0, core, local)
            lay_out(1, 1 - core, local)
            if unit == 0:
                @pl.when(dp > 0)
                def _():
                    hand_back((dp - 1, 1))

            elif unit == 3:
                hand_back(core_dev)
            if local < 2:
                move_rows(*((0, 9), (9, 19))[local])

    def lay_out(half, column_half, local):
        kind_at = 3 * device + local
        kinds = (
            (kind_at < 24, 32, 9),
            (((kind_at >= 24) & (kind_at < 32)) | (kind_at >= 64), 96, 3),
            ((kind_at >= 32) & (kind_at < 64), 24, 12),
        )
        for fits, rows, tiles in kinds:

            @pl.when(fits)
            def _():
                for tile in range(tiles):
                    for group in range(rows // 8):
                        at = rows * tile + 8 * group
                        to = 576 * local + 16 * group * tiles + tile + column_half * tiles
                        flat[pl.ds(to, 8, stride=2 * tiles), :] = total[
                            half, local, at : at + 8, :
                        ]

    def hand_back(dev):
        send(flat.at[0:72], flat.at[1728:1800], fix_send.at[0], fix_recv.at[0], dev)

    shift = 32 * lax.rem(device, 4)
    skip = (9 * device) // 4
    stays = lane < LANES - shift

    def move_rows(first, last):
        @pl.loop(first, last)
        def _(at):
            rows = at * 56
            one = pltpu.roll(flat[pl.ds(rows + skip, 56), :], LANES - shift, 1)
            two = pltpu.roll(flat[pl.ds(rows + skip + 1, 56), :], LANES - shift, 1)
            placed[pl.ds(aligned(rows, 8), 56), :] = jnp.where(stays, one, two)

    corner = (xx == 1) & (yy == 1)
    last = dp == CHIPS - 1

    def bias_step(hop, _):
        def leaves(here, slot, dev):
            @pl.when(here)
            def _():
                send(bias_sum, bias_in.at[slot], bias_send.at[0], bias_recv.at[slot], dev)

        def comes(here, slot):
            @pl.when(here)
            def _():
                wait_recv(bias_in.at[slot], bias_recv.at[slot])
                bias_sum[...] += bias_in[slot]

        if hop == 0:
            leaves(xx == 0, 0, x_dev)
        elif hop == 1:
            comes(xx == 1, 0)
            leaves((xx == 1) & (yy == 0), 1, y_dev)
        else:
            comes(corner, 1)
            leaves(corner & (zz < 3), 2 + 2 * zz + blk, (CHIPS - 1, 1))
            leaves(last & (blk == 0), 8, core_dev)

    steps = {
        "bias": bias_step,
        "pair": pair_step,
        "add": pair_add,
        "first": first_step,
        "second": second_step,
        "third": third_step,
        "chain": chain_step,
        "finish": finish_step,
        "place": place_step,
    }

    def serve(after):
        for what, plane, unit in SCHEDULE.get(after, ()):
            steps[what](plane, unit)

    def put_unit(at, rows, values):
        chip, unit = (at // 6, at % 6) if isinstance(at, int) else (lax.div(at, 6), lax.rem(at, 6))
        grad[chip, unit, rows, :] = values.astype(LOW)

    def reduce_cols(first, count):
        before = 96 * (first - 64) % LANES
        return slice(96 * (first - 64) - before, 96 * (first - 64 + count)), before

    def put_reduced(first, count, before, part):
        for unit in range(count):
            for tile in range(3):
                put_unit(
                    first + unit,
                    slice(96 * tile, 96 * tile + 96),
                    part[
                        before + 96 * unit : before + 96 * unit + 96,
                        LANES * tile : LANES * tile + LANES,
                    ],
                )

    def slope_step(at):
        half = oth if at < 3 else blk
        part_at = at % 3 * 512
        cols = pl.ds(aligned(half * 1536 + part_at, 512), 512)
        grad_active = dot_nt(gred_own[...], wr[cols, :])
        grad_expanded = (grad_active * slope[:, cols].astype(FULL)).astype(LOW)
        gexp_own[half, :, part_at : part_at + 512] = grad_expanded
        sums = col_sum(grad_expanded.astype(FULL))
        for tile in range(4):
            bias_sum[pl.ds(30 + half * 12 + at % 3 * 4 + tile, 1), :] = sums[
                :, LANES * tile : LANES * tile + LANES
            ]

    reduced_own = gred_own[:, own_384]
    begun = {}
    for chip in range(12, CHIPS):
        cols, _ = reduce_cols(6 * chip, 2)
        begun[chip] = dot_tn(act_own[:, cols], reduced_own)
    slope_step(0)
    for copy in act_copies:
        copy.wait_recv()
    core_copies[4].wait_recv()
    reduced_both = both(reduced_own, gred_oth[...])

    for third in range(3):
        for chip in range(12, CHIPS):
            first = 6 * chip + 2 * third
            cols, before = reduce_cols(first, 2)
            if third == 0:
                part = begun[chip] + dot_tn(act_oth[:, cols], gred_oth[...])
            else:
                part = dot_tn(both(act_own[:, cols], act_oth[:, cols]), reduced_both)
            put_reduced(first, 2, before, part)
        serve("reduce" + str(third))
    cols, _ = reduce_cols(64, 8)
    put_reduced(64, 8, 0, dot_tn(both(act_own[:, cols], act_oth[:, cols]), reduced_both))
    serve("reduce3")

    for at in range(1, 6):
        slope_step(at)
        if at == 2:
            core_copies.append(to_core(5, gexp_own.at[oth], gexp_oth))
            serve("slopes0")

    serve("slopes")
    grad_mixed = resid_two[...]
    for half in range(2):
        grad_mixed = grad_mixed + dot_nt(
            gexp_own[half], we[:, 1536 * half : 1536 * half + 1536]
        )

    normal = norm_one[...]
    put_bias(18, col_sum(grad_mixed * normal))
    put_bias(24, col_sum(grad_mixed))
    pulled = grad_mixed * first_gain[...]
    pulled = scale_one * (pulled - row_mean(pulled) - normal * row_mean(pulled * normal))
    resid_one[...] = pulled
    pulled_low = pulled.astype(LOW)
    gbr_own[...] = pulled_low
    put_bias(12, col_sum(pulled_low.astype(FULL)))
    core_copies.append(to_core(6, gbr_own.at[:, oth_384], gbr_oth))

    serve("norm")

    core_copies[2].wait_recv()
    core_copies[5].wait_recv()

    @pl.loop(0, 6, unroll=3)
    def _(at):
        cols = pl.ds(aligned(at * 256, 256), 256)
        part = dot_tn(
            both(mix_own[...], mix_oth[...]), both(gexp_own[blk, :, cols], gexp_oth[:, cols])
        )
        rows = pl.ds(aligned(at * 48, 48), 48)
        for unit in range(32):
            piece = part[24 * unit : 24 * unit + 24, :]
            put_unit(32 + unit, rows, both(piece[:, :LANES], piece[:, LANES:]))

    serve("expand")
    gatt[...] = dot_nt(gbr_own[...], wo[...]).astype(LOW)
    core_copies[1].wait_recv()
    core_copies[6].wait_recv()
    part = dot_tn(both(att_own[...], att_oth[...]), both(gbr_own[:, own_384], gbr_oth[...]))
    for unit in range(8):
        for tile in range(3):
            put_unit(24 + unit, slice(96 * tile, 96 * tile + 96), part[
                96 * unit : 96 * unit + 96, LANES * tile : LANES * tile + LANES
            ])
    serve("output")

    qt[...] = q_own[...].T
    gat[...] = gatt[...].T
    load_te.wait()

    def head_pair(pair):
        cols = pl.ds(aligned(pair * LANES, LANES), LANES)
        ga_pair = gatt[:, cols]
        k_pair = k_row[:, cols]
        v_pair = v_row[:, cols]
        grad_query = None
        for side in range(2):
            rows = pl.ds(aligned(pair * LANES + side * HEAD_DIM, HEAD_DIM), HEAD_DIM)
            soft_low = soft[2 * pair + side]
            grad_soft = dot_nt(ga_pair * head_lanes[side], v_pair)
            soft_full = soft_low.astype(FULL)
            taught = te[2 * pair + side].astype(FULL) * live_map[...]
            shift = jnp.sum(taught - grad_soft * soft_full, axis=-1, keepdims=True)
            grad_scores = (soft_full * (grad_soft + shift) - taught).astype(LOW)
            part = dot_nn(grad_scores, k_pair * head_lanes[side])
            grad_query = part if grad_query is None else grad_query + part
            slot = pl.ds(aligned(pair * ROW, ROW), ROW)
            at = side * HEAD_DIM
            slope[at : at + HEAD_DIM, slot] = dot_nn(qt[rows, :], grad_scores).astype(LOW)
            at = at + LANES
            slope[at : at + HEAD_DIM, slot] = dot_nn(gat[rows, :], soft_low).astype(LOW)
        gpj_own[:, cols] = (grad_query * HEAD_DIM ** (-0.5)).astype(LOW)

    for pair in range(HEADS // 2):
        head_pair(pair)
        serve("heads" + str(pair))

    def turned(pair, block, first):
        lanes = pl.ds(aligned(pair * ROW + block * BLOCK, BLOCK), BLOCK)
        return slope[first : first + LANES, lanes].T

    for copy in act_copies:
        copy.wait_send()
    for pair in range(HEADS // 2):
        for first in (0, LANES):
            at = pair * LANES + first * (WIDTH // LANES)
            act_own[:, at : at + LANES] = turned(pair, oth, first)
    core_copies.append(to_core(7, act_own.at[:, : 2 * WIDTH], dkv_in))
    core_copies[7].wait_recv()
    for pair in range(HEADS // 2):
        for first in (0, LANES):
            at = pair * LANES + first * (WIDTH // LANES)
            gpj_own[:, WIDTH + at : WIDTH + at + LANES] = (
                turned(pair, blk, first).astype(FULL) + dkv_in[:, at : at + LANES].astype(FULL)
            ).astype(LOW)
    serve("keys")
    own_1152 = pl.ds(aligned(blk * 1152, 1152), 1152)
    oth_1152 = pl.ds(aligned(oth * 1152, 1152), 1152)
    core_copies.append(to_core(8, gpj_own.at[:, oth_1152], gpj_oth))
    put_bias(0, col_sum(gpj_own[:, :WIDTH].astype(FULL)))
    put_bias(6, col_sum(gpj_own[:, 2 * WIDTH :].astype(FULL)))

    def input_gradient_part():
        gin_own[...] = (resid_one[...] + dot_nt(gpj_own[...], wp[...])).astype(LOW)
        pltpu.make_async_copy(gin_own, input_gradient, out_sem.at[1]).start()

    input_gradient_part()
    serve("input")

    core_copies[8].wait_recv()

    @pl.loop(0, 3, unroll=3)
    def _(at):
        cols = pl.ds(aligned(at * 384, 384), 384)
        mine = pl.ds(aligned(blk * 1152 + at * 384, 384), 384)
        part = dot_tn(
            both(x_row[own_rows, :], x_row[oth_rows, :]), both(gpj_own[:, mine], gpj_oth[:, cols])
        )
        for unit in range(24):
            for tile in range(3):
                rows = pl.ds(aligned(at * 96 + 32 * tile, 32), 32)
                put_unit(unit, rows, part[
                    32 * unit : 32 * unit + 32, LANES * tile : LANES * tile + LANES
                ])

    serve("project")

    serve("end")

    @pl.when(last & (blk == 1))
    def _():
        for at in range(2, 9):
            wait_recv(bias_in.at[at], bias_recv.at[at])
        flat[1728:1800, :] = sum((bias_in[at] for at in range(2, 9)), bias_sum[...])

    @pl.when(device < 2 * CHIPS - 1)
    def _():
        wait_recv(flat.at[1728:1800], fix_recv.at[0])

    early = pl.ds(0, 19 * 56)
    late = pl.ds(19 * 56, 12 * 56)
    stores = [
        pltpu.make_async_copy(placed.at[rows], grads.at[rows], out_sem.at[2 + at])
        for at, rows in enumerate((early, late))
    ]
    stores[0].start()
    move_rows(19, 31)
    stores[1].start()

    for copy in core_copies:
        if copy is not None:
            copy.wait_send()

    for plane in range(4):
        for unit in range(6):
            if paired(plane, unit):

                @pl.when(jnp.logical_not(kept(plane)))
                def _():
                    pair_copy(plane, unit).wait_send()

            def sent():
                for copy in first_copies(plane, unit):
                    copy.wait_send()
                second_copy(plane, unit).wait_send()

                @pl.when(zz != plane)
                def _():
                    far_copy(plane, unit).wait_send()

                @pl.when((zz == plane) & (blk != unit // 3))
                def _():
                    beside_copy(unit).wait_send()

            taking_part(plane, unit, sent)

    @pl.when(jnp.logical_not(last & (blk == 1)))
    def _():
        wait_send(bias_sum, bias_send.at[0])

    @pl.when(device > 0)
    def _():
        wait_send(flat.at[0:72], fix_send.at[0])

    store_out.wait()
    pltpu.make_async_copy(gin_own, input_gradient, out_sem.at[1]).wait()
    for store in stores:
        store.wait()


def hand_over(*refs):
    sources, targets, held, sems = refs[:3], refs[3:6], refs[6:9], refs[9]
    pieces = []
    for source, target, buffer in zip(sources, targets, held):
        rows = 248 if source.shape[0] % 248 == 0 else source.shape[0]
        for first in range(0, source.shape[0], rows):
            piece = pl.ds(first, rows)
            pieces.append((source.at[piece], buffer.at[piece], target.at[piece]))
    reads = []
    writes = []
    for at, (source, buffer, target) in enumerate(pieces):
        reads.append(pltpu.make_async_copy(source, buffer, sems.at[0, at]))
        writes.append(pltpu.make_async_copy(buffer, target, sems.at[1, at]))
    for read in reads:
        read.start()
    for read, write in zip(reads, writes):
        read.wait()
        write.start()
    for write in writes:
        write.wait()


def fused_layer(
    hidden_in,
    project_weight,
    output_weight,
    expand_weight,
    reduce_weight,
    query_bias,
    value_bias,
    output_bias,
    first_gain,
    first_shift,
    expand_bias,
    reduce_bias,
    second_gain,
    second_shift,
    upstream,
    teacher_maps,
    start_vector,
    end_vector,
    valid_length,
    start_index,
    end_index,
    answerable,
):
    vectors = (
        query_bias,
        value_bias,
        output_bias,
        first_gain,
        first_shift,
        expand_bias,
        reduce_bias,
        second_gain,
        second_shift,
        start_vector,
        end_vector,
    )
    scalars = (valid_length, start_index, end_index, answerable)
    anywhere = pl.BlockSpec(memory_space=pl.ANY)
    in_vmem = pl.BlockSpec(memory_space=pltpu.VMEM)

    def low(*shape):
        return pltpu.VMEM(shape, LOW)

    def full(*shape):
        return pltpu.VMEM(shape, FULL)

    dma = pltpu.SemaphoreType.DMA
    scratch = [
        low(WIDTH, 3 * WIDTH),
        low(WIDTH, WIDTH),
        low(WIDTH, FF),
        low(FF, WIDTH),
        low(HEADS, BLOCK, ROW),
        low(BLOCK, WIDTH),
        low(ROW, WIDTH),
        tuple(full(1, vector.shape[0]) for vector in vectors),
        low(BLOCK, WIDTH),
        low(ROW, WIDTH),
        low(ROW, WIDTH),
        low(HEADS, BLOCK, ROW),
        low(BLOCK, WIDTH),
        low(BLOCK, WIDTH),
        low(BLOCK, WIDTH),
        low(BLOCK, WIDTH),
        low(BLOCK, FF),
        low(BLOCK, FF),
        low(BLOCK, FF),
        full(BLOCK, WIDTH),
        full(BLOCK, WIDTH),
        full(BLOCK, WIDTH),
        low(BLOCK, WIDTH),
        low(BLOCK, WIDTH // 2),
        low(2, BLOCK, FF // 2),
        low(BLOCK, FF // 2),
        low(BLOCK, WIDTH),
        low(BLOCK, WIDTH // 2),
        low(BLOCK, WIDTH),
        low(WIDTH, BLOCK),
        low(WIDTH, BLOCK),
        low(BLOCK, 2 * WIDTH),
        low(BLOCK, 3 * WIDTH),
        low(BLOCK, 3 * WIDTH // 2),
        full(BLOCK, ROW),
        low(BLOCK, WIDTH),
        low(BLOCK, WIDTH),
        low(CHIPS, 6, UNIT, LANES),
        low(2, max(map(len, PAIRED)), 4, UNIT, LANES),
        low(4, 6, 2, UNIT, LANES),
        low(4, 6, UNIT, LANES),
        low(24 + 6 * sum(CHAINED), UNIT, LANES),
        full(2, 3, UNIT, LANES),
        full(1816, LANES),
        full(1736, LANES),
        full(72, LANES),
        full(9, 72, LANES),
        dma((9,)),
        dma((len(vectors),)),
        dma((12,)),
        dma((12,)),
        dma((4, 6)),
        dma((4, 6)),
        dma((4, 6, 2)),
        dma((4, 6, 2)),
        dma((4, 6)),
        dma((4, 6)),
        dma((4, 6)),
        dma((24 + 6 * sum(CHAINED),)),
        dma((3,)),
        dma((1,)),
        dma((9,)),
        dma((1,)),
        dma((1,)),
        dma((4,)),
    ]
    results = (
        jax.ShapeDtypeStruct((BLOCK, WIDTH), LOW),
        jax.ShapeDtypeStruct((BLOCK, WIDTH), LOW),
        jax.ShapeDtypeStruct((1736, LANES), FULL),
    )
    made = pl.pallas_call(
        layer_kernel,
        out_shape=results,
        in_specs=[anywhere] * 7 + [(anywhere,) * len(vectors), (in_vmem,) * len(scalars)],
        out_specs=(anywhere,) * 3,
        scratch_shapes=scratch,
        compiler_params=pltpu.CompilerParams(
            collective_id=0, has_side_effects=True, vmem_limit_bytes=63 * 2**20
        ),
        name="encoder_layer",
    )(
        hidden_in.reshape(BLOCK, WIDTH),
        upstream.reshape(BLOCK, WIDTH),
        teacher_maps.reshape(HEADS, BLOCK, ROW),
        project_weight,
        output_weight,
        expand_weight,
        reduce_weight,
        vectors,
        scalars,
    )
    layer_output, input_gradient, grads = pl.pallas_call(
        hand_over,
        out_shape=results,
        in_specs=[anywhere] * 3,
        out_specs=(anywhere,) * 3,
        scratch_shapes=[pltpu.VMEM(result.shape, result.dtype) for result in results] + [dma((2, 9))],
        name="hand_over",
    )(*made)
    return (
        layer_output.reshape(1, BLOCK, WIDTH),
        input_gradient.reshape(1, BLOCK, WIDTH),
        grads.reshape(-1)[: 3 * 2 * UNIT * LANES + UNIT],
    )


def layer_norm(field_in, gain_vec, shift_vec):
    centre = field_in - jnp.mean(field_in, axis=-1, keepdims=True)
    spread = jnp.mean(centre * centre, axis=-1, keepdims=True)
    return centre * lax.rsqrt(spread + norm_eps) * gain_vec + shift_vec


def gelu_exact(field_in):
    return jax.nn.gelu(field_in, approximate=False)


def outer_sum(left, right):
    return jnp.einsum("nd,ne->de", left, right, preferred_element_type=jnp.float32)


def column_sum(values_low):
    return jnp.sum(values_low.astype(jnp.float32), axis=0)


def plain_layer(
    hidden_in,
    project_weight,
    output_weight,
    expand_weight,
    reduce_weight,
    query_bias,
    value_bias,
    output_bias,
    first_gain,
    first_shift,
    expand_bias,
    reduce_bias,
    second_gain,
    second_shift,
    upstream,
    teacher_maps,
    start_vector,
    end_vector,
    valid_length,
    start_index,
    end_index,
    answerable,
):
    row_count, block_len, width = hidden_in.shape
    blocks = lax.axis_size("blk")
    length = block_len * blocks
    offset = lax.axis_index("blk") * block_len
    token_count = row_count * block_len
    positions = offset + jnp.arange(block_len, dtype=jnp.int32)
    key_live = jnp.arange(length, dtype=jnp.int32)[None, :] < valid_length[:, None]
    row_live = positions[None, :] < valid_length[:, None]
    score_scale = HEAD_DIM ** (-0.5)
    tokens = hidden_in.reshape(token_count, width)
    joined_bias = jnp.concatenate([query_bias, jnp.zeros_like(query_bias), value_bias])
    project = (
        jnp.dot(tokens, project_weight, preferred_element_type=jnp.float32) + joined_bias
    ).astype(jnp.bfloat16)
    queries = project[:, :width].reshape(row_count, block_len, HEADS, HEAD_DIM)
    keys_own = project[:, width : 2 * width].reshape(row_count, block_len, width)
    values_own = project[:, 2 * width :].reshape(row_count, block_len, width)
    keys_all, values_all = (
        lax.all_gather(keys_own, "blk", axis=1, tiled=True),
        lax.all_gather(values_own, "blk", axis=1, tiled=True),
    )

    def scores_of(keys_full):
        raw = (
            jnp.einsum(
                "rqhe,rkhe->rhqk",
                queries,
                keys_full.reshape(row_count, length, HEADS, HEAD_DIM),
                preferred_element_type=jnp.float32,
            )
            * score_scale
        )
        return jnp.where(key_live[:, None, None, :], raw, -1e30)

    scores = scores_of(keys_all)
    row_peak = jnp.max(scores, axis=-1, keepdims=True)
    expo_terms = jnp.exp(scores - row_peak)
    row_total = jnp.sum(expo_terms, axis=-1, keepdims=True)
    soft_low = (expo_terms / row_total).astype(jnp.bfloat16)
    log_total = row_peak + jnp.log(row_total)
    attended = (
        jnp.einsum(
            "rhqk,rkhe->rqhe",
            soft_low,
            values_all.reshape(row_count, length, HEADS, HEAD_DIM),
            preferred_element_type=jnp.float32,
        )
        .reshape(token_count, width)
        .astype(jnp.bfloat16)
    )
    branch = jnp.dot(attended, output_weight, preferred_element_type=jnp.float32) + output_bias
    resid_one = tokens.astype(jnp.float32) + branch
    mixed, first_pull = jax.vjp(layer_norm, resid_one, first_gain, first_shift)
    mixed_low = mixed.astype(jnp.bfloat16)
    expanded = jnp.dot(mixed_low, expand_weight, preferred_element_type=jnp.float32) + expand_bias
    active, gelu_pull = jax.vjp(gelu_exact, expanded)
    active_low = active.astype(jnp.bfloat16)
    reduced = jnp.dot(active_low, reduce_weight, preferred_element_type=jnp.float32) + reduce_bias
    result, second_pull = jax.vjp(layer_norm, mixed + reduced, second_gain, second_shift)
    layer_output = result.astype(jnp.bfloat16).reshape(row_count, block_len, width)
    start_slot = jnp.where(answerable > 0, start_index, 0)
    end_slot = jnp.where(answerable > 0, end_index, 0)
    cotangent = (
        upstream.astype(jnp.float32) * row_live[..., None].astype(jnp.float32)
        + (positions[None, :] == start_slot[:, None])[..., None].astype(jnp.float32) * start_vector
        + (positions[None, :] == end_slot[:, None])[..., None].astype(jnp.float32) * end_vector
    )
    grad_resid_two, grad_second_gain, grad_second_shift = second_pull(
        cotangent.reshape(token_count, width)
    )
    grad_reduced = grad_resid_two.astype(jnp.bfloat16)
    grad_active = jnp.einsum(
        "nd,fd->nf", grad_reduced, reduce_weight, preferred_element_type=jnp.float32
    )
    grad_expanded = gelu_pull(grad_active)[0].astype(jnp.bfloat16)
    grad_mixed = grad_resid_two + jnp.einsum(
        "nf,df->nd", grad_expanded, expand_weight, preferred_element_type=jnp.float32
    )
    grad_resid_one, grad_first_gain, grad_first_shift = first_pull(grad_mixed)
    grad_branch = grad_resid_one.astype(jnp.bfloat16)
    grad_attended = jnp.einsum(
        "ne,de->nd", grad_branch, output_weight, preferred_element_type=jnp.float32
    )
    grad_attended = grad_attended.astype(jnp.bfloat16).reshape(
        row_count, block_len, HEADS, HEAD_DIM
    )
    keys_back, values_back = (
        lax.all_gather(keys_own, "blk", axis=1, tiled=True),
        lax.all_gather(values_own, "blk", axis=1, tiled=True),
    )
    keys_heads = keys_back.reshape(row_count, length, HEADS, HEAD_DIM)
    values_heads = values_back.reshape(row_count, length, HEADS, HEAD_DIM)
    soft = jnp.exp(scores_of(keys_back) - log_total)
    both_live = row_live[:, None, :, None] & key_live[:, None, None, :]
    teacher_live = jnp.where(both_live, teacher_maps.astype(jnp.float32), 0.0)
    teacher_total = jnp.sum(teacher_live, axis=-1, keepdims=True)
    grad_soft = jnp.einsum(
        "rqhe,rkhe->rhqk", grad_attended, values_heads, preferred_element_type=jnp.float32
    )
    row_delta = jnp.sum(grad_soft * soft, axis=-1, keepdims=True)
    grad_scores = (
        soft * (grad_soft - row_delta) + (teacher_total * soft - teacher_live) / length
    ).astype(jnp.bfloat16)
    grad_query = (
        jnp.einsum("rhqk,rkhe->rqhe", grad_scores, keys_heads, preferred_element_type=jnp.float32)
        * score_scale
    )
    grad_keys = (
        jnp.einsum(
            "rhqk,rqhe->rkhe", grad_scores, queries, preferred_element_type=jnp.float32
        ).reshape(row_count, length, width)
        * score_scale
    )
    grad_values = jnp.einsum(
        "rhqk,rqhe->rkhe", soft_low, grad_attended, preferred_element_type=jnp.float32
    ).reshape(row_count, length, width)
    keys_grad_own, values_grad_own = (
        lax.psum_scatter(
            grad_keys.astype(jnp.bfloat16), "blk", scatter_dimension=1, tiled=True
        ).astype(jnp.float32),
        lax.psum_scatter(
            grad_values.astype(jnp.bfloat16), "blk", scatter_dimension=1, tiled=True
        ).astype(jnp.float32),
    )
    grad_project = jnp.concatenate(
        [
            grad_query.reshape(token_count, width),
            keys_grad_own.reshape(token_count, width),
            values_grad_own.reshape(token_count, width),
        ],
        axis=1,
    ).astype(jnp.bfloat16)
    grad_input = grad_resid_one + jnp.einsum(
        "ne,de->nd", grad_project, project_weight, preferred_element_type=jnp.float32
    )
    input_gradient = grad_input.astype(jnp.bfloat16).reshape(row_count, block_len, width)
    (
        tokens_both,
        project_both,
        attended_both,
        branch_both,
        mixed_both,
        expanded_both,
        active_both,
        reduced_both,
    ) = (
        lax.all_gather(tokens, "blk", axis=0, tiled=True),
        lax.all_gather(grad_project, "blk", axis=0, tiled=True),
        lax.all_gather(attended, "blk", axis=0, tiled=True),
        lax.all_gather(grad_branch, "blk", axis=0, tiled=True),
        lax.all_gather(mixed_low, "blk", axis=0, tiled=True),
        lax.all_gather(grad_expanded, "blk", axis=0, tiled=True),
        lax.all_gather(active_low, "blk", axis=0, tiled=True),
        lax.all_gather(grad_reduced, "blk", axis=0, tiled=True),
    )
    project_sums = column_sum(project_both)
    norm_grads = lax.psum(
        (grad_first_gain, grad_first_shift, grad_second_gain, grad_second_shift), "blk"
    )
    flat_grads = jnp.concatenate(
        [
            outer_sum(tokens_both, project_both).reshape(-1),
            outer_sum(attended_both, branch_both).reshape(-1),
            outer_sum(mixed_both, expanded_both).reshape(-1),
            outer_sum(active_both, reduced_both).reshape(-1),
            project_sums[:width],
            project_sums[2 * width :],
            column_sum(branch_both),
            norm_grads[0],
            norm_grads[1],
            column_sum(expanded_both),
            column_sum(reduced_both),
            norm_grads[2],
            norm_grads[3],
        ]
    )
    data_count = lax.axis_size("dp")
    piece_len = flat_grads.shape[0] // (data_count * blocks)
    mine = lax.dynamic_index_in_dim(
        flat_grads.reshape(data_count, blocks, piece_len), lax.axis_index("blk"), 1, keepdims=False
    )
    weight_gradients = lax.psum_scatter(mine, "dp", scatter_dimension=0, tiled=True).reshape(
        piece_len
    )
    return (layer_output, input_gradient, weight_gradients)


def solution(mesh):
    placed = (
        P("dp", "blk", None),
        P(),
        P(),
        P(),
        P(),
        P(),
        P(),
        P(),
        P(),
        P(),
        P(),
        P(),
        P(),
        P(),
        P("dp", "blk", None),
        P("dp", None, "blk", None),
        P(),
        P(),
        P("dp"),
        P("dp"),
        P("dp"),
        P("dp"),
    )
    fits = (mesh.shape["dp"], mesh.shape["blk"]) == (CHIPS, 2)
    layer = fused_layer if fits else plain_layer
    return jax.shard_map(
        layer,
        mesh=mesh,
        in_specs=placed,
        out_specs=(P("dp", "blk", None), P("dp", "blk", None), P(("dp", "blk"))),
        check_vma=False,
    )
```
